32 devices in a mesh: grp: 2 (over x), pool: 8 (over z, y), tp: 2 (over core).
Axes of the slice: x: 2, y: 2, z: 4, core: 2. Of those that a mesh axis runs over, the one named last changes fastest.
Arguments:
- hidden: bfloat16 [768, 8192], P(('grp', 'pool'), 'tp'), parts along dimension 0, may hold values from -6 to 6
- queries: bfloat16 [768, 4096], P(('grp', 'pool'), 'tp'), parts along dimension 0, may hold values from -8 to 8
- key_value_weight: bfloat16 [8192, 1024], P('tp'), may hold values from -0.0625 to 0.0625
- adapter_down_weight: bfloat16 [8, 8192, 128], P('pool', 'tp'), may hold values from -0.0625 to 0.0625
- adapter_up_weight: bfloat16 [8, 2, 64, 512], P('pool', None, None, 'tp'), may hold values from -0.75 to 0.75
- stored_cache_keys: bfloat16 [768, 4, 32, 128], P(('grp', 'pool'), 'tp'), parts along dimension 0, may hold values from -4 to 4
- stored_cache_values: bfloat16 [768, 4, 32, 128], P(('grp', 'pool'), 'tp'), parts along dimension 0, may hold values from -6 to 6
- row_adapter_index: int32 [768, 1], P(('grp', 'pool')), parts along dimension 0, may hold values from 0 to 7; in each aligned block of 48 rows (0 to 47, 48 to 95, ...) at most 12 rows name the same one
- stored_cache_lengths: int32 [768], P(('grp', 'pool')), parts along dimension 0, may hold values from 2 to 32, as said below
- adapter_slot_table: int32 [8], replicated, may hold values from 0 to 7, each once
Outputs:
- token_key_value: bfloat16 [768, 1024], P(('grp', 'pool'), 'tp'), parts along dimension 0
- attended: bfloat16 [768, 4096], P(('grp', 'pool'), 'tp'), parts along dimension 0
The draws below stay inside these ranges and needn't reach their ends.
There are 2 independent parts, one for each index of `grp`. The reference program is written for one: setup_inputs(seed, part) draws one part's arguments, and reference() takes and returns one part's arrays. A program takes and returns all parts, laid end to end along the dimension named above; an argument that names none is the same for every part. Nothing has to cross between parts.
Inputs may be any that keep to these rules, and one draw needn't show every extreme that they name: `row_adapter_index`: among the rows of one index of pool at most 12 name the same adapter, and in some such block one adapter is named by exactly 12 rows. `stored_cache_lengths`: some row has exactly 32 valid positions. `adapter_slot_table`: each adapter has its own slot.
All inputs are finite; a program needn't handle non-finite values.
Results may differ from the reference program's by a relative error of at most 0.0061.
Values may be sent and summed in bfloat16 or wider, within the bound.
No kernel may reach another device: no remote copies, remote signals or barrier semaphores. Data moves between devices by JAX's collectives and lax.ppermute only.
A program may use at most 128 MiB of HBM per device.

```python
import math
import jax
import jax.numpy as jnp
import numpy as np
from jax import lax

MODEL_WIDTH = 8192
KEY_VALUE_HEADS = 4
QH = 32
HEAD_SIZE = 128
ADAPTER_RANK = 64
CACHE = 32
ROWS_DEV = 48
ROWS = 384
ADAPTER_COUNT = 8
CAP = 12


def draw_queries(key, part):
    key = jax.random.fold_in(key, 11)
    result = jnp.clip(jax.random.normal(key, (ROWS, KEY_VALUE_HEADS, QH // KEY_VALUE_HEADS, HEAD_SIZE), jnp.float32), -6.0, 6.0)
    return result.reshape(ROWS, QH * HEAD_SIZE).astype(jnp.bfloat16)


def draw_stored_cache_keys(key, part):
    key = jax.random.fold_in(key, 23)
    result = jnp.clip(jax.random.normal(key, (ROWS, KEY_VALUE_HEADS, CACHE, HEAD_SIZE), jnp.float32), -4.0, 4.0)
    return result.astype(jnp.bfloat16)


def draw_stored_cache_lengths(key, part):
    key = jax.random.fold_in(key, 37)
    first_key, second_key = jax.random.split(key)
    lengths = jax.random.randint(first_key, (ROWS,), 2, CACHE + 1)
    chosen = jax.random.randint(second_key, (), 0, ROWS)
    return jnp.where(jnp.arange(ROWS) == chosen, CACHE, lengths).astype(jnp.int32)


def levels(stream_key, extent, cuts, low, high):
    gain = 1.0
    for axis_at, blocks in cuts:
        heights = jax.random.uniform(jax.random.fold_in(jax.random.fold_in(stream_key, 6), axis_at), (blocks,), jnp.float32, low / len(cuts), high / len(cuts))
        gain = gain * jnp.repeat(jnp.exp(heights), extent[axis_at] // blocks).reshape((-1,) + (1,) * (len(extent) - 1 - axis_at))
    return gain


def deal_out(own_key, own, number, rows, amount, top, bound, lean):
    ranking = jax.random.permutation(own_key, amount)
    packed, ordinary = load_shares(amount, rows * top, bound, lean, True), load_shares(amount, rows * top, bound, lean, False)
    places = jnp.arange(amount)

    def named(sizes, rotation):
        used = int((sizes > 0).sum())
        fixed = max(1, used // 4)
        shifted = fixed + (places - fixed + rotation * (used - fixed)) % max(1, amount - fixed)
        return jnp.zeros((amount,), jnp.int32).at[ranking[jnp.where(places < fixed, places, shifted)]].set(jnp.asarray(sizes, jnp.int32))

    sizes = jnp.where(number % 4 == 0, named(packed, number // 4), named(ordinary, number - number // 4 - 1))
    mixed = jax.random.permutation(jax.random.fold_in(own, 3), amount)
    giver, taker = mixed[0:amount // 2 * 2:2], mixed[1:amount // 2 * 2:2]
    margin = jnp.minimum(sizes[giver] - 1, bound - sizes[taker]) // 2
    margin = jnp.where((giver == ranking[0]) | (taker == ranking[0]) | (sizes[taker] == 0), 0, jnp.maximum(margin, 0))
    shifted = jax.random.randint(jax.random.fold_in(own, 4), (amount // 2,), 0, 1 << 20) % (margin + 1)
    sizes = sizes.at[giver].add(-shifted).at[taker].add(shifted)
    items = jnp.searchsorted(jnp.cumsum(sizes), jnp.arange(rows * top), side="right").astype(jnp.int32)
    grid = items.reshape(top, rows).T
    grid = grid[jax.random.permutation(jax.random.fold_in(own, 1), rows)]
    rotation = jax.random.randint(jax.random.fold_in(own, 2), (rows, 1), 0, top)
    return jnp.take_along_axis(grid, (jnp.arange(top)[None, :] + rotation) % top, axis=1)


def load_shares(amount, total, reach, slope, full):
    portions = [(1 << 20) // math.isqrt(standing ** slope) + 1 for standing in range(1, amount + 1)]
    largest = reach if full else min(reach, max(-(-total // amount), total * portions[0] // sum(portions)))
    least = 1 if total - largest >= amount - 1 else 0
    holding, spare = [largest] + [least] * (amount - 1), total - largest - least * (amount - 1)
    while spare > 0:
        candidates = [i for i in range(1, amount) if holding[i] < largest] or [i for i in range(1, amount) if holding[i] < reach]
        mass, budget = sum([portions[i] for i in candidates]), spare
        for i in candidates:
            more = min(reach - holding[i], max(1, budget * portions[i] // mass), spare)
            holding[i] = holding[i] + more
            spare = spare - more
    return np.array(holding)


def centred(rng, shape, scale, most, cuts=(), kind=jnp.bfloat16):
    entries = scale * jax.random.normal(rng, shape, jnp.float32)
    if cuts:
        entries = entries * levels(rng, shape, cuts, -0.22, 0.18)
    return jnp.clip(entries, -most, most).astype(kind)


def setup_inputs(seed: int = 0, part: int = 0) -> dict:
    keys = jax.random.split(jax.random.key(seed), 11)
    own_keys = jax.random.split(jax.random.fold_in(keys[10], part), 11)
    hidden = centred(own_keys[0], (ROWS, MODEL_WIDTH), 1.0, 6.0, ((0, 8), (1, 2)))
    queries = draw_queries(jax.random.fold_in(jax.random.fold_in(keys[10], part), 71), part)
    key_value_weight = centred(keys[2], (MODEL_WIDTH, 2 * KEY_VALUE_HEADS * HEAD_SIZE), MODEL_WIDTH ** -0.5, 0.0625, ((0, 2),))
    adapter_down_weight = centred(keys[3], (ADAPTER_COUNT, MODEL_WIDTH, 2 * ADAPTER_RANK), MODEL_WIDTH ** -0.5, 0.0625, ((0, 8), (1, 2)))
    adapter_up_weight = centred(keys[4], (ADAPTER_COUNT, 2, ADAPTER_RANK, KEY_VALUE_HEADS * HEAD_SIZE), ADAPTER_RANK ** -0.5, 0.75, ((0, 8), (3, 2)))
    stored_cache_keys = draw_stored_cache_keys(jax.random.fold_in(jax.random.fold_in(keys[10], part), 71), part)
    stored_cache_values = centred(own_keys[6], (ROWS, KEY_VALUE_HEADS, CACHE, HEAD_SIZE), 1.0, 6.0, ((0, 8), (1, 2)))
    row_adapter_index_keys = jax.random.split(jax.random.fold_in(own_keys[7], 1), ROWS // ROWS_DEV)
    row_adapter_index_turns = jax.random.permutation(jax.random.fold_in(own_keys[7], 3), ROWS // ROWS_DEV)
    row_adapter_index = jax.vmap(lambda own, number: deal_out(jax.random.fold_in(own_keys[7], 2), own, number, ROWS_DEV, ADAPTER_COUNT, 1, CAP, 2))(row_adapter_index_keys, row_adapter_index_turns).reshape((ROWS, 1))
    stored_cache_lengths = draw_stored_cache_lengths(jax.random.fold_in(jax.random.fold_in(keys[10], part), 71), part)
    adapter_slot_table = jax.random.permutation(keys[9], ADAPTER_COUNT).astype(jnp.int32)
    return dict(hidden=hidden, queries=queries, key_value_weight=key_value_weight, adapter_down_weight=adapter_down_weight, adapter_up_weight=adapter_up_weight, stored_cache_keys=stored_cache_keys, stored_cache_values=stored_cache_values, row_adapter_index=row_adapter_index, stored_cache_lengths=stored_cache_lengths, adapter_slot_table=adapter_slot_table)


def adapter_update(hidden, adapter_down_weight, adapter_up_weight, row_slot_index):
    def per_row(operands):
        row_vector, pool_slot_index = operands
        down_weight_rows = lax.dynamic_index_in_dim(adapter_down_weight, pool_slot_index, 0, keepdims=False)
        up_weight_rows = lax.dynamic_index_in_dim(adapter_up_weight, pool_slot_index, 0, keepdims=False)
        reduced_input = jnp.dot(row_vector[None, :], down_weight_rows, preferred_element_type=jnp.float32)[0]
        reduced_input = lax.optimization_barrier(reduced_input.astype(jnp.bfloat16)).astype(jnp.float32)
        paired_rows = reduced_input.reshape(2, ADAPTER_RANK)
        return jnp.einsum("ck,ckm->cm", paired_rows, up_weight_rows.astype(jnp.float32))

    return lax.map(per_row, (hidden, row_slot_index))


def reference(hidden, queries, key_value_weight, adapter_down_weight, adapter_up_weight, stored_cache_keys, stored_cache_values, row_adapter_index, stored_cache_lengths, adapter_slot_table):
    batch_row_count = hidden.shape[0]
    group_size = QH // KEY_VALUE_HEADS
    projected_rows = jnp.dot(hidden, key_value_weight, preferred_element_type=jnp.float32)
    row_slot_index = adapter_slot_table[row_adapter_index[:, 0]].astype(jnp.int32)
    adapter_terms = adapter_update(hidden, adapter_down_weight, adapter_up_weight, row_slot_index)
    adapter_terms = adapter_terms.reshape(batch_row_count, 2, KEY_VALUE_HEADS, HEAD_SIZE).transpose(0, 2, 1, 3).reshape(batch_row_count, 2 * KEY_VALUE_HEADS * HEAD_SIZE)
    token_key_value = (projected_rows + adapter_terms).astype(jnp.bfloat16)
    heads_kv = token_key_value.reshape(batch_row_count, KEY_VALUE_HEADS, 2, HEAD_SIZE).astype(jnp.float32)
    new_keys = heads_kv[:, :, 0]
    new_values = heads_kv[:, :, 1]
    query_heads = queries.reshape(batch_row_count, KEY_VALUE_HEADS, group_size, HEAD_SIZE).astype(jnp.float32)
    score_scale = HEAD_SIZE ** -0.5
    cache_scores = jnp.einsum("rgqd,rgpd->rgqp", query_heads, stored_cache_keys.astype(jnp.float32)) * score_scale
    valid_mask = jnp.arange(CACHE)[None, :] < stored_cache_lengths[:, None]
    cache_scores = jnp.where(valid_mask[:, None, None, :], cache_scores, -jnp.inf)
    own_scores = jnp.einsum("rgqd,rgd->rgq", query_heads, new_keys) * score_scale
    highest = jnp.maximum(jnp.max(cache_scores, axis=-1), own_scores)
    cache_exp = jnp.exp(cache_scores - highest[..., None])
    own_exp = jnp.exp(own_scores - highest)
    denominator = jnp.sum(cache_exp, axis=-1) + own_exp
    cache_weights = lax.optimization_barrier((cache_exp / denominator[..., None]).astype(jnp.bfloat16)).astype(jnp.float32)
    own_weights = lax.optimization_barrier((own_exp / denominator).astype(jnp.bfloat16)).astype(jnp.float32)
    attended = jnp.einsum("rgqp,rgpd->rgqd", cache_weights, stored_cache_values.astype(jnp.float32))
    attended = attended + own_weights[..., None] * new_values[:, :, None, :]
    return token_key_value, attended.reshape(batch_row_count, QH * HEAD_SIZE).astype(jnp.bfloat16)
```

```python
import functools

import jax
import jax.numpy as jnp
from jax import lax
from jax.experimental import pallas as pl
from jax.experimental.pallas import tpu as pltpu
from jax.sharding import PartitionSpec as P

BF16 = jnp.bfloat16
F32 = jnp.float32
I32 = jnp.int32
VMEM_LIMIT = 48 * 1024 * 1024


def iota(shape, dim):
    return lax.broadcasted_iota(I32, shape, dim)


def split_count(cap):
    pieces = 4
    while cap * pieces % 16:
        pieces *= 2
    return pieces


def dot(a, b):
    return jnp.dot(a, b, preferred_element_type=F32)


def dot_first(a, b):
    return lax.dot_general(a, b, (((0,), (0,)), ((), ())), preferred_element_type=F32)


def exact_select(one_hot, x):
    high = x.astype(BF16)
    rest = x - high.astype(F32)
    middle = rest.astype(BF16)
    low = (rest - middle.astype(F32)).astype(BF16)
    return dot(one_hot, high) + (dot(one_hot, middle) + dot(one_hot, low))


def placement(rel, rank, cap, pieces):
    rows = rel.shape[1]
    code = rel * (pieces * cap) + rank
    codes = jnp.concatenate([code + piece * cap for piece in range(pieces)], axis=1)
    return codes


def pack_kernel(n, cap, pieces, me_ref, idx_ref, table_ref, hidden_ref, *out_refs):
    code_refs, chunk_refs = out_refs[:2], out_refs[2:]
    rows = hidden_ref.shape[0]
    width = hidden_ref.shape[1] // pieces
    me = me_ref[0]
    named = (iota((n, rows), 0) == idx_ref[...]).astype(F32).astype(BF16)
    table = jnp.broadcast_to(table_ref[...].astype(F32).astype(BF16), (16, n))
    slot = dot(table, named)[0:1, :].astype(I32)
    rel = lax.bitwise_xor(slot, me)
    member = (iota((n, rows), 0) == rel).astype(F32)
    before = (iota((rows, rows), 0) < iota((rows, rows), 1)).astype(F32).astype(BF16)
    count = dot(member.astype(BF16), before)
    rank = jnp.sum(member * count, axis=0, keepdims=True).astype(I32)
    code_refs[0][...] = rel
    code_refs[1][...] = rank
    codes = placement(rel, rank, cap, pieces)
    total = n * pieces * cap
    one_hot = (iota((total, pieces * rows), 0) == codes).astype(F32).astype(BF16)
    stacked = jnp.concatenate(
        [hidden_ref[:, piece * width : (piece + 1) * width] for piece in range(pieces)], axis=0
    )
    packed = dot(one_hot, stacked).astype(BF16)
    for s in range(n):
        chunk_refs[s][...] = packed[s * pieces * cap : (s + 1) * pieces * cap]


def shrink_kernel(n, cap, pieces, *refs):
    chunk_refs, down_ref, out_ref = refs[:n], refs[n], refs[n + 1]
    per = pieces * cap
    width = chunk_refs[0].shape[1]
    rank2 = down_ref.shape[2]
    received = jnp.concatenate([ref[...] for ref in chunk_refs], axis=0)
    total = jnp.zeros((n * per, rank2), F32)
    piece_of = (iota((n * per, rank2), 0) // cap) % pieces
    for piece in range(pieces):
        part = dot(received, down_ref[0, piece * width : (piece + 1) * width, :])
        total = total + jnp.where(piece_of == piece, part, 0.0)
    out_row, in_row = iota((n * cap, n * per), 0), iota((n * cap, n * per), 1)
    same = (out_row // cap == in_row // per) & (out_row % cap == in_row % cap)
    out_ref[...] = exact_select(same.astype(F32).astype(BF16), total)


def expand_kernel(n, cap, mine_ref, other_ref, up_ref, *out_refs):
    rank = up_ref.shape[2]
    head = 128
    blocks = up_ref.shape[3] // head
    reduced = (mine_ref[...] + other_ref[...]).astype(BF16)
    terms = []
    for c in range(2):
        kept = reduced[:, c * rank : (c + 1) * rank]
        wide = dot(kept, up_ref[0, c]).astype(BF16)
        terms += [wide[:, g * head : (g + 1) * head] for g in range(blocks)]
    stacked = jnp.concatenate(terms, axis=0)
    pieces = 2 * blocks
    per = pieces * cap
    size = n * per
    out_row, in_row = iota((size, size), 0), iota((size, size), 1)
    source = (out_row // cap % pieces) * (n * cap) + (out_row // per) * cap + out_row % cap
    moved = dot((source == in_row).astype(F32).astype(BF16), stacked).astype(BF16)
    for s in range(n):
        out_refs[s][...] = moved[s * per : (s + 1) * per]


def combine_kernel(n, cap, *refs):
    delta_refs = refs[:n]
    rel_ref, rank_ref, base_ref, other_ref, query_ref, max_ref, sum_ref, acc_ref, token_ref, out_ref = refs[n:]
    rows = base_ref.shape[0]
    head = 128
    groups = base_ref.shape[1] // (2 * head)
    pieces = 2 * groups
    total = n * pieces * cap
    codes = placement(rel_ref[...], rank_ref[...], cap, pieces)
    one_hot = (iota((total, pieces * rows), 0) == codes).astype(F32).astype(BF16)
    received = jnp.concatenate([ref[...] for ref in delta_refs], axis=0)
    delta = dot_first(one_hot, received)
    heads = query_ref.shape[1] // head
    per_group = heads // groups
    scale = head ** (-0.5)
    for g in range(groups):
        made = []
        for c in range(2):
            at = (g * 2 + c) * head
            piece = c * groups + g
            value = base_ref[:, at : at + head] + other_ref[:, at : at + head]
            value = (value + delta[piece * rows : (piece + 1) * rows]).astype(BF16)
            token_ref[:, at : at + head] = value
            made.append(value.astype(F32))
        key, value = made
        for h in range(g * per_group, (g + 1) * per_group):
            lanes = slice(h * head, (h + 1) * head)
            own = jnp.sum(query_ref[:, lanes].astype(F32) * key, axis=1, keepdims=True) * scale
            cache_max = max_ref[:, h : h + 1]
            highest = jnp.maximum(own, cache_max)
            cache_factor = jnp.exp(cache_max - highest)
            own_factor = jnp.exp(own - highest)
            inverse = 1.0 / (sum_ref[:, h : h + 1] * cache_factor + own_factor)
            out = acc_ref[:, lanes] * (cache_factor * inverse) + value * (own_factor * inverse)
            out_ref[:, lanes] = out.astype(BF16)


def call(kernel, outs, flops, bytes_accessed, smem_first=False, inputs=0):
    vmem = pl.BlockSpec(memory_space=pltpu.VMEM)
    specs = [vmem] * inputs
    if smem_first:
        specs[0] = pl.BlockSpec(memory_space=pltpu.SMEM)
    return pl.pallas_call(
        kernel,
        out_shape=outs,
        in_specs=specs,
        out_specs=[vmem] * len(outs),
        compiler_params=pltpu.CompilerParams(vmem_limit_bytes=VMEM_LIMIT),
        cost_estimate=pl.CostEstimate(flops=flops, bytes_accessed=bytes_accessed, transcendentals=0),
    )


def shards(
    hidden,
    queries,
    key_value_weight,
    adapter_down_weight,
    adapter_up_weight,
    stored_cache_keys,
    stored_cache_values,
    row_adapter_index,
    stored_cache_lengths,
    adapter_slot_table,
):
    n = lax.axis_size("pool")
    rows, width = hidden.shape
    cap = -(-2 * rows // n)
    pieces = split_count(cap)
    me = lax.axis_index("pool")
    groups = stored_cache_keys.shape[1]
    head = stored_cache_keys.shape[3]
    columns = key_value_weight.shape[1] // 2
    out_pieces = 2 * groups
    rank2 = adapter_down_weight.shape[2]

    def exchange(chunks):
        return [chunks[0]] + [
            lax.ppermute(chunks[s], "pool", [(i, i ^ s) for i in range(n)]) for s in range(1, n)
        ]

    swap = functools.partial(lax.ppermute, axis_name="tp", perm=[(0, 1), (1, 0)])

    packed = call(
        functools.partial(pack_kernel, n, cap, pieces),
        [jax.ShapeDtypeStruct((1, rows), I32)] * 2
        + [jax.ShapeDtypeStruct((pieces * cap, width // pieces), BF16)] * n,
        2 * n * cap * width * 64,
        3 * rows * width * 2,
        True,
        4,
    )(me.reshape(1), row_adapter_index.reshape(1, rows), adapter_slot_table.reshape(1, n), hidden)
    rel, rank = packed[:2]
    arrived = exchange(packed[2:])

    half = lax.axis_index("tp")
    partial_sum = jnp.dot(hidden, key_value_weight, preferred_element_type=F32)
    base_mine = lax.dynamic_slice_in_dim(partial_sum, half * columns, columns, axis=1)
    base_other = swap(lax.dynamic_slice_in_dim(partial_sum, (1 - half) * columns, columns, axis=1))

    query_heads = queries.reshape(rows, groups, -1, head)
    scores = jnp.einsum("rgqd,rgpd->rgqp", query_heads, stored_cache_keys, preferred_element_type=F32)
    scores = scores * (head ** (-0.5))
    valid = jnp.arange(stored_cache_keys.shape[2])[None, :] < stored_cache_lengths[:, None]
    scores = jnp.where(valid[:, None, None, :], scores, -jnp.inf)
    cache_max = jnp.max(scores, axis=-1)
    weights = jnp.exp(scores - cache_max[..., None])
    cache_sum = jnp.sum(weights, axis=-1).reshape(rows, -1)
    attended = jnp.einsum(
        "rgqp,rgpd->rgqd", weights.astype(BF16), stored_cache_values, preferred_element_type=F32
    ).reshape(rows, -1)
    cache_max = cache_max.reshape(rows, -1)

    (reduced,) = call(
        functools.partial(shrink_kernel, n, cap, pieces),
        [jax.ShapeDtypeStruct((n * cap, rank2), F32)],
        2 * n * cap * width * rank2,
        n * cap * width * 2 + width * rank2 * 2,
        False,
        n + 1,
    )(*arrived, adapter_down_weight)
    reduced_other = swap(reduced)
    terms = call(
        functools.partial(expand_kernel, n, cap),
        [jax.ShapeDtypeStruct((out_pieces * cap, head), BF16)] * n,
        2 * n * cap * rank2 * columns,
        n * cap * columns * 4,
        False,
        3,
    )(reduced, reduced_other, adapter_up_weight)
    deltas = exchange(terms)
    token, out = call(
        functools.partial(combine_kernel, n, cap),
        [jax.ShapeDtypeStruct((rows, columns), BF16), jax.ShapeDtypeStruct(queries.shape, BF16)],
        2 * n * cap * columns * rows,
        rows * 2048 * 8,
        False,
        n + 8,
    )(*deltas, rel, rank, base_mine, base_other, queries, cache_max, cache_sum, attended)
    return token, out


def solution(mesh):
    in_specs = (
        P(("grp", "pool"), "tp"),
        P(("grp", "pool"), "tp"),
        P("tp", None),
        P("pool", "tp", None),
        P("pool", None, None, "tp"),
        P(("grp", "pool"), "tp", None, None),
        P(("grp", "pool"), "tp", None, None),
        P(("grp", "pool"), None),
        P(("grp", "pool")),
        P(),
    )
    out_specs = (P(("grp", "pool"), "tp"), P(("grp", "pool"), "tp"))
    return jax.shard_map(shards, mesh=mesh, in_specs=in_specs, out_specs=out_specs, check_vma=False)
```

```python
import functools

import jax
import jax.numpy as jnp
from jax import lax
from jax.experimental import pallas as pl
from jax.experimental.pallas import tpu as pltpu
from jax.sharding import PartitionSpec as P

BF16 = jnp.bfloat16
F32 = jnp.float32
I32 = jnp.int32
VMEM_LIMIT = 48 * 1024 * 1024


def iota(shape, dim):
    return lax.broadcasted_iota(I32, shape, dim)


def split_count(cap):
    pieces = 4
    while cap * pieces % 16:
        pieces *= 2
    return pieces


def dot(a, b):
    return jnp.dot(a, b, preferred_element_type=F32)


def dot_first(a, b):
    return lax.dot_general(a, b, (((0,), (0,)), ((), ())), preferred_element_type=F32)


def exact_select(one_hot, x):
    high = x.astype(BF16)
    rest = x - high.astype(F32)
    middle = rest.astype(BF16)
    low = (rest - middle.astype(F32)).astype(BF16)
    return dot(one_hot, high) + (dot(one_hot, middle) + dot(one_hot, low))


def placement(slot, rank, cap, pieces):
    code = slot * (pieces * cap) + rank
    codes = jnp.concatenate([code + piece * cap for piece in range(pieces)], axis=1)
    return codes


def pack_kernel(n, cap, pieces, idx_ref, table_ref, hidden_ref, slot_ref, rank_ref, packed_ref):
    rows = hidden_ref.shape[0]
    width = hidden_ref.shape[1] // pieces
    named = (iota((n, rows), 0) == idx_ref[...]).astype(F32).astype(BF16)
    table = jnp.broadcast_to(table_ref[...].astype(F32).astype(BF16), (16, n))
    slot = dot(table, named)[0:1, :].astype(I32)
    member = (iota((n, rows), 0) == slot).astype(F32)
    before = (iota((rows, rows), 0) < iota((rows, rows), 1)).astype(F32).astype(BF16)
    count = dot(member.astype(BF16), before)
    rank = jnp.sum(member * count, axis=0, keepdims=True).astype(I32)
    slot_ref[...] = slot
    rank_ref[...] = rank
    codes = placement(slot, rank, cap, pieces)
    total = n * pieces * cap
    one_hot = (iota((total, pieces * rows), 0) == codes).astype(F32).astype(BF16)
    stacked = jnp.concatenate(
        [hidden_ref[:, piece * width : (piece + 1) * width] for piece in range(pieces)], axis=0
    )
    packed_ref[...] = dot(one_hot, stacked).astype(BF16)


def shrink_kernel(n, cap, pieces, received_ref, down_ref, out_ref):
    per = pieces * cap
    width = received_ref.shape[1]
    rank2 = down_ref.shape[2]
    received = received_ref[...]
    total = jnp.zeros((n * per, rank2), F32)
    piece_of = (iota((n * per, rank2), 0) // cap) % pieces
    for piece in range(pieces):
        part = dot(received, down_ref[0, piece * width : (piece + 1) * width, :])
        total = total + jnp.where(piece_of == piece, part, 0.0)
    out_row, in_row = iota((n * cap, n * per), 0), iota((n * cap, n * per), 1)
    same = (out_row // cap == in_row // per) & (out_row % cap == in_row % cap)
    out_ref[...] = exact_select(same.astype(F32).astype(BF16), total)


def expand_kernel(n, cap, mine_ref, other_ref, up_ref, out_ref):
    rank = up_ref.shape[2]
    head = 128
    blocks = up_ref.shape[3] // head
    reduced = (mine_ref[...] + other_ref[...]).astype(BF16)
    terms = []
    for c in range(2):
        kept = reduced[:, c * rank : (c + 1) * rank]
        wide = dot(kept, up_ref[0, c]).astype(BF16)
        terms += [wide[:, g * head : (g + 1) * head] for g in range(blocks)]
    stacked = jnp.concatenate(terms, axis=0)
    pieces = 2 * blocks
    per = pieces * cap
    size = n * per
    out_row, in_row = iota((size, size), 0), iota((size, size), 1)
    source = (out_row // cap % pieces) * (n * cap) + (out_row // per) * cap + out_row % cap
    out_ref[...] = dot((source == in_row).astype(F32).astype(BF16), stacked).astype(BF16)


def combine_kernel(
    n,
    cap,
    delta_ref,
    slot_ref,
    rank_ref,
    base_ref,
    other_ref,
    query_ref,
    max_ref,
    sum_ref,
    acc_ref,
    token_ref,
    out_ref,
):
    rows = base_ref.shape[0]
    head = 128
    groups = base_ref.shape[1] // (2 * head)
    pieces = 2 * groups
    total = n * pieces * cap
    codes = placement(slot_ref[...], rank_ref[...], cap, pieces)
    one_hot = (iota((total, pieces * rows), 0) == codes).astype(F32).astype(BF16)
    delta = dot_first(one_hot, delta_ref[...])
    heads = query_ref.shape[1] // head
    per_group = heads // groups
    scale = head ** (-0.5)
    for g in range(groups):
        made = []
        for c in range(2):
            at = (g * 2 + c) * head
            piece = c * groups + g
            value = base_ref[:, at : at + head] + other_ref[:, at : at + head]
            value = (value + delta[piece * rows : (piece + 1) * rows]).astype(BF16)
            token_ref[:, at : at + head] = value
            made.append(value.astype(F32))
        key, value = made
        for h in range(g * per_group, (g + 1) * per_group):
            lanes = slice(h * head, (h + 1) * head)
            own = jnp.sum(query_ref[:, lanes].astype(F32) * key, axis=1, keepdims=True) * scale
            cache_max = max_ref[:, h : h + 1]
            highest = jnp.maximum(own, cache_max)
            cache_factor = jnp.exp(cache_max - highest)
            own_factor = jnp.exp(own - highest)
            inverse = 1.0 / (sum_ref[:, h : h + 1] * cache_factor + own_factor)
            out = acc_ref[:, lanes] * (cache_factor * inverse) + value * (own_factor * inverse)
            out_ref[:, lanes] = out.astype(BF16)


def call(kernel, outs, flops, bytes_accessed, inputs):
    vmem = pl.BlockSpec(memory_space=pltpu.VMEM)
    return pl.pallas_call(
        kernel,
        out_shape=outs,
        in_specs=[vmem] * inputs,
        out_specs=[vmem] * len(outs),
        compiler_params=pltpu.CompilerParams(vmem_limit_bytes=VMEM_LIMIT),
        cost_estimate=pl.CostEstimate(flops=flops, bytes_accessed=bytes_accessed, transcendentals=0),
    )


def shards(
    hidden,
    queries,
    key_value_weight,
    adapter_down_weight,
    adapter_up_weight,
    stored_cache_keys,
    stored_cache_values,
    row_adapter_index,
    stored_cache_lengths,
    adapter_slot_table,
):
    n = lax.axis_size("pool")
    rows, width = hidden.shape
    cap = -(-2 * rows // n)
    pieces = split_count(cap)
    groups = stored_cache_keys.shape[1]
    head = stored_cache_keys.shape[3]
    columns = key_value_weight.shape[1] // 2
    out_pieces = 2 * groups
    rank2 = adapter_down_weight.shape[2]

    def exchange(chunks):
        return lax.all_to_all(chunks, "pool", split_axis=0, concat_axis=0, tiled=True)

    swap = functools.partial(lax.ppermute, axis_name="tp", perm=[(0, 1), (1, 0)])

    slot, rank, packed = call(
        functools.partial(pack_kernel, n, cap, pieces),
        [jax.ShapeDtypeStruct((1, rows), I32)] * 2
        + [jax.ShapeDtypeStruct((n * pieces * cap, width // pieces), BF16)],
        2 * n * cap * width * 64,
        3 * rows * width * 2,
        3,
    )(row_adapter_index.reshape(1, rows), adapter_slot_table.reshape(1, n), hidden)
    arrived = exchange(packed)

    half = lax.axis_index("tp")
    partial_sum = jnp.dot(hidden, key_value_weight, preferred_element_type=F32)
    base_mine = lax.dynamic_slice_in_dim(partial_sum, half * columns, columns, axis=1)
    base_other = swap(lax.dynamic_slice_in_dim(partial_sum, (1 - half) * columns, columns, axis=1))

    query_heads = queries.reshape(rows, groups, -1, head)
    scores = jnp.einsum("rgqd,rgpd->rgqp", query_heads, stored_cache_keys, preferred_element_type=F32)
    scores = scores * (head ** (-0.5))
    valid = jnp.arange(stored_cache_keys.shape[2])[None, :] < stored_cache_lengths[:, None]
    scores = jnp.where(valid[:, None, None, :], scores, -jnp.inf)
    cache_max = jnp.max(scores, axis=-1)
    weights = jnp.exp(scores - cache_max[..., None])
    cache_sum = jnp.sum(weights, axis=-1).reshape(rows, -1)
    attended = jnp.einsum(
        "rgqp,rgpd->rgqd", weights.astype(BF16), stored_cache_values, preferred_element_type=F32
    ).reshape(rows, -1)
    cache_max = cache_max.reshape(rows, -1)

    (reduced,) = call(
        functools.partial(shrink_kernel, n, cap, pieces),
        [jax.ShapeDtypeStruct((n * cap, rank2), F32)],
        2 * n * cap * width * rank2,
        n * cap * width * 2 + width * rank2 * 2,
        2,
    )(arrived, adapter_down_weight)
    reduced_other = swap(reduced)
    (terms,) = call(
        functools.partial(expand_kernel, n, cap),
        [jax.ShapeDtypeStruct((n * out_pieces * cap, head), BF16)],
        2 * n * cap * rank2 * columns,
        n * cap * columns * 4,
        3,
    )(reduced, reduced_other, adapter_up_weight)
    deltas = exchange(terms)
    token, out = call(
        functools.partial(combine_kernel, n, cap),
        [jax.ShapeDtypeStruct((rows, columns), BF16), jax.ShapeDtypeStruct(queries.shape, BF16)],
        2 * n * cap * columns * rows,
        rows * 2048 * 8,
        9,
    )(deltas, slot, rank, base_mine, base_other, queries, cache_max, cache_sum, attended)
    return token, out


def solution(mesh):
    in_specs = (
        P(("grp", "pool"), "tp"),
        P(("grp", "pool"), "tp"),
        P("tp", None),
        P("pool", "tp", None),
        P("pool", None, None, "tp"),
        P(("grp", "pool"), "tp", None, None),
        P(("grp", "pool"), "tp", None, None),
        P(("grp", "pool"), None),
        P(("grp", "pool")),
        P(),
    )
    out_specs = (P(("grp", "pool"), "tp"), P(("grp", "pool"), "tp"))
    return jax.shard_map(shards, mesh=mesh, in_specs=in_specs, out_specs=out_specs, check_vma=False)
```

```python
import functools

import jax
import jax.numpy as jnp
from jax import lax
from jax.experimental import pallas as pl
from jax.experimental.pallas import tpu as pltpu
from jax.sharding import PartitionSpec as P

BF16 = jnp.bfloat16
F32 = jnp.float32
I32 = jnp.int32
VMEM_LIMIT = 48 * 1024 * 1024


def iota(shape, dim):
    return lax.broadcasted_iota(I32, shape, dim)


def split_count(cap):
    pieces = 4
    while cap * pieces % 16:
        pieces *= 2
    return pieces


def dot(a, b):
    return jnp.dot(a, b, preferred_element_type=F32)


def dot_first(a, b):
    return lax.dot_general(a, b, (((0,), (0,)), ((), ())), preferred_element_type=F32)


def exact_select(one_hot, x):
    high = x.astype(BF16)
    rest = x - high.astype(F32)
    middle = rest.astype(BF16)
    low = (rest - middle.astype(F32)).astype(BF16)
    return dot(one_hot, high) + (dot(one_hot, middle) + dot(one_hot, low))


def placement(slot, rank, cap, pieces):
    code = slot * (pieces * cap) + rank
    codes = jnp.concatenate([code + piece * cap for piece in range(pieces)], axis=1)
    return codes


def pack_kernel(n, cap, pieces, me_ref, idx_hbm, table_hbm, hidden_hbm, slot_ref, rank_ref, near_ref, *refs):
    far_refs, (idx_ref, table_ref, hidden_ref, sems) = refs[:-4], refs[-4:]
    copies = [
        pltpu.make_async_copy(source, target, sems.at[i])
        for i, (source, target) in enumerate(
            [(idx_hbm, idx_ref), (table_hbm, table_ref), (hidden_hbm, hidden_ref)]
        )
    ]
    for copy in copies:
        copy.start()
    rows = hidden_ref.shape[0]
    width = hidden_ref.shape[1] // pieces
    per = pieces * cap
    me = me_ref[0]
    half = n // 2
    copies[0].wait()
    copies[1].wait()
    named = (iota((n, rows), 0) == idx_ref[...]).astype(F32).astype(BF16)
    table = jnp.broadcast_to(table_ref[...].astype(F32).astype(BF16), (16, n))
    slot = dot(table, named)[0:1, :].astype(I32)
    member = (iota((n, rows), 0) == slot).astype(F32)
    before = (iota((rows, rows), 0) < iota((rows, rows), 1)).astype(F32).astype(BF16)
    count = dot(member.astype(BF16), before)
    rank = jnp.sum(member * count, axis=0, keepdims=True).astype(I32)
    slot_ref[...] = slot
    rank_ref[...] = rank
    apart = lax.bitwise_xor(slot, me)
    place = jnp.where(apart < half, lax.bitwise_and(slot, half - 1), apart)
    codes = placement(place, rank, cap, pieces)
    one_hot = (iota((n * per, pieces * rows), 0) == codes).astype(F32).astype(BF16)
    copies[2].wait()
    stacked = jnp.concatenate(
        [hidden_ref[:, piece * width : (piece + 1) * width] for piece in range(pieces)], axis=0
    )
    packed = dot(one_hot, stacked).astype(BF16)
    near_ref[...] = packed[: half * per]
    for s in range(half, n):
        far_refs[s - half][...] = packed[s * per : (s + 1) * per]


def shrink_kernel(n, cap, pieces, *refs):
    received_refs, down_ref, out_ref = refs[:-2], refs[-2], refs[-1]
    per = pieces * cap
    width = received_refs[0].shape[1]
    rank2 = down_ref.shape[2]
    received = jnp.concatenate([ref[...] for ref in received_refs], axis=0)
    total = jnp.zeros((n * per, rank2), F32)
    piece_of = (iota((n * per, rank2), 0) // cap) % pieces
    for piece in range(pieces):
        part = dot(received, down_ref[0, piece * width : (piece + 1) * width, :])
        total = total + jnp.where(piece_of == piece, part, 0.0)
    out_row, in_row = iota((n * cap, n * per), 0), iota((n * cap, n * per), 1)
    same = (out_row // cap == in_row // per) & (out_row % cap == in_row % cap)
    out_ref[...] = exact_select(same.astype(F32).astype(BF16), total)


def expand_kernel(n, cap, me_ref, mine_ref, other_ref, up_ref, out_ref):
    rank = up_ref.shape[2]
    head = 128
    blocks = up_ref.shape[3] // head
    reduced = (mine_ref[...] + other_ref[...]).astype(BF16)
    terms = []
    for c in range(2):
        kept = reduced[:, c * rank : (c + 1) * rank]
        wide = dot(kept, up_ref[0, c]).astype(BF16)
        terms += [wide[:, g * head : (g + 1) * head] for g in range(blocks)]
    stacked = jnp.concatenate(terms, axis=0)
    pieces = 2 * blocks
    per = pieces * cap
    size = n * per
    out_row, in_row = iota((size, size), 0), iota((size, size), 1)
    apart = lax.bitwise_xor(out_row // per, me_ref[0])
    place = jnp.where(apart < n // 2, lax.bitwise_and(out_row // per, n // 2 - 1), apart)
    source = (out_row // cap % pieces) * (n * cap) + place * cap + out_row % cap
    out_ref[...] = dot((source == in_row).astype(F32).astype(BF16), stacked).astype(BF16)


def combine_kernel(
    n,
    cap,
    delta_ref,
    slot_ref,
    rank_ref,
    base_ref,
    other_ref,
    query_ref,
    max_ref,
    sum_ref,
    acc_ref,
    token_ref,
    out_ref,
):
    rows = base_ref.shape[0]
    head = 128
    groups = base_ref.shape[1] // (2 * head)
    pieces = 2 * groups
    total = n * pieces * cap
    codes = placement(slot_ref[...], rank_ref[...], cap, pieces)
    one_hot = (iota((total, pieces * rows), 0) == codes).astype(F32).astype(BF16)
    delta = dot_first(one_hot, delta_ref[...])
    heads = query_ref.shape[1] // head
    per_group = heads // groups
    scale = head ** (-0.5)
    for g in range(groups):
        made = []
        for c in range(2):
            at = (g * 2 + c) * head
            piece = c * groups + g
            value = base_ref[:, at : at + head] + other_ref[:, at : at + head]
            value = (value + delta[piece * rows : (piece + 1) * rows]).astype(BF16)
            token_ref[:, at : at + head] = value
            made.append(value.astype(F32))
        key, value = made
        for h in range(g * per_group, (g + 1) * per_group):
            lanes = slice(h * head, (h + 1) * head)
            own = jnp.sum(query_ref[:, lanes].astype(F32) * key, axis=1, keepdims=True) * scale
            cache_max = max_ref[:, h : h + 1]
            highest = jnp.maximum(own, cache_max)
            cache_factor = jnp.exp(cache_max - highest)
            own_factor = jnp.exp(own - highest)
            inverse = 1.0 / (sum_ref[:, h : h + 1] * cache_factor + own_factor)
            out = acc_ref[:, lanes] * (cache_factor * inverse) + value * (own_factor * inverse)
            out_ref[:, lanes] = out.astype(BF16)


VMEM = pl.BlockSpec(memory_space=pltpu.VMEM)
SMEM = pl.BlockSpec(memory_space=pltpu.SMEM)
ANY = pl.BlockSpec(memory_space=pl.ANY)


def call(kernel, outs, flops, bytes_accessed, specs, scratch=()):
    return pl.pallas_call(
        kernel,
        out_shape=outs,
        in_specs=specs,
        out_specs=[VMEM] * len(outs),
        scratch_shapes=scratch,
        compiler_params=pltpu.CompilerParams(vmem_limit_bytes=VMEM_LIMIT),
        cost_estimate=pl.CostEstimate(flops=flops, bytes_accessed=bytes_accessed, transcendentals=0),
    )


def shards(
    hidden,
    queries,
    key_value_weight,
    adapter_down_weight,
    adapter_up_weight,
    stored_cache_keys,
    stored_cache_values,
    row_adapter_index,
    stored_cache_lengths,
    adapter_slot_table,
):
    n = lax.axis_size("pool")
    rows, width = hidden.shape
    cap = -(-2 * rows // n)
    pieces = split_count(cap)
    groups = stored_cache_keys.shape[1]
    head = stored_cache_keys.shape[3]
    columns = key_value_weight.shape[1] // 2
    out_pieces = 2 * groups
    rank2 = adapter_down_weight.shape[2]

    swap = functools.partial(lax.ppermute, axis_name="tp", perm=[(0, 1), (1, 0)])

    half = n // 2
    per = pieces * cap
    me = lax.axis_index("pool").reshape(1)
    slot, rank, near, *far = call(
        functools.partial(pack_kernel, n, cap, pieces),
        [jax.ShapeDtypeStruct((1, rows), I32)] * 2
        + [jax.ShapeDtypeStruct((half * per, width // pieces), BF16)]
        + [jax.ShapeDtypeStruct((per, width // pieces), BF16)] * half,
        2 * n * cap * width * 64,
        3 * rows * width * 2,
        [SMEM, ANY, ANY, ANY],
        [
            pltpu.VMEM((1, rows), I32),
            pltpu.VMEM((1, n), I32),
            pltpu.VMEM((rows, width), BF16),
            pltpu.SemaphoreType.DMA((3,)),
        ],
    )(me, row_adapter_index.reshape(1, rows), adapter_slot_table.reshape(1, n), hidden)
    far = [
        lax.ppermute(chunk, "pool", [(i, i ^ s) for i in range(n)]) for s, chunk in enumerate(far, half)
    ]
    near = lax.all_to_all(
        near,
        "pool",
        split_axis=0,
        concat_axis=0,
        tiled=True,
        axis_index_groups=[list(range(half)), list(range(half, n))],
    )

    core = lax.axis_index("tp")
    partial_sum = jnp.dot(hidden, key_value_weight, preferred_element_type=F32)
    base_mine = lax.dynamic_slice_in_dim(partial_sum, core * columns, columns, axis=1)
    base_other = swap(lax.dynamic_slice_in_dim(partial_sum, (1 - core) * columns, columns, axis=1))

    query_heads = queries.reshape(rows, groups, -1, head)
    scores = jnp.einsum("rgqd,rgpd->rgqp", query_heads, stored_cache_keys, preferred_element_type=F32)
    scores = scores * (head ** (-0.5))
    valid = jnp.arange(stored_cache_keys.shape[2])[None, :] < stored_cache_lengths[:, None]
    scores = jnp.where(valid[:, None, None, :], scores, -jnp.inf)
    cache_max = jnp.max(scores, axis=-1)
    weights = jnp.exp(scores - cache_max[..., None])
    cache_sum = jnp.sum(weights, axis=-1).reshape(rows, -1)
    attended = jnp.einsum(
        "rgqp,rgpd->rgqd", weights.astype(BF16), stored_cache_values, preferred_element_type=F32
    ).reshape(rows, -1)
    cache_max = cache_max.reshape(rows, -1)

    (reduced,) = call(
        functools.partial(shrink_kernel, n, cap, pieces),
        [jax.ShapeDtypeStruct((n * cap, rank2), F32)],
        2 * n * cap * width * rank2,
        n * cap * width * 2 + width * rank2 * 2,
        [VMEM] * (half + 2),
    )(near, *far, adapter_down_weight)
    reduced_other = swap(reduced)
    (terms,) = call(
        functools.partial(expand_kernel, n, cap),
        [jax.ShapeDtypeStruct((n * out_pieces * cap, head), BF16)],
        2 * n * cap * rank2 * columns,
        n * cap * columns * 4,
        [SMEM, VMEM, VMEM, VMEM],
    )(me, reduced, reduced_other, adapter_up_weight)
    deltas = lax.all_to_all(terms, "pool", split_axis=0, concat_axis=0, tiled=True)
    token, out = call(
        functools.partial(combine_kernel, n, cap),
        [jax.ShapeDtypeStruct((rows, columns), BF16), jax.ShapeDtypeStruct(queries.shape, BF16)],
        2 * n * cap * columns * rows,
        rows * 2048 * 8,
        [VMEM] * 9,
    )(deltas, slot, rank, base_mine, base_other, queries, cache_max, cache_sum, attended)
    return token, out


def solution(mesh):
    in_specs = (
        P(("grp", "pool"), "tp"),
        P(("grp", "pool"), "tp"),
        P("tp", None),
        P("pool", "tp", None),
        P("pool", None, None, "tp"),
        P(("grp", "pool"), "tp", None, None),
        P(("grp", "pool"), "tp", None, None),
        P(("grp", "pool"), None),
        P(("grp", "pool")),
        P(),
    )
    out_specs = (P(("grp", "pool"), "tp"), P(("grp", "pool"), "tp"))
    return jax.shard_map(shards, mesh=mesh, in_specs=in_specs, out_specs=out_specs, check_vma=False)
```

```python
import functools

import jax
import jax.numpy as jnp
from jax import lax
from jax.experimental import pallas as pl
from jax.experimental.pallas import tpu as pltpu
from jax.sharding import PartitionSpec as P

BF16 = jnp.bfloat16
F32 = jnp.float32
I32 = jnp.int32
VMEM_LIMIT = 48 * 1024 * 1024


def iota(shape, dim):
    return lax.broadcasted_iota(I32, shape, dim)


def split_count(cap):
    pieces = 4
    while cap * pieces % 16:
        pieces *= 2
    return pieces


def dot(a, b):
    return jnp.dot(a, b, preferred_element_type=F32)


def dot_first(a, b):
    return lax.dot_general(a, b, (((0,), (0,)), ((), ())), preferred_element_type=F32)


def exact_select(one_hot, x):
    high = x.astype(BF16)
    rest = x - high.astype(F32)
    middle = rest.astype(BF16)
    low = (rest - middle.astype(F32)).astype(BF16)
    return dot(one_hot, high) + (dot(one_hot, middle) + dot(one_hot, low))


def codes_of(place, rank, cap, pieces):
    code = place * (pieces * cap) + rank
    return jnp.concatenate([code + piece * cap for piece in range(pieces)], axis=1)


def one_hot_of(codes, first, count):
    return ((iota((count, codes.shape[1]), 0) + first) == codes).astype(F32).astype(BF16)


def stack_pieces(hidden, pieces):
    width = hidden.shape[1] // pieces
    return jnp.concatenate(
        [hidden[:, piece * width : (piece + 1) * width] for piece in range(pieces)], axis=0
    )


def pack_far_kernel(n, cap, pieces, me_ref, idx_hbm, table_hbm, hidden_hbm, place_ref, rank_ref, *refs):
    far_refs, (idx_ref, table_ref, hidden_ref, sems) = refs[:-4], refs[-4:]
    copies = [
        pltpu.make_async_copy(source, target, sems.at[i])
        for i, (source, target) in enumerate(
            [(idx_hbm, idx_ref), (table_hbm, table_ref), (hidden_hbm, hidden_ref)]
        )
    ]
    for copy in copies:
        copy.start()
    rows = hidden_ref.shape[0]
    per = pieces * cap
    half = n // 2
    copies[0].wait()
    copies[1].wait()
    named = (iota((n, rows), 0) == idx_ref[...]).astype(F32).astype(BF16)
    table = jnp.broadcast_to(table_ref[...].astype(F32).astype(BF16), (16, n))
    slot = dot(table, named)[0:1, :].astype(I32)
    member = (iota((n, rows), 0) == slot).astype(F32)
    before = (iota((rows, rows), 0) < iota((rows, rows), 1)).astype(F32).astype(BF16)
    count = dot(member.astype(BF16), before)
    rank = jnp.sum(member * count, axis=0, keepdims=True).astype(I32)
    apart = lax.bitwise_xor(slot, me_ref[0])
    place = jnp.where(apart < half, lax.bitwise_and(slot, half - 1), apart)
    place_ref[...] = place
    rank_ref[...] = rank
    one_hot = one_hot_of(codes_of(place, rank, cap, pieces), half * per, half * per)
    copies[2].wait()
    packed = dot(one_hot, stack_pieces(hidden_ref[...], pieces)).astype(BF16)
    for s in range(half):
        far_refs[s][...] = packed[s * per : (s + 1) * per]


def pack_near_kernel(cap, pieces, place_ref, rank_ref, hidden_ref, near_ref):
    one_hot = one_hot_of(codes_of(place_ref[...], rank_ref[...], cap, pieces), 0, near_ref.shape[0])
    near_ref[...] = dot(one_hot, stack_pieces(hidden_ref[...], pieces)).astype(BF16)


def shrink_kernel(cap, pieces, count, *refs):
    received_refs, down_ref, out_ref = refs[:count], refs[count], refs[-1]
    per = pieces * cap
    width = received_refs[0].shape[1]
    rank2 = down_ref.shape[2]
    received = jnp.concatenate([ref[...] for ref in received_refs], axis=0)
    size = received.shape[0]
    total = jnp.zeros((size, rank2), F32)
    piece_of = (iota((size, rank2), 0) // cap) % pieces
    for piece in range(pieces):
        part = dot(received, down_ref[0, piece * width : (piece + 1) * width, :])
        total = total + jnp.where(piece_of == piece, part, 0.0)
    out_row, in_row = iota((size // pieces, size), 0), iota((size // pieces, size), 1)
    same = (out_row // cap == in_row // per) & (out_row % cap == in_row % cap)
    out_ref[...] = exact_select(same.astype(F32).astype(BF16), total)


def expand_kernel(cap, mine_ref, other_ref, up_ref, *out_refs):
    rank = up_ref.shape[2]
    head = 128
    blocks = up_ref.shape[3] // head
    reduced = (mine_ref[...] + other_ref[...]).astype(BF16)
    terms = []
    for c in range(2):
        kept = reduced[:, c * rank : (c + 1) * rank]
        wide = dot(kept, up_ref[0, c]).astype(BF16)
        terms += [wide[:, g * head : (g + 1) * head] for g in range(blocks)]
    stacked = jnp.concatenate(terms, axis=0)
    pieces = 2 * blocks
    per = pieces * cap
    size = stacked.shape[0]
    out_row, in_row = iota((size, size), 0), iota((size, size), 1)
    source = (out_row // cap % pieces) * (size // pieces) + (out_row // per) * cap + out_row % cap
    moved = dot((source == in_row).astype(F32).astype(BF16), stacked).astype(BF16)
    each = size // len(out_refs)
    for s, out_ref in enumerate(out_refs):
        out_ref[...] = moved[s * each : (s + 1) * each]


def precombine_kernel(cap, near_ref, place_ref, rank_ref, mine_ref, other_ref, base_ref, far_ref):
    rows = base_ref.shape[0]
    head = 128
    groups = base_ref.shape[1] // (2 * head)
    pieces = 2 * groups
    size = near_ref.shape[0]
    codes = codes_of(place_ref[...], rank_ref[...], cap, pieces)
    delta = dot_first(one_hot_of(codes, 0, size), near_ref[...])
    for g in range(groups):
        for c in range(2):
            at = (g * 2 + c) * head
            piece = c * groups + g
            value = mine_ref[:, at : at + head] + other_ref[:, at : at + head]
            base_ref[:, at : at + head] = value + delta[piece * rows : (piece + 1) * rows]
    same = (iota((size, size), 0) == iota((size, size), 1)).astype(F32).astype(BF16)
    far_ref[...] = dot_first(one_hot_of(codes, size, size), same).astype(BF16)


def combine_kernel(*refs):
    delta_refs = refs[:-8]
    one_hot_ref, base_ref, query_ref, max_ref, sum_ref, acc_ref, token_ref, out_ref = refs[-8:]
    rows = base_ref.shape[0]
    head = 128
    groups = base_ref.shape[1] // (2 * head)
    received = jnp.concatenate([ref[...] for ref in delta_refs], axis=0)
    delta = dot(one_hot_ref[...], received)
    heads = query_ref.shape[1] // head
    per_group = heads // groups
    scale = head ** (-0.5)
    lane = iota((rows, head), 1)
    own = jnp.zeros((rows, head), F32)
    values = []
    for g in range(groups):
        made = []
        for c in range(2):
            at = (g * 2 + c) * head
            piece = c * groups + g
            made.append((base_ref[:, at : at + head] + delta[piece * rows : (piece + 1) * rows]).astype(BF16))
            token_ref[:, at : at + head] = made[-1]
        key = made[0].astype(F32)
        values.append(made[1].astype(F32))
        for h in range(g * per_group, (g + 1) * per_group):
            query = query_ref[:, h * head : (h + 1) * head].astype(F32)
            own = jnp.where(lane == h, jnp.sum(query * key, axis=1, keepdims=True), own)
    own = own[:, :heads] * scale
    cache_max = max_ref[...]
    highest = jnp.maximum(own, cache_max)
    cache_factor = jnp.exp(cache_max - highest)
    own_factor = jnp.exp(own - highest)
    inverse = 1.0 / (sum_ref[...] * cache_factor + own_factor)
    cache_factor = cache_factor * inverse
    own_factor = own_factor * inverse
    for h in range(heads):
        lanes = slice(h * head, (h + 1) * head)
        out = acc_ref[:, lanes] * cache_factor[:, h : h + 1]
        out = out + values[h // per_group] * own_factor[:, h : h + 1]
        out_ref[:, lanes] = out.astype(BF16)


VMEM = pl.BlockSpec(memory_space=pltpu.VMEM)
SMEM = pl.BlockSpec(memory_space=pltpu.SMEM)
HBM = pl.BlockSpec(memory_space=pltpu.HBM)
ANY = pl.BlockSpec(memory_space=pl.ANY)


def call(kernel, outs, flops, bytes_accessed, specs, scratch=()):
    return pl.pallas_call(
        kernel,
        out_shape=outs,
        in_specs=specs,
        out_specs=[VMEM] * len(outs),
        scratch_shapes=scratch,
        compiler_params=pltpu.CompilerParams(vmem_limit_bytes=VMEM_LIMIT),
        cost_estimate=pl.CostEstimate(flops=flops, bytes_accessed=bytes_accessed, transcendentals=0),
    )


def shards(
    hidden,
    queries,
    key_value_weight,
    adapter_down_weight,
    adapter_up_weight,
    stored_cache_keys,
    stored_cache_values,
    row_adapter_index,
    stored_cache_lengths,
    adapter_slot_table,
):
    n = lax.axis_size("pool")
    rows, width = hidden.shape
    cap = -(-2 * rows // n)
    pieces = split_count(cap)
    groups = stored_cache_keys.shape[1]
    head = stored_cache_keys.shape[3]
    columns = key_value_weight.shape[1] // 2
    out_pieces = 2 * groups
    rank2 = adapter_down_weight.shape[2]

    swap = functools.partial(lax.ppermute, axis_name="tp", perm=[(0, 1), (1, 0)])

    half = n // 2
    per = pieces * cap
    me = lax.axis_index("pool").reshape(1)
    place, rank, *far = call(
        functools.partial(pack_far_kernel, n, cap, pieces),
        [jax.ShapeDtypeStruct((1, rows), I32)] * 2
        + [jax.ShapeDtypeStruct((per, width // pieces), BF16)] * half,
        n * cap * width * 64,
        2 * rows * width * 2,
        [SMEM, HBM, HBM, HBM],
        [
            pltpu.VMEM((1, rows), I32),
            pltpu.VMEM((1, n), I32),
            pltpu.VMEM((rows, width), BF16),
            pltpu.SemaphoreType.DMA((3,)),
        ],
    )(me, row_adapter_index.reshape(1, rows), adapter_slot_table.reshape(1, n), hidden)

    def far_exchange(chunks):
        return [
            lax.ppermute(chunk, "pool", [(i, i ^ s) for i in range(n)])
            for s, chunk in enumerate(chunks, half)
        ]

    near_exchange = functools.partial(
        lax.all_to_all,
        axis_name="pool",
        split_axis=0,
        concat_axis=0,
        tiled=True,
        axis_index_groups=[list(range(half)), list(range(half, n))],
    )
    far = far_exchange(far)
    (near,) = call(
        functools.partial(pack_near_kernel, cap, pieces),
        [jax.ShapeDtypeStruct((half * per, width // pieces), BF16)],
        n * cap * width * 64,
        2 * rows * width * 2,
        [VMEM] * 3,
    )(place, rank, hidden)
    near = near_exchange(near)

    core = lax.axis_index("tp")
    partial_sum = jnp.dot(hidden, key_value_weight, preferred_element_type=F32)
    base_mine = lax.dynamic_slice_in_dim(partial_sum, core * columns, columns, axis=1)
    base_other = swap(lax.dynamic_slice_in_dim(partial_sum, (1 - core) * columns, columns, axis=1))

    query_heads = queries.reshape(rows, groups, -1, head)
    scores = jnp.einsum("rgqd,rgpd->rgqp", query_heads, stored_cache_keys, preferred_element_type=F32)
    scores = scores * (head ** (-0.5))
    valid = jnp.arange(stored_cache_keys.shape[2])[None, :] < stored_cache_lengths[:, None]
    scores = jnp.where(valid[:, None, None, :], scores, -jnp.inf)
    cache_max = jnp.max(scores, axis=-1)
    weights = jnp.exp(scores - cache_max[..., None])
    cache_sum = jnp.sum(weights, axis=-1).reshape(rows, -1)
    attended = jnp.einsum(
        "rgqp,rgpd->rgqd", weights.astype(BF16), stored_cache_values, preferred_element_type=F32
    ).reshape(rows, -1)
    cache_max = cache_max.reshape(rows, -1)

    def correct(chunks, outs, *after):
        count = len(chunks)
        (reduced,) = call(
            functools.partial(shrink_kernel, cap, pieces, count),
            [jax.ShapeDtypeStruct((half * cap, rank2), F32)],
            n * cap * width * rank2,
            half * cap * width * 2 + width * rank2 * 2,
            [VMEM] * (count + 1) + [ANY] * len(after),
        )(*chunks, adapter_down_weight, *after)
        return call(
            functools.partial(expand_kernel, cap),
            [jax.ShapeDtypeStruct((half * out_pieces * cap // outs, head), BF16)] * outs,
            n * cap * rank2 * columns,
            half * cap * columns * 4,
            [VMEM] * 3,
        )(reduced, swap(reduced), adapter_up_weight)

    size = half * out_pieces * cap
    base, far_one_hot = call(
        functools.partial(precombine_kernel, cap),
        [
            jax.ShapeDtypeStruct((rows, columns), F32),
            jax.ShapeDtypeStruct((out_pieces * rows, size), BF16),
        ],
        4 * size * columns * rows,
        rows * columns * 12,
        [VMEM] * 5,
    )(near_exchange(correct([near], 1)[0]), place, rank, base_mine, base_other)
    token, out = call(
        combine_kernel,
        [jax.ShapeDtypeStruct((rows, columns), BF16), jax.ShapeDtypeStruct(queries.shape, BF16)],
        2 * size * columns * rows,
        rows * 2048 * 8,
        [VMEM] * (half + 6),
    )(
        *far_exchange(correct(far, half, base, attended)),
        far_one_hot,
        base,
        queries,
        cache_max,
        cache_sum,
        attended,
    )
    return token, out


def solution(mesh):
    in_specs = (
        P(("grp", "pool"), "tp"),
        P(("grp", "pool"), "tp"),
        P("tp", None),
        P("pool", "tp", None),
        P("pool", None, None, "tp"),
        P(("grp", "pool"), "tp", None, None),
        P(("grp", "pool"), "tp", None, None),
        P(("grp", "pool"), None),
        P(("grp", "pool")),
        P(),
    )
    out_specs = (P(("grp", "pool"), "tp"), P(("grp", "pool"), "tp"))
    return jax.shard_map(shards, mesh=mesh, in_specs=in_specs, out_specs=out_specs, check_vma=False)
```

```python
import functools

import jax
import jax.numpy as jnp
from jax import lax
from jax.experimental import pallas as pl
from jax.experimental.pallas import tpu as pltpu
from jax.sharding import PartitionSpec as P

BF16 = jnp.bfloat16
F32 = jnp.float32
I32 = jnp.int32
VMEM_LIMIT = 48 * 1024 * 1024


def iota(shape, dim):
    return lax.broadcasted_iota(I32, shape, dim)


def split_count(cap):
    pieces = 4
    while cap * pieces % 16:
        pieces *= 2
    return pieces


def dot(a, b):
    return jnp.dot(a, b, preferred_element_type=F32)


def dot_first(a, b):
    return lax.dot_general(a, b, (((0,), (0,)), ((), ())), preferred_element_type=F32)


def exact_select(one_hot, x):
    high = x.astype(BF16)
    rest = x - high.astype(F32)
    middle = rest.astype(BF16)
    low = (rest - middle.astype(F32)).astype(BF16)
    return dot(one_hot, high) + (dot(one_hot, middle) + dot(one_hot, low))


def codes_of(place, rank, cap, pieces):
    code = place * (pieces * cap) + rank
    return jnp.concatenate([code + piece * cap for piece in range(pieces)], axis=1)


def one_hot_of(codes, first, count):
    return ((iota((count, codes.shape[1]), 0) + first) == codes).astype(F32).astype(BF16)


def stack_pieces(hidden, pieces):
    width = hidden.shape[1] // pieces
    return jnp.concatenate(
        [hidden[:, piece * width : (piece + 1) * width] for piece in range(pieces)], axis=0
    )


def pack_far_kernel(n, cap, pieces, me_ref, idx_hbm, table_hbm, hidden_hbm, slot_ref, place_ref, rank_ref, *refs):
    far_refs, (idx_ref, table_ref, hidden_ref, sems) = refs[:-4], refs[-4:]
    copies = [
        pltpu.make_async_copy(source, target, sems.at[i])
        for i, (source, target) in enumerate(
            [(idx_hbm, idx_ref), (table_hbm, table_ref), (hidden_hbm, hidden_ref)]
        )
    ]
    for copy in copies:
        copy.start()
    rows = hidden_ref.shape[0]
    per = pieces * cap
    half = n // 2
    copies[0].wait()
    copies[1].wait()
    named = (iota((n, rows), 0) == idx_ref[...]).astype(F32).astype(BF16)
    table = jnp.broadcast_to(table_ref[...].astype(F32).astype(BF16), (16, n))
    slot = dot(table, named)[0:1, :].astype(I32)
    member = (iota((n, rows), 0) == slot).astype(F32)
    before = (iota((rows, rows), 0) < iota((rows, rows), 1)).astype(F32).astype(BF16)
    count = dot(member.astype(BF16), before)
    rank = jnp.sum(member * count, axis=0, keepdims=True).astype(I32)
    apart = lax.bitwise_xor(slot, me_ref[0])
    place = jnp.where(apart < half, lax.bitwise_and(slot, half - 1), apart)
    slot_ref[...] = slot
    place_ref[...] = place
    rank_ref[...] = rank
    one_hot = one_hot_of(codes_of(place, rank, cap, pieces), half * per, half * per)
    copies[2].wait()
    packed = dot(one_hot, stack_pieces(hidden_ref[...], pieces)).astype(BF16)
    for s in range(half):
        far_refs[s][...] = packed[s * per : (s + 1) * per]


def pack_near_kernel(cap, pieces, place_ref, rank_ref, hidden_ref, near_ref):
    one_hot = one_hot_of(codes_of(place_ref[...], rank_ref[...], cap, pieces), 0, near_ref.shape[0])
    near_ref[...] = dot(one_hot, stack_pieces(hidden_ref[...], pieces)).astype(BF16)


def shrink_kernel(cap, pieces, count, *refs):
    received_refs, down_ref, out_ref = refs[:count], refs[count], refs[-1]
    per = pieces * cap
    width = received_refs[0].shape[1]
    rank2 = down_ref.shape[2]
    received = jnp.concatenate([ref[...] for ref in received_refs], axis=0)
    size = received.shape[0]
    total = jnp.zeros((size, rank2), F32)
    piece_of = (iota((size, rank2), 0) // cap) % pieces
    for piece in range(pieces):
        part = dot(received, down_ref[0, piece * width : (piece + 1) * width, :])
        total = total + jnp.where(piece_of == piece, part, 0.0)
    out_row, in_row = iota((size // pieces, size), 0), iota((size // pieces, size), 1)
    same = (out_row // cap == in_row // per) & (out_row % cap == in_row % cap)
    out_ref[...] = exact_select(same.astype(F32).astype(BF16), total)


def expand_kernel(n, cap, me_ref, near_ref, near_other_ref, far_ref, far_other_ref, up_ref, out_ref):
    rank = up_ref.shape[2]
    head = 128
    blocks = up_ref.shape[3] // head
    reduced = jnp.concatenate(
        [near_ref[...] + near_other_ref[...], far_ref[...] + far_other_ref[...]], axis=0
    ).astype(BF16)
    terms = []
    for c in range(2):
        kept = reduced[:, c * rank : (c + 1) * rank]
        wide = dot(kept, up_ref[0, c]).astype(BF16)
        terms += [wide[:, g * head : (g + 1) * head] for g in range(blocks)]
    stacked = jnp.concatenate(terms, axis=0)
    pieces = 2 * blocks
    per = pieces * cap
    size = n * per
    half = n // 2
    out_row, in_row = iota((size, size), 0), iota((size, size), 1)
    apart = lax.bitwise_xor(out_row // per, me_ref[0])
    place = jnp.where(apart < half, lax.bitwise_and(out_row // per, half - 1), apart)
    source = (out_row // cap % pieces) * (n * cap) + place * cap + out_row % cap
    out_ref[...] = dot((source == in_row).astype(F32).astype(BF16), stacked).astype(BF16)


def prepare_kernel(cap, slot_ref, rank_ref, mine_ref, other_ref, base_ref, one_hot_ref):
    pieces = one_hot_ref.shape[0] // slot_ref.shape[1]
    size = one_hot_ref.shape[1]
    base_ref[...] = mine_ref[...] + other_ref[...]
    one_hot = one_hot_of(codes_of(slot_ref[...], rank_ref[...], cap, pieces), 0, size)
    same = (iota((size, size), 0) == iota((size, size), 1)).astype(F32).astype(BF16)
    one_hot_ref[...] = dot_first(one_hot, same).astype(BF16)


def combine_kernel(
    delta_ref, one_hot_ref, base_ref, query_ref, max_ref, sum_ref, acc_ref, token_ref, out_ref
):
    rows = base_ref.shape[0]
    head = 128
    groups = base_ref.shape[1] // (2 * head)
    delta = dot(one_hot_ref[...], delta_ref[...])
    heads = query_ref.shape[1] // head
    per_group = heads // groups
    scale = head ** (-0.5)
    lane = iota((rows, head), 1)
    own = jnp.zeros((rows, head), F32)
    values = []
    for g in range(groups):
        made = []
        for c in range(2):
            at = (g * 2 + c) * head
            piece = c * groups + g
            made.append((base_ref[:, at : at + head] + delta[piece * rows : (piece + 1) * rows]).astype(BF16))
            token_ref[:, at : at + head] = made[-1]
        key = made[0].astype(F32)
        values.append(made[1].astype(F32))
        for h in range(g * per_group, (g + 1) * per_group):
            query = query_ref[:, h * head : (h + 1) * head].astype(F32)
            own = jnp.where(lane == h, jnp.sum(query * key, axis=1, keepdims=True), own)
    own = own[:, :heads] * scale
    cache_max = max_ref[...]
    highest = jnp.maximum(own, cache_max)
    cache_factor = jnp.exp(cache_max - highest)
    own_factor = jnp.exp(own - highest)
    inverse = 1.0 / (sum_ref[...] * cache_factor + own_factor)
    cache_factor = cache_factor * inverse
    own_factor = own_factor * inverse
    for h in range(heads):
        lanes = slice(h * head, (h + 1) * head)
        out = acc_ref[:, lanes] * cache_factor[:, h : h + 1]
        out = out + values[h // per_group] * own_factor[:, h : h + 1]
        out_ref[:, lanes] = out.astype(BF16)


VMEM = pl.BlockSpec(memory_space=pltpu.VMEM)
SMEM = pl.BlockSpec(memory_space=pltpu.SMEM)
HBM = pl.BlockSpec(memory_space=pltpu.HBM)
ANY = pl.BlockSpec(memory_space=pl.ANY)


def call(kernel, outs, flops, bytes_accessed, specs, scratch=()):
    return pl.pallas_call(
        kernel,
        out_shape=outs,
        in_specs=specs,
        out_specs=[VMEM] * len(outs),
        scratch_shapes=scratch,
        compiler_params=pltpu.CompilerParams(vmem_limit_bytes=VMEM_LIMIT),
        cost_estimate=pl.CostEstimate(flops=flops, bytes_accessed=bytes_accessed, transcendentals=0),
    )


def shards(
    hidden,
    queries,
    key_value_weight,
    adapter_down_weight,
    adapter_up_weight,
    stored_cache_keys,
    stored_cache_values,
    row_adapter_index,
    stored_cache_lengths,
    adapter_slot_table,
):
    n = lax.axis_size("pool")
    rows, width = hidden.shape
    cap = -(-2 * rows // n)
    pieces = split_count(cap)
    groups = stored_cache_keys.shape[1]
    head = stored_cache_keys.shape[3]
    columns = key_value_weight.shape[1] // 2
    out_pieces = 2 * groups
    rank2 = adapter_down_weight.shape[2]

    swap = functools.partial(lax.ppermute, axis_name="tp", perm=[(0, 1), (1, 0)])

    half = n // 2
    per = pieces * cap
    me = lax.axis_index("pool").reshape(1)
    slot, place, rank, *far = call(
        functools.partial(pack_far_kernel, n, cap, pieces),
        [jax.ShapeDtypeStruct((1, rows), I32)] * 3
        + [jax.ShapeDtypeStruct((per, width // pieces), BF16)] * half,
        n * cap * width * 64,
        2 * rows * width * 2,
        [SMEM, HBM, HBM, HBM],
        [
            pltpu.VMEM((1, rows), I32),
            pltpu.VMEM((1, n), I32),
            pltpu.VMEM((rows, width), BF16),
            pltpu.SemaphoreType.DMA((3,)),
        ],
    )(me, row_adapter_index.reshape(1, rows), adapter_slot_table.reshape(1, n), hidden)

    far = [
        lax.ppermute(chunk, "pool", [(i, i ^ s) for i in range(n)]) for s, chunk in enumerate(far, half)
    ]
    (near,) = call(
        functools.partial(pack_near_kernel, cap, pieces),
        [jax.ShapeDtypeStruct((half * per, width // pieces), BF16)],
        n * cap * width * 64,
        2 * rows * width * 2,
        [VMEM] * 3,
    )(place, rank, hidden)
    near = lax.all_to_all(
        near,
        "pool",
        split_axis=0,
        concat_axis=0,
        tiled=True,
        axis_index_groups=[list(range(half)), list(range(half, n))],
    )

    core = lax.axis_index("tp")
    partial_sum = jnp.dot(hidden, key_value_weight, preferred_element_type=F32)
    base_mine = lax.dynamic_slice_in_dim(partial_sum, core * columns, columns, axis=1)
    base_other = swap(lax.dynamic_slice_in_dim(partial_sum, (1 - core) * columns, columns, axis=1))

    query_heads = queries.reshape(rows, groups, -1, head)
    scores = jnp.einsum("rgqd,rgpd->rgqp", query_heads, stored_cache_keys, preferred_element_type=F32)
    scores = scores * (head ** (-0.5))
    valid = jnp.arange(stored_cache_keys.shape[2])[None, :] < stored_cache_lengths[:, None]
    scores = jnp.where(valid[:, None, None, :], scores, -jnp.inf)
    cache_max = jnp.max(scores, axis=-1)
    weights = jnp.exp(scores - cache_max[..., None])
    cache_sum = jnp.sum(weights, axis=-1).reshape(rows, -1)
    attended = jnp.einsum(
        "rgqp,rgpd->rgqd", weights.astype(BF16), stored_cache_values, preferred_element_type=F32
    ).reshape(rows, -1)
    cache_max = cache_max.reshape(rows, -1)

    def shrink(chunks, *after):
        return call(
            functools.partial(shrink_kernel, cap, pieces, len(chunks)),
            [jax.ShapeDtypeStruct((half * cap, rank2), F32)],
            n * cap * width * rank2,
            half * cap * width * 2 + width * rank2 * 2,
            [VMEM] * (len(chunks) + 1) + [ANY] * len(after),
        )(*chunks, adapter_down_weight, *after)[0]

    size = n * out_pieces * cap
    base, one_hot = call(
        functools.partial(prepare_kernel, cap),
        [
            jax.ShapeDtypeStruct((rows, columns), F32),
            jax.ShapeDtypeStruct((out_pieces * rows, size), BF16),
        ],
        2 * size * size * rows,
        rows * columns * 12,
        [VMEM] * 4,
    )(slot, rank, base_mine, base_other)
    near_sum = shrink([near])
    near_other = swap(near_sum)
    far_sum = shrink(far, base, near_sum)
    (terms,) = call(
        functools.partial(expand_kernel, n, cap),
        [jax.ShapeDtypeStruct((size, head), BF16)],
        2 * n * cap * rank2 * columns,
        n * cap * columns * 4,
        [SMEM] + [VMEM] * 5,
    )(me, near_sum, near_other, far_sum, swap(far_sum), adapter_up_weight)
    deltas = lax.all_to_all(terms, "pool", split_axis=0, concat_axis=0, tiled=True)
    token, out = call(
        combine_kernel,
        [jax.ShapeDtypeStruct((rows, columns), BF16), jax.ShapeDtypeStruct(queries.shape, BF16)],
        2 * size * columns * rows,
        rows * 2048 * 8,
        [VMEM] * 7,
    )(deltas, one_hot, base, queries, cache_max, cache_sum, attended)
    return token, out


def solution(mesh):
    in_specs = (
        P(("grp", "pool"), "tp"),
        P(("grp", "pool"), "tp"),
        P("tp", None),
        P("pool", "tp", None),
        P("pool", None, None, "tp"),
        P(("grp", "pool"), "tp", None, None),
        P(("grp", "pool"), "tp", None, None),
        P(("grp", "pool"), None),
        P(("grp", "pool")),
        P(),
    )
    out_specs = (P(("grp", "pool"), "tp"), P(("grp", "pool"), "tp"))
    return jax.shard_map(shards, mesh=mesh, in_specs=in_specs, out_specs=out_specs, check_vma=False)
```

```python
import functools

import jax
import jax.numpy as jnp
from jax import lax
from jax.experimental import pallas as pl
from jax.experimental.pallas import tpu as pltpu
from jax.sharding import PartitionSpec as P

BF16 = jnp.bfloat16
F32 = jnp.float32
I32 = jnp.int32
VMEM_LIMIT = 48 * 1024 * 1024


def iota(shape, dim):
    return lax.broadcasted_iota(I32, shape, dim)


def split_count(cap):
    pieces = 4
    while cap * pieces % 16:
        pieces *= 2
    return pieces


def dot(a, b):
    return jnp.dot(a, b, preferred_element_type=F32)


def dot_first(a, b):
    return lax.dot_general(a, b, (((0,), (0,)), ((), ())), preferred_element_type=F32)


def exact_select(one_hot, x):
    high = x.astype(BF16)
    rest = x - high.astype(F32)
    middle = rest.astype(BF16)
    low = (rest - middle.astype(F32)).astype(BF16)
    return dot(one_hot, high) + (dot(one_hot, middle) + dot(one_hot, low))


def codes_of(place, rank, cap, pieces):
    code = place * (pieces * cap) + rank
    return jnp.concatenate([code + piece * cap for piece in range(pieces)], axis=1)


def one_hot_of(codes, first, count):
    return ((iota((count, codes.shape[1]), 0) + first) == codes).astype(F32).astype(BF16)


def stack_pieces(hidden, pieces):
    width = hidden.shape[1] // pieces
    return jnp.concatenate(
        [hidden[:, piece * width : (piece + 1) * width] for piece in range(pieces)], axis=0
    )


def pack_far_kernel(
    n, cap, pieces, me_ref, idx_ref, table_ref, hidden_ref, slot_ref, place_ref, rank_ref, *far_refs
):
    rows = hidden_ref.shape[0]
    per = pieces * cap
    half = n // 2
    lane = iota((1, rows), 1)
    slot = jnp.zeros((1, rows), I32)
    for r in range(rows):
        slot = jnp.where(lane == r, table_ref[idx_ref[r]], slot)
    member = (iota((n, rows), 0) == slot).astype(F32)
    before = (iota((rows, rows), 0) < iota((rows, rows), 1)).astype(F32).astype(BF16)
    count = dot(member.astype(BF16), before)
    rank = jnp.sum(member * count, axis=0, keepdims=True).astype(I32)
    apart = lax.bitwise_xor(slot, me_ref[0])
    place = jnp.where(apart < half, lax.bitwise_and(slot, half - 1), apart)
    slot_ref[...] = slot
    place_ref[...] = place
    rank_ref[...] = rank
    one_hot = one_hot_of(codes_of(place, rank, cap, pieces), half * per, half * per)
    packed = dot(one_hot, stack_pieces(hidden_ref[...], pieces)).astype(BF16)
    for s in range(half):
        far_refs[s][...] = packed[s * per : (s + 1) * per]


def pack_near_kernel(cap, pieces, place_ref, rank_ref, hidden_ref, _, near_ref):
    one_hot = one_hot_of(codes_of(place_ref[...], rank_ref[...], cap, pieces), 0, near_ref.shape[0])
    near_ref[...] = dot(one_hot, stack_pieces(hidden_ref[...], pieces)).astype(BF16)


def shrink_kernel(cap, pieces, count, *refs):
    received_refs, down_ref, out_ref = refs[:count], refs[count], refs[-1]
    per = pieces * cap
    width = received_refs[0].shape[1]
    rank2 = down_ref.shape[2]
    received = jnp.concatenate([ref[...] for ref in received_refs], axis=0)
    size = received.shape[0]
    total = jnp.zeros((size, rank2), F32)
    piece_of = (iota((size, rank2), 0) // cap) % pieces
    for piece in range(pieces):
        part = dot(received, down_ref[0, piece * width : (piece + 1) * width, :])
        total = total + jnp.where(piece_of == piece, part, 0.0)
    out_row, in_row = iota((size // pieces, size), 0), iota((size // pieces, size), 1)
    same = (out_row // cap == in_row // per) & (out_row % cap == in_row % cap)
    out_ref[...] = exact_select(same.astype(F32).astype(BF16), total)


def expand_kernel(n, cap, me_ref, near_ref, near_other_ref, far_ref, far_other_ref, up_ref, out_ref):
    rank = up_ref.shape[2]
    head = 128
    blocks = up_ref.shape[3] // head
    reduced = jnp.concatenate(
        [near_ref[...] + near_other_ref[...], far_ref[...] + far_other_ref[...]], axis=0
    ).astype(BF16)
    terms = []
    for c in range(2):
        kept = reduced[:, c * rank : (c + 1) * rank]
        wide = dot(kept, up_ref[0, c]).astype(BF16)
        terms += [wide[:, g * head : (g + 1) * head] for g in range(blocks)]
    stacked = jnp.concatenate(terms, axis=0)
    pieces = 2 * blocks
    per = pieces * cap
    size = n * per
    half = n // 2
    out_row, in_row = iota((size, size), 0), iota((size, size), 1)
    apart = lax.bitwise_xor(out_row // per, me_ref[0])
    place = jnp.where(apart < half, lax.bitwise_and(out_row // per, half - 1), apart)
    source = (out_row // cap % pieces) * (n * cap) + place * cap + out_row % cap
    out_ref[...] = dot((source == in_row).astype(F32).astype(BF16), stacked).astype(BF16)


def prepare_kernel(cap, slot_ref, rank_ref, mine_ref, other_ref, base_ref, one_hot_ref):
    pieces = one_hot_ref.shape[0] // slot_ref.shape[1]
    size = one_hot_ref.shape[1]
    base_ref[...] = mine_ref[...] + other_ref[...]
    one_hot = one_hot_of(codes_of(slot_ref[...], rank_ref[...], cap, pieces), 0, size)
    same = (iota((size, size), 0) == iota((size, size), 1)).astype(F32).astype(BF16)
    one_hot_ref[...] = dot_first(one_hot, same).astype(BF16)


def combine_kernel(
    delta_ref, one_hot_ref, base_ref, query_ref, max_ref, sum_ref, acc_ref, token_ref, out_ref
):
    rows = base_ref.shape[0]
    head = 128
    groups = base_ref.shape[1] // (2 * head)
    delta = dot(one_hot_ref[...], delta_ref[...])
    heads = query_ref.shape[1] // head
    per_group = heads // groups
    scale = head ** (-0.5)
    lane = iota((rows, head), 1)
    own = jnp.zeros((rows, head), F32)
    values = []
    for g in range(groups):
        made = []
        for c in range(2):
            at = (g * 2 + c) * head
            piece = c * groups + g
            made.append((base_ref[:, at : at + head] + delta[piece * rows : (piece + 1) * rows]).astype(BF16))
            token_ref[:, at : at + head] = made[-1]
        key = made[0].astype(F32)
        values.append(made[1].astype(F32))
        for h in range(g * per_group, (g + 1) * per_group):
            query = query_ref[:, h * head : (h + 1) * head].astype(F32)
            own = jnp.where(lane == h, jnp.sum(query * key, axis=1, keepdims=True), own)
    own = own[:, :heads] * scale
    cache_max = max_ref[...]
    highest = jnp.maximum(own, cache_max)
    cache_factor = jnp.exp(cache_max - highest)
    own_factor = jnp.exp(own - highest)
    inverse = 1.0 / (sum_ref[...] * cache_factor + own_factor)
    cache_factor = cache_factor * inverse
    own_factor = own_factor * inverse
    for h in range(heads):
        lanes = slice(h * head, (h + 1) * head)
        out = acc_ref[:, lanes] * cache_factor[:, h : h + 1]
        out = out + values[h // per_group] * own_factor[:, h : h + 1]
        out_ref[:, lanes] = out.astype(BF16)


VMEM = pl.BlockSpec(memory_space=pltpu.VMEM)
SMEM = pl.BlockSpec(memory_space=pltpu.SMEM)
ANY = pl.BlockSpec(memory_space=pl.ANY)


def call(kernel, outs, flops, bytes_accessed, specs, scratch=()):
    return pl.pallas_call(
        kernel,
        out_shape=outs,
        in_specs=specs,
        out_specs=[VMEM] * len(outs),
        scratch_shapes=scratch,
        compiler_params=pltpu.CompilerParams(vmem_limit_bytes=VMEM_LIMIT),
        cost_estimate=pl.CostEstimate(flops=flops, bytes_accessed=bytes_accessed, transcendentals=0),
    )


def shards(
    hidden,
    queries,
    key_value_weight,
    adapter_down_weight,
    adapter_up_weight,
    stored_cache_keys,
    stored_cache_values,
    row_adapter_index,
    stored_cache_lengths,
    adapter_slot_table,
):
    n = lax.axis_size("pool")
    rows, width = hidden.shape
    cap = -(-2 * rows // n)
    pieces = split_count(cap)
    groups = stored_cache_keys.shape[1]
    head = stored_cache_keys.shape[3]
    columns = key_value_weight.shape[1] // 2
    out_pieces = 2 * groups
    rank2 = adapter_down_weight.shape[2]

    swap = functools.partial(lax.ppermute, axis_name="tp", perm=[(0, 1), (1, 0)])

    half = n // 2
    per = pieces * cap
    me = lax.axis_index("pool").reshape(1)
    slot, place, rank, *far = call(
        functools.partial(pack_far_kernel, n, cap, pieces),
        [jax.ShapeDtypeStruct((1, rows), I32)] * 3
        + [jax.ShapeDtypeStruct((per, width // pieces), BF16)] * half,
        n * cap * width * 64,
        2 * rows * width * 2,
        [SMEM, SMEM, SMEM, VMEM],
    )(me, row_adapter_index.reshape(rows), adapter_slot_table, hidden)
    far = [
        lax.ppermute(chunk, "pool", [(i, i ^ s) for i in range(n)]) for s, chunk in enumerate(far, half)
    ]
    core = lax.axis_index("tp")
    partial_sum = jnp.dot(hidden, key_value_weight, preferred_element_type=F32)
    base_mine = lax.dynamic_slice_in_dim(partial_sum, core * columns, columns, axis=1)
    base_other = swap(lax.dynamic_slice_in_dim(partial_sum, (1 - core) * columns, columns, axis=1))

    query_heads = queries.reshape(rows, groups, -1, head)
    scores = jnp.einsum("rgqd,rgpd->rgqp", query_heads, stored_cache_keys, preferred_element_type=F32)
    scores = scores * (head ** (-0.5))
    valid = jnp.arange(stored_cache_keys.shape[2])[None, :] < stored_cache_lengths[:, None]
    scores = jnp.where(valid[:, None, None, :], scores, -jnp.inf)
    cache_max = jnp.max(scores, axis=-1)
    (near,) = call(
        functools.partial(pack_near_kernel, cap, pieces),
        [jax.ShapeDtypeStruct((half * per, width // pieces), BF16)],
        n * cap * width * 64,
        2 * rows * width * 2,
        [VMEM] * 3 + [ANY],
    )(place, rank, hidden, cache_max)
    near = lax.all_to_all(
        near,
        "pool",
        split_axis=0,
        concat_axis=0,
        tiled=True,
        axis_index_groups=[list(range(half)), list(range(half, n))],
    )

    weights = jnp.exp(scores - cache_max[..., None])
    cache_sum = jnp.sum(weights, axis=-1).reshape(rows, -1)
    attended = jnp.einsum(
        "rgqp,rgpd->rgqd", weights.astype(BF16), stored_cache_values, preferred_element_type=F32
    ).reshape(rows, -1)
    cache_max = cache_max.reshape(rows, -1)

    def shrink(chunks, *after):
        return call(
            functools.partial(shrink_kernel, cap, pieces, len(chunks)),
            [jax.ShapeDtypeStruct((half * cap, rank2), F32)],
            n * cap * width * rank2,
            half * cap * width * 2 + width * rank2 * 2,
            [VMEM] * (len(chunks) + 1) + [ANY] * len(after),
        )(*chunks, adapter_down_weight, *after)[0]

    size = n * out_pieces * cap
    base, one_hot = call(
        functools.partial(prepare_kernel, cap),
        [
            jax.ShapeDtypeStruct((rows, columns), F32),
            jax.ShapeDtypeStruct((out_pieces * rows, size), BF16),
        ],
        2 * size * size * rows,
        rows * columns * 12,
        [VMEM] * 4,
    )(slot, rank, base_mine, base_other)
    near_sum = shrink([near])
    near_other = swap(near_sum)
    far_sum = shrink(far, base, near_sum)
    (terms,) = call(
        functools.partial(expand_kernel, n, cap),
        [jax.ShapeDtypeStruct((size, head), BF16)],
        2 * n * cap * rank2 * columns,
        n * cap * columns * 4,
        [SMEM] + [VMEM] * 5,
    )(me, near_sum, near_other, far_sum, swap(far_sum), adapter_up_weight)
    deltas = lax.all_to_all(terms, "pool", split_axis=0, concat_axis=0, tiled=True)
    token, out = call(
        combine_kernel,
        [jax.ShapeDtypeStruct((rows, columns), BF16), jax.ShapeDtypeStruct(queries.shape, BF16)],
        2 * size * columns * rows,
        rows * 2048 * 8,
        [VMEM] * 7,
    )(deltas, one_hot, base, queries, cache_max, cache_sum, attended)
    return token, out


def solution(mesh):
    in_specs = (
        P(("grp", "pool"), "tp"),
        P(("grp", "pool"), "tp"),
        P("tp", None),
        P("pool", "tp", None),
        P("pool", None, None, "tp"),
        P(("grp", "pool"), "tp", None, None),
        P(("grp", "pool"), "tp", None, None),
        P(("grp", "pool"), None),
        P(("grp", "pool")),
        P(),
    )
    out_specs = (P(("grp", "pool"), "tp"), P(("grp", "pool"), "tp"))
    return jax.shard_map(shards, mesh=mesh, in_specs=in_specs, out_specs=out_specs, check_vma=False)
```

```python
import functools

import jax
import jax.numpy as jnp
from jax import lax
from jax.experimental import pallas as pl
from jax.experimental.pallas import tpu as pltpu
from jax.sharding import PartitionSpec as P

BF16 = jnp.bfloat16
F32 = jnp.float32
I32 = jnp.int32
VMEM_LIMIT = 48 * 1024 * 1024


def iota(shape, dim):
    return lax.broadcasted_iota(I32, shape, dim)


def split_count(cap):
    pieces = 4
    while cap * pieces % 16:
        pieces *= 2
    return pieces


def dot(a, b):
    return jnp.dot(a, b, preferred_element_type=F32)


def dot_first(a, b):
    return lax.dot_general(a, b, (((0,), (0,)), ((), ())), preferred_element_type=F32)


def exact_select(one_hot, x):
    high = x.astype(BF16)
    rest = x - high.astype(F32)
    middle = rest.astype(BF16)
    low = (rest - middle.astype(F32)).astype(BF16)
    return dot(one_hot, high) + (dot(one_hot, middle) + dot(one_hot, low))


def codes_of(place, rank, cap, pieces):
    code = place * (pieces * cap) + rank
    return jnp.concatenate([code + piece * cap for piece in range(pieces)], axis=1)


def one_hot_of(codes, first, count):
    return ((iota((count, codes.shape[1]), 0) + first) == codes).astype(F32).astype(BF16)


def stack_pieces(hidden, pieces):
    width = hidden.shape[1] // pieces
    return jnp.concatenate(
        [hidden[:, piece * width : (piece + 1) * width] for piece in range(pieces)], axis=0
    )


def pack_kernel(n, cap, pieces, me_ref, idx_ref, table_ref, hidden_ref, slot_ref, rank_ref, *out_refs):
    rows = hidden_ref.shape[0]
    named = (iota((n, rows), 0) == idx_ref[...]).astype(F32).astype(BF16)
    table = jnp.broadcast_to(table_ref[...].astype(F32).astype(BF16), (16, n))
    slot = dot(table, named)[0:1, :].astype(I32)
    member = (iota((n, rows), 0) == slot).astype(F32)
    before = (iota((rows, rows), 0) < iota((rows, rows), 1)).astype(F32).astype(BF16)
    count = dot(member.astype(BF16), before)
    rank = jnp.sum(member * count, axis=0, keepdims=True).astype(I32)
    slot_ref[...] = slot
    rank_ref[...] = rank
    per = pieces * cap
    apart = lax.bitwise_xor(slot, me_ref[0])
    one_hot = one_hot_of(codes_of(apart, rank, cap, pieces), 0, n * per)
    packed = dot(one_hot, stack_pieces(hidden_ref[...], pieces)).astype(BF16)
    for s, out_ref in enumerate(out_refs):
        out_ref[...] = packed[s * per : (s + 1) * per]


def shrink_kernel(n, cap, pieces, order, *refs):
    received_refs, (down_ref, base_ref, out_ref) = dict(zip(order, refs[:n])), refs[n:]
    per = pieces * cap
    width = refs[0].shape[1]
    rank2 = down_ref.shape[2]
    received = jnp.concatenate([received_refs[s][...] for s in range(n)], axis=0)
    size = received.shape[0]
    total = jnp.zeros((size, rank2), F32)
    piece_of = (iota((size, rank2), 0) // cap) % pieces
    for piece in range(pieces):
        part = dot(received, down_ref[0, piece * width : (piece + 1) * width, :])
        total = total + jnp.where(piece_of == piece, part, 0.0)
    out_row, in_row = iota((size // pieces, size), 0), iota((size // pieces, size), 1)
    same = (out_row // cap == in_row // per) & (out_row % cap == in_row % cap)
    reduced = exact_select(same.astype(F32).astype(BF16), total)
    size = reduced.shape[0]
    out_ref[:size, :] = reduced
    rows = base_ref.shape[0]
    for i in range(base_ref.shape[1] // rank2):
        first = size + i * rows
        out_ref[first : first + rows, :] = base_ref[:, i * rank2 : (i + 1) * rank2]


def expand_kernel(n, cap, me_ref, mine_ref, other_ref, up_ref, out_ref):
    rank = up_ref.shape[2]
    head = 128
    blocks = up_ref.shape[3] // head
    reduced = (mine_ref[: n * cap, :] + other_ref[: n * cap, :]).astype(BF16)
    terms = []
    for c in range(2):
        kept = reduced[:, c * rank : (c + 1) * rank]
        wide = dot(kept, up_ref[0, c]).astype(BF16)
        terms += [wide[:, g * head : (g + 1) * head] for g in range(blocks)]
    stacked = jnp.concatenate(terms, axis=0)
    pieces = 2 * blocks
    per = pieces * cap
    size = n * per
    out_row, in_row = iota((size, size), 0), iota((size, size), 1)
    apart = lax.bitwise_xor(out_row // per, me_ref[0])
    source = (out_row // cap % pieces) * (n * cap) + apart * cap + out_row % cap
    out_ref[...] = dot((source == in_row).astype(F32).astype(BF16), stacked).astype(BF16)


def prepare_kernel(n, cap, slot_ref, rank_ref, mine_ref, other_ref, _, base_ref, one_hot_ref):
    pieces = one_hot_ref.shape[0] // slot_ref.shape[1]
    size = one_hot_ref.shape[1]
    rows = mine_ref.shape[0]
    width = other_ref.shape[1]
    for i in range(mine_ref.shape[1] // width):
        lanes, first = slice(i * width, (i + 1) * width), n * cap + i * rows
        base_ref[:, lanes] = mine_ref[:, lanes] + other_ref[first : first + rows, :]
    one_hot = one_hot_of(codes_of(slot_ref[...], rank_ref[...], cap, pieces), 0, size)
    same = (iota((size, size), 0) == iota((size, size), 1)).astype(F32).astype(BF16)
    one_hot_ref[...] = dot_first(one_hot, same).astype(BF16)


def base_kernel(core_ref, hidden_ref, weight_ref, first_ref, second_ref, mine_ref, other_ref, total_ref):
    step = pl.program_id(0)
    part = dot(hidden_ref[...], weight_ref[...])

    @pl.when(step == 0)
    def _():
        total_ref[...] = part

    @pl.when(step > 0)
    def _():
        total_ref[...] += part

    @pl.when(step == pl.num_programs(0) - 1)
    def _():
        columns = mine_ref.shape[1]
        first, second = total_ref[:, :columns], total_ref[:, columns:]
        mine_ref[...] = jnp.where(core_ref[0] == 0, first, second)
        other_ref[...] = jnp.where(core_ref[0] == 0, second, first)


def cache_kernel(query_ref, key_ref, value_ref, length_ref, _, acc_ref, max_ref, sum_ref):
    rows, groups, positions, head = key_ref.shape
    per_group = query_ref.shape[1] // (groups * head)
    tile = 16
    wide, deep = tile * positions, tile * per_group
    scale = head ** (-0.5)
    row_of = iota((deep, wide), 0) % tile
    own_row = row_of == iota((deep, wide), 1) // positions
    position = iota((deep, wide), 1) % positions
    lane = iota((tile, head), 1)
    for first in range(0, rows, tile):
        at = slice(first, first + tile)
        length = jnp.concatenate([length_ref[at, :]] * per_group, axis=0)
        valid = own_row & (position < length)
        tops = jnp.zeros((tile, head), F32)
        sums = jnp.zeros((tile, head), F32)
        for g in range(groups):
            query = jnp.concatenate(
                [query_ref[at, h * head : (h + 1) * head] for h in range(g * per_group, (g + 1) * per_group)],
                axis=0,
            )
            key = key_ref[at, g].reshape(wide, head)
            value = value_ref[at, g].reshape(wide, head)
            scores = lax.dot_general(query, key, (((1,), (1,)), ((), ())), preferred_element_type=F32)
            scores = jnp.where(valid, scores * scale, -jnp.inf)
            top = jnp.max(scores, axis=1, keepdims=True)
            weight = jnp.exp(scores - top)
            total = jnp.sum(weight, axis=1, keepdims=True)
            mixed = dot(weight.astype(BF16), value)
            for i in range(per_group):
                h = g * per_group + i
                part = slice(i * tile, (i + 1) * tile)
                acc_ref[at, h * head : (h + 1) * head] = mixed[part]
                tops = jnp.where(lane == h, top[part], tops)
                sums = jnp.where(lane == h, total[part], sums)
        max_ref[at, :] = tops
        sum_ref[at, :] = sums


def combine_kernel(
    delta_ref, one_hot_ref, base_ref, query_ref, max_ref, sum_ref, acc_ref, token_ref, out_ref
):
    rows = base_ref.shape[0]
    head = 128
    groups = base_ref.shape[1] // (2 * head)
    delta = dot(one_hot_ref[...], delta_ref[...])
    heads = query_ref.shape[1] // head
    per_group = heads // groups
    scale = head ** (-0.5)
    lane = iota((rows, head), 1)
    own = jnp.zeros((rows, head), F32)
    values = []
    for g in range(groups):
        made = []
        for c in range(2):
            at = (g * 2 + c) * head
            piece = c * groups + g
            made.append((base_ref[:, at : at + head] + delta[piece * rows : (piece + 1) * rows]).astype(BF16))
            token_ref[:, at : at + head] = made[-1]
        key = made[0].astype(F32)
        values.append(made[1].astype(F32))
        for h in range(g * per_group, (g + 1) * per_group):
            query = query_ref[:, h * head : (h + 1) * head].astype(F32)
            own = jnp.where(lane == h, jnp.sum(query * key, axis=1, keepdims=True), own)
    own = own[:, :heads] * scale
    cache_max = max_ref[:, :heads]
    highest = jnp.maximum(own, cache_max)
    cache_factor = jnp.exp(cache_max - highest)
    own_factor = jnp.exp(own - highest)
    inverse = 1.0 / (sum_ref[:, :heads] * cache_factor + own_factor)
    cache_factor = cache_factor * inverse
    own_factor = own_factor * inverse
    for h in range(heads):
        lanes = slice(h * head, (h + 1) * head)
        out = acc_ref[:, lanes] * cache_factor[:, h : h + 1]
        out = out + values[h // per_group] * own_factor[:, h : h + 1]
        out_ref[:, lanes] = out.astype(BF16)


VMEM = pl.BlockSpec(memory_space=pltpu.VMEM)
SMEM = pl.BlockSpec(memory_space=pltpu.SMEM)
HBM = pl.BlockSpec(memory_space=pltpu.HBM)
ANY = pl.BlockSpec(memory_space=pl.ANY)
NO_COST = pl.CostEstimate(flops=0, bytes_accessed=0, transcendentals=0)


def call(kernel, outs, specs):
    return pl.pallas_call(
        kernel,
        out_shape=outs,
        in_specs=specs,
        out_specs=[VMEM] * len(outs),
        compiler_params=pltpu.CompilerParams(vmem_limit_bytes=VMEM_LIMIT),
        cost_estimate=NO_COST,
    )


def shards(
    hidden,
    queries,
    key_value_weight,
    adapter_down_weight,
    adapter_up_weight,
    stored_cache_keys,
    stored_cache_values,
    row_adapter_index,
    stored_cache_lengths,
    adapter_slot_table,
):
    n = lax.axis_size("pool")
    rows, width = hidden.shape
    cap = -(-2 * rows // n)
    pieces = split_count(cap)
    groups = stored_cache_keys.shape[1]
    head = stored_cache_keys.shape[3]
    columns = key_value_weight.shape[1] // 2
    out_pieces = 2 * groups
    rank2 = adapter_down_weight.shape[2]

    swap = functools.partial(lax.ppermute, axis_name="tp", perm=[(0, 1), (1, 0)])

    me = lax.axis_index("pool").reshape(1)
    slot, rank, *packed = call(
        functools.partial(pack_kernel, n, cap, pieces),
        [jax.ShapeDtypeStruct((1, rows), I32)] * 2
        + [jax.ShapeDtypeStruct((pieces * cap, width // pieces), BF16)] * n,
        [SMEM, VMEM, VMEM, VMEM],
    )(me, row_adapter_index.reshape(1, rows), adapter_slot_table.reshape(1, n), hidden)
    order = [0, 1, 2, *range(n // 2, n), *range(3, n // 2)]
    arrived = {0: packed[0]}
    for s in order[1:]:
        arrived[s] = lax.ppermute(packed[s], "pool", [(i, i ^ s) for i in range(n)])

    depth = 512
    base_mine, base_other = pl.pallas_call(
        base_kernel,
        grid=(width // depth,),
        in_specs=[
            SMEM,
            pl.BlockSpec((rows, depth), lambda k: (0, k)),
            pl.BlockSpec((depth, 2 * columns), lambda k: (k, 0)),
            ANY,
            ANY,
        ],
        out_specs=[pl.BlockSpec((rows, columns), lambda k: (0, 0))] * 2,
        out_shape=[jax.ShapeDtypeStruct((rows, columns), F32)] * 2,
        scratch_shapes=[pltpu.VMEM((rows, 2 * columns), F32)],
        compiler_params=pltpu.CompilerParams(vmem_limit_bytes=VMEM_LIMIT),
        cost_estimate=pl.CostEstimate(
            flops=4 * rows * width * columns, bytes_accessed=16 * width * columns, transcendentals=0
        ),
    )(lax.axis_index("tp").reshape(1), hidden, key_value_weight, arrived[1], arrived[2])

    size = n * out_pieces * cap
    (sums,) = call(
        functools.partial(shrink_kernel, n, cap, pieces, order),
        [jax.ShapeDtypeStruct((n * cap + rows * columns // rank2, rank2), F32)],
        [VMEM] * (n + 2),
    )(*[arrived[s] for s in order], adapter_down_weight, base_other)
    other_sums = swap(sums)
    (terms,) = call(
        functools.partial(expand_kernel, n, cap),
        [jax.ShapeDtypeStruct((size, head), BF16)],
        [SMEM] + [VMEM] * 3,
    )(me, sums, other_sums, adapter_up_weight)
    base, one_hot = call(
        functools.partial(prepare_kernel, n, cap),
        [
            jax.ShapeDtypeStruct((rows, columns), F32),
            jax.ShapeDtypeStruct((out_pieces * rows, size), BF16),
        ],
        [VMEM] * 4 + [ANY],
    )(slot, rank, base_mine, other_sums, terms)
    deltas = lax.all_to_all(terms, "pool", split_axis=0, concat_axis=0, tiled=True)
    attended, cache_max, cache_sum = call(
        cache_kernel,
        [jax.ShapeDtypeStruct(queries.shape, F32)] + [jax.ShapeDtypeStruct((rows, head), F32)] * 2,
        [VMEM] * 4 + [ANY],
    )(queries, stored_cache_keys, stored_cache_values, stored_cache_lengths.reshape(rows, 1), terms)
    token, out = call(
        combine_kernel,
        [jax.ShapeDtypeStruct((rows, columns), BF16), jax.ShapeDtypeStruct(queries.shape, BF16)],
        [VMEM] * 7,
    )(deltas, one_hot, base, queries, cache_max, cache_sum, attended)
    return token, out


def solution(mesh):
    in_specs = (
        P(("grp", "pool"), "tp"),
        P(("grp", "pool"), "tp"),
        P("tp", None),
        P("pool", "tp", None),
        P("pool", None, None, "tp"),
        P(("grp", "pool"), "tp", None, None),
        P(("grp", "pool"), "tp", None, None),
        P(("grp", "pool"), None),
        P(("grp", "pool")),
        P(),
    )
    out_specs = (P(("grp", "pool"), "tp"), P(("grp", "pool"), "tp"))
    return jax.shard_map(shards, mesh=mesh, in_specs=in_specs, out_specs=out_specs, check_vma=False)
```

```python
import functools

import jax
import jax.numpy as jnp
from jax import lax
from jax.experimental import pallas as pl
from jax.experimental.pallas import tpu as pltpu
from jax.sharding import PartitionSpec as P

BF16 = jnp.bfloat16
F32 = jnp.float32
I32 = jnp.int32
VMEM_LIMIT = 48 * 1024 * 1024


def iota(shape, dim):
    return lax.broadcasted_iota(I32, shape, dim)


def split_count(cap):
    pieces = 4
    while cap * pieces % 16:
        pieces *= 2
    return pieces


def dot(a, b):
    return jnp.dot(a, b, preferred_element_type=F32)


def dot_first(a, b):
    return lax.dot_general(a, b, (((0,), (0,)), ((), ())), preferred_element_type=F32)


def select_sum(one_hot, x):
    high = x.astype(BF16)
    low = (x - high.astype(F32)).astype(BF16)
    both = dot(one_hot, jnp.concatenate([high, low], axis=1))
    return both[:, : x.shape[1]] + both[:, x.shape[1] :]


def codes_of(place, rank, cap, pieces):
    code = place * (pieces * cap) + rank
    return jnp.concatenate([code + piece * cap for piece in range(pieces)], axis=1)


def one_hot_of(codes, first, count):
    return ((iota((count, codes.shape[1]), 0) + first) == codes).astype(F32).astype(BF16)


def stack_pieces(hidden, pieces):
    width = hidden.shape[1] // pieces
    return jnp.concatenate(
        [hidden[:, piece * width : (piece + 1) * width] for piece in range(pieces)], axis=0
    )


def route_kernel(n, idx_ref, table_ref, slot_ref, rank_ref):
    rows = idx_ref.shape[1]
    named = (iota((n, rows), 0) == idx_ref[...]).astype(F32).astype(BF16)
    table = jnp.broadcast_to(table_ref[...].astype(F32).astype(BF16), (16, n))
    slot = dot(table, named)[0:1, :].astype(I32)
    member = (iota((n, rows), 0) == slot).astype(F32)
    before = (iota((rows, rows), 0) < iota((rows, rows), 1)).astype(F32).astype(BF16)
    count = dot(member.astype(BF16), before)
    slot_ref[...] = slot
    rank_ref[...] = jnp.sum(member * count, axis=0, keepdims=True).astype(I32)


def pack_kernel(n, cap, pieces, me_ref, slot_ref, rank_ref, hidden_ref, stacked_ref, *out_refs):
    per = pieces * cap
    apart = lax.bitwise_xor(slot_ref[...], me_ref[0])
    one_hot = one_hot_of(codes_of(apart, rank_ref[...], cap, pieces), 0, n * per)
    stacked = stack_pieces(hidden_ref[...], pieces)
    stacked_ref[...] = stacked
    packed = dot(one_hot, stacked).astype(BF16)
    for s, out_ref in enumerate(out_refs):
        out_ref[...] = packed[s * per : (s + 1) * per]


def tables_kernel(n, cap, pieces, out_pieces, me_ref, _, shrink_ref, expand_ref):
    per = pieces * cap
    out_row, in_row = iota(shrink_ref.shape, 0), iota(shrink_ref.shape, 1)
    same = (out_row // cap == in_row // per) & (out_row % cap == in_row % cap)
    shrink_ref[...] = same.astype(F32).astype(BF16)
    per = out_pieces * cap
    out_row, in_row = iota(expand_ref.shape, 0), iota(expand_ref.shape, 1)
    apart = lax.bitwise_xor(out_row // per, me_ref[0])
    source = (out_row // cap % out_pieces) * (n * cap) + apart * cap + out_row % cap
    expand_ref[...] = (source == in_row).astype(F32).astype(BF16)


def shrink_kernel(n, cap, pieces, order, *refs):
    received_refs, (down_ref, table_ref, base_ref, out_ref) = dict(zip(order, refs[:n])), refs[n:]
    width = refs[0].shape[1]
    rank2 = down_ref.shape[2]
    received = jnp.concatenate([received_refs[s][...] for s in range(n)], axis=0)
    size = received.shape[0]
    total = jnp.zeros((size, rank2), F32)
    piece_of = (iota((size, rank2), 0) // cap) % pieces
    for piece in range(0, pieces, 2):
        pair = [down_ref[0, i * width : (i + 1) * width, :] for i in (piece, piece + 1)]
        part = dot(received, jnp.concatenate(pair, axis=1))
        total = total + jnp.where(piece_of == piece, part[:, :rank2], 0.0)
        total = total + jnp.where(piece_of == piece + 1, part[:, rank2:], 0.0)
    reduced = select_sum(table_ref[...], total)
    size = reduced.shape[0]
    out_ref[:size, :] = reduced
    rows = base_ref.shape[0]
    for i in range(base_ref.shape[1] // rank2):
        first = size + i * rows
        out_ref[first : first + rows, :] = base_ref[:, i * rank2 : (i + 1) * rank2]


def expand_kernel(n, cap, mine_ref, other_ref, up_ref, table_ref, out_ref):
    rank = up_ref.shape[2]
    head = 128
    blocks = up_ref.shape[3] // head
    reduced = (mine_ref[: n * cap, :] + other_ref[: n * cap, :]).astype(BF16)
    terms = []
    for c in range(2):
        kept = reduced[:, c * rank : (c + 1) * rank]
        wide = dot(kept, up_ref[0, c]).astype(BF16)
        terms += [wide[:, g * head : (g + 1) * head] for g in range(blocks)]
    out_ref[...] = dot(table_ref[...], jnp.concatenate(terms, axis=0)).astype(BF16)


def prepare_kernel(n, cap, slot_ref, rank_ref, mine_ref, other_ref, _, base_ref, one_hot_ref):
    pieces = one_hot_ref.shape[0] // slot_ref.shape[1]
    size = one_hot_ref.shape[1]
    rows = mine_ref.shape[0]
    width = other_ref.shape[1]
    for i in range(mine_ref.shape[1] // width):
        lanes, first = slice(i * width, (i + 1) * width), n * cap + i * rows
        base_ref[:, lanes] = mine_ref[:, lanes] + other_ref[first : first + rows, :]
    one_hot = one_hot_of(codes_of(slot_ref[...], rank_ref[...], cap, pieces), 0, size)
    same = (iota((size, size), 0) == iota((size, size), 1)).astype(F32).astype(BF16)
    one_hot_ref[...] = dot_first(one_hot, same).astype(BF16)


def base_kernel(
    pieces, core_ref, stacked_ref, weight_hbm, first_ref, second_ref, mine_ref, other_ref, weight_ref, sems
):
    depth = weight_ref.shape[0] // pieces
    copies = []
    for k in range(pieces):
        part = pl.ds(k * depth, depth)
        copies.append(pltpu.make_async_copy(weight_hbm.at[part, :], weight_ref.at[part, :], sems.at[k]))
        copies[k].start()
    rows, columns = mine_ref.shape
    total = jnp.zeros((rows, 2 * columns), F32)
    for k in range(pieces):
        copies[k].wait()
        total = total + dot(stacked_ref[k * rows : (k + 1) * rows, :], weight_ref[k * depth : (k + 1) * depth, :])
    first, second = total[:, :columns], total[:, columns:]
    mine_ref[...] = jnp.where(core_ref[0] == 0, first, second)
    other_ref[...] = jnp.where(core_ref[0] == 0, second, first)


def cache_kernel(query_ref, key_ref, value_ref, length_ref, _, acc_ref, max_ref, sum_ref):
    rows, groups, positions, head = key_ref.shape
    per_group = query_ref.shape[1] // (groups * head)
    tile = 16
    wide, deep = tile * positions, tile * per_group
    scale = head ** (-0.5)
    row_of = iota((deep, wide), 0) % tile
    own_row = row_of == iota((deep, wide), 1) // positions
    position = iota((deep, wide), 1) % positions
    lane = iota((tile, head), 1)
    for first in range(0, rows, tile):
        at = slice(first, first + tile)
        length = jnp.concatenate([length_ref[at, :]] * per_group, axis=0)
        valid = own_row & (position < length)
        tops = jnp.zeros((tile, head), F32)
        sums = jnp.zeros((tile, head), F32)
        for g in range(groups):
            query = jnp.concatenate(
                [query_ref[at, h * head : (h + 1) * head] for h in range(g * per_group, (g + 1) * per_group)],
                axis=0,
            )
            key = key_ref[at, g].reshape(wide, head)
            value = value_ref[at, g].reshape(wide, head)
            scores = lax.dot_general(query, key, (((1,), (1,)), ((), ())), preferred_element_type=F32)
            scores = jnp.where(valid, scores * scale, -jnp.inf)
            top = jnp.max(scores, axis=1, keepdims=True)
            weight = jnp.exp(scores - top)
            total = jnp.sum(weight, axis=1, keepdims=True)
            mixed = dot(weight.astype(BF16), value)
            for i in range(per_group):
                h = g * per_group + i
                part = slice(i * tile, (i + 1) * tile)
                acc_ref[at, h * head : (h + 1) * head] = mixed[part]
                tops = jnp.where(lane == h, top[part], tops)
                sums = jnp.where(lane == h, total[part], sums)
        max_ref[at, :] = tops
        sum_ref[at, :] = sums


def combine_kernel(
    delta_ref, one_hot_ref, base_ref, query_ref, max_ref, sum_ref, acc_ref, token_ref, out_ref
):
    rows = base_ref.shape[0]
    head = 128
    groups = base_ref.shape[1] // (2 * head)
    delta = dot(one_hot_ref[...], delta_ref[...])
    heads = query_ref.shape[1] // head
    per_group = heads // groups
    scale = head ** (-0.5)
    lane = iota((rows, head), 1)
    own = jnp.zeros((rows, head), F32)
    values = []
    for g in range(groups):
        made = []
        for c in range(2):
            at = (g * 2 + c) * head
            piece = c * groups + g
            made.append((base_ref[:, at : at + head] + delta[piece * rows : (piece + 1) * rows]).astype(BF16))
            token_ref[:, at : at + head] = made[-1]
        key = made[0].astype(F32)
        values.append(made[1].astype(F32))
        for h in range(g * per_group, (g + 1) * per_group):
            query = query_ref[:, h * head : (h + 1) * head].astype(F32)
            own = jnp.where(lane == h, jnp.sum(query * key, axis=1, keepdims=True), own)
    own = own[:, :heads] * scale
    cache_max = max_ref[:, :heads]
    highest = jnp.maximum(own, cache_max)
    cache_factor = jnp.exp(cache_max - highest)
    own_factor = jnp.exp(own - highest)
    inverse = 1.0 / (sum_ref[:, :heads] * cache_factor + own_factor)
    cache_factor = cache_factor * inverse
    own_factor = own_factor * inverse
    for h in range(heads):
        lanes = slice(h * head, (h + 1) * head)
        out = acc_ref[:, lanes] * cache_factor[:, h : h + 1]
        out = out + values[h // per_group] * own_factor[:, h : h + 1]
        out_ref[:, lanes] = out.astype(BF16)


VMEM = pl.BlockSpec(memory_space=pltpu.VMEM)
SMEM = pl.BlockSpec(memory_space=pltpu.SMEM)
HBM = pl.BlockSpec(memory_space=pltpu.HBM)
ANY = pl.BlockSpec(memory_space=pl.ANY)
NO_COST = pl.CostEstimate(flops=0, bytes_accessed=0, transcendentals=0)


def call(kernel, outs, specs, scratch=(), cost=NO_COST):
    return pl.pallas_call(
        kernel,
        out_shape=outs,
        in_specs=specs,
        out_specs=[VMEM] * len(outs),
        scratch_shapes=scratch,
        compiler_params=pltpu.CompilerParams(vmem_limit_bytes=VMEM_LIMIT),
        cost_estimate=cost,
    )


def shards(
    hidden,
    queries,
    key_value_weight,
    adapter_down_weight,
    adapter_up_weight,
    stored_cache_keys,
    stored_cache_values,
    row_adapter_index,
    stored_cache_lengths,
    adapter_slot_table,
):
    n = lax.axis_size("pool")
    rows, width = hidden.shape
    cap = -(-2 * rows // n)
    pieces = split_count(cap)
    groups = stored_cache_keys.shape[1]
    head = stored_cache_keys.shape[3]
    columns = key_value_weight.shape[1] // 2
    out_pieces = 2 * groups
    rank2 = adapter_down_weight.shape[2]

    swap = functools.partial(lax.ppermute, axis_name="tp", perm=[(0, 1), (1, 0)])

    me = lax.axis_index("pool").reshape(1)
    slot, rank = call(
        functools.partial(route_kernel, n), [jax.ShapeDtypeStruct((1, rows), I32)] * 2, [VMEM] * 2
    )(row_adapter_index.reshape(1, rows), adapter_slot_table.reshape(1, n))
    stacked, *packed = call(
        functools.partial(pack_kernel, n, cap, pieces),
        [jax.ShapeDtypeStruct((pieces * rows, width // pieces), BF16)]
        + [jax.ShapeDtypeStruct((pieces * cap, width // pieces), BF16)] * n,
        [SMEM, VMEM, VMEM, VMEM],
    )(me, slot, rank, hidden)
    half = n // 2
    order = [0, half, 1, half + 1, 2, *range(half + 2, n), *range(3, half)]
    arrived = {0: packed[0]}
    for s in order[1:]:
        arrived[s] = lax.ppermute(packed[s], "pool", [(i, i ^ s) for i in range(n)])

    base_mine, base_other = call(
        functools.partial(base_kernel, pieces),
        [jax.ShapeDtypeStruct((rows, columns), F32)] * 2,
        [SMEM, VMEM, ANY, ANY, ANY],
        [pltpu.VMEM((width, 2 * columns), BF16), pltpu.SemaphoreType.DMA((pieces,))],
        pl.CostEstimate(
            flops=4 * rows * width * columns, bytes_accessed=16 * width * columns, transcendentals=0
        ),
    )(lax.axis_index("tp").reshape(1), stacked, key_value_weight, arrived[1], arrived[2])

    size = n * out_pieces * cap
    shrink_table, expand_table = call(
        functools.partial(tables_kernel, n, cap, pieces, out_pieces),
        [
            jax.ShapeDtypeStruct((n * cap, n * pieces * cap), BF16),
            jax.ShapeDtypeStruct((size, size), BF16),
        ],
        [SMEM, ANY],
    )(me, base_mine)
    (sums,) = call(
        functools.partial(shrink_kernel, n, cap, pieces, order),
        [jax.ShapeDtypeStruct((n * cap + rows * columns // rank2, rank2), F32)],
        [VMEM] * (n + 3),
    )(*[arrived[s] for s in order], adapter_down_weight, shrink_table, base_other)
    other_sums = swap(sums)
    (terms,) = call(
        functools.partial(expand_kernel, n, cap),
        [jax.ShapeDtypeStruct((size, head), BF16)],
        [VMEM] * 4,
    )(sums, other_sums, adapter_up_weight, expand_table)
    base, one_hot = call(
        functools.partial(prepare_kernel, n, cap),
        [
            jax.ShapeDtypeStruct((rows, columns), F32),
            jax.ShapeDtypeStruct((out_pieces * rows, size), BF16),
        ],
        [VMEM] * 4 + [ANY],
    )(slot, rank, base_mine, other_sums, terms)
    deltas = lax.all_to_all(terms, "pool", split_axis=0, concat_axis=0, tiled=True)
    attended, cache_max, cache_sum = call(
        cache_kernel,
        [jax.ShapeDtypeStruct(queries.shape, F32)] + [jax.ShapeDtypeStruct((rows, head), F32)] * 2,
        [VMEM] * 4 + [ANY],
    )(queries, stored_cache_keys, stored_cache_values, stored_cache_lengths.reshape(rows, 1), terms)
    token, out = call(
        combine_kernel,
        [jax.ShapeDtypeStruct((rows, columns), BF16), jax.ShapeDtypeStruct(queries.shape, BF16)],
        [VMEM] * 7,
    )(deltas, one_hot, base, queries, cache_max, cache_sum, attended)
    return token, out


def solution(mesh):
    in_specs = (
        P(("grp", "pool"), "tp"),
        P(("grp", "pool"), "tp"),
        P("tp", None),
        P("pool", "tp", None),
        P("pool", None, None, "tp"),
        P(("grp", "pool"), "tp", None, None),
        P(("grp", "pool"), "tp", None, None),
        P(("grp", "pool"), None),
        P(("grp", "pool")),
        P(),
    )
    out_specs = (P(("grp", "pool"), "tp"), P(("grp", "pool"), "tp"))
    return jax.shard_map(shards, mesh=mesh, in_specs=in_specs, out_specs=out_specs, check_vma=False)
```

```python
import functools

import jax
import jax.numpy as jnp
from jax import lax
from jax.experimental import pallas as pl
from jax.experimental.pallas import tpu as pltpu
from jax.sharding import PartitionSpec as P

BF16 = jnp.bfloat16
F32 = jnp.float32
I32 = jnp.int32
VMEM_LIMIT = 48 * 1024 * 1024


def iota(shape, dim):
    return lax.broadcasted_iota(I32, shape, dim)


def split_count(cap):
    pieces = 4
    while cap * pieces % 16:
        pieces *= 2
    return pieces


def dot(a, b):
    return jnp.dot(a, b, preferred_element_type=F32)


def dot_first(a, b):
    return lax.dot_general(a, b, (((0,), (0,)), ((), ())), preferred_element_type=F32)


def select_sum(one_hot, x):
    high = x.astype(BF16)
    low = (x - high.astype(F32)).astype(BF16)
    both = dot(one_hot, jnp.concatenate([high, low], axis=1))
    return both[:, : x.shape[1]] + both[:, x.shape[1] :]


def codes_of(place, rank, cap, pieces):
    code = place * (pieces * cap) + rank
    return jnp.concatenate([code + piece * cap for piece in range(pieces)], axis=1)


def one_hot_of(codes, first, count):
    return ((iota((count, codes.shape[1]), 0) + first) == codes).astype(F32).astype(BF16)


def stack_pieces(hidden, pieces):
    width = hidden.shape[1] // pieces
    return jnp.concatenate(
        [hidden[:, piece * width : (piece + 1) * width] for piece in range(pieces)], axis=0
    )


def pack_kernel(n, cap, pieces, me_ref, idx_ref, table_ref, hidden_ref, slot_ref, rank_ref, *out_refs):
    rows = hidden_ref.shape[0]
    named = (iota((n, rows), 0) == idx_ref[...]).astype(F32).astype(BF16)
    table = jnp.broadcast_to(table_ref[...].astype(F32).astype(BF16), (16, n))
    slot = dot(table, named)[0:1, :].astype(I32)
    member = (iota((n, rows), 0) == slot).astype(F32)
    before = (iota((rows, rows), 0) < iota((rows, rows), 1)).astype(F32).astype(BF16)
    count = dot(member.astype(BF16), before)
    rank = jnp.sum(member * count, axis=0, keepdims=True).astype(I32)
    slot_ref[...] = slot
    rank_ref[...] = rank
    per = pieces * cap
    apart = lax.bitwise_xor(slot, me_ref[0])
    one_hot = one_hot_of(codes_of(apart, rank, cap, pieces), 0, n * per)
    packed = dot(one_hot, stack_pieces(hidden_ref[...], pieces)).astype(BF16)
    for s, out_ref in enumerate(out_refs):
        out_ref[...] = packed[s * per : (s + 1) * per]


def tables_kernel(n, cap, pieces, out_pieces, me_ref, _, shrink_ref, expand_ref):
    per = pieces * cap
    out_row, in_row = iota(shrink_ref.shape, 0), iota(shrink_ref.shape, 1)
    same = (out_row // cap == in_row // per) & (out_row % cap == in_row % cap)
    shrink_ref[...] = same.astype(F32).astype(BF16)
    per = out_pieces * cap
    out_row, in_row = iota(expand_ref.shape, 0), iota(expand_ref.shape, 1)
    apart = lax.bitwise_xor(out_row // per, me_ref[0])
    source = (out_row // cap % out_pieces) * (n * cap) + apart * cap + out_row % cap
    expand_ref[...] = (source == in_row).astype(F32).astype(BF16)


def shrink(cap, pieces, received_refs, down_ref, table_ref):
    width = received_refs[0].shape[1]
    rank2 = down_ref.shape[2]
    received = jnp.concatenate([ref[...] for ref in received_refs], axis=0)
    size = received.shape[0]
    total = jnp.zeros((size, rank2), F32)
    piece_of = (iota((size, rank2), 0) // cap) % pieces
    for piece in range(pieces):
        part = dot(received, down_ref[0, piece * width : (piece + 1) * width, :])
        total = total + jnp.where(piece_of == piece, part, 0.0)
    return select_sum(table_ref[...], total)


def shrink_near_kernel(cap, pieces, *refs):
    refs[-1][...] = shrink(cap, pieces, refs[:-3], *refs[-3:-1])


def shrink_far_kernel(cap, pieces, *refs):
    near_ref, base_ref, out_ref = refs[-3:]
    half = near_ref.shape[0]
    out_ref[:half, :] = near_ref[...]
    out_ref[half : 2 * half, :] = shrink(cap, pieces, refs[:-5], *refs[-5:-3])
    rows = base_ref.shape[0]
    lanes = out_ref.shape[1]
    for i in range(base_ref.shape[1] // lanes):
        first = 2 * half + i * rows
        out_ref[first : first + rows, :] = base_ref[:, i * lanes : (i + 1) * lanes]


def expand_kernel(n, cap, mine_ref, other_ref, up_ref, table_ref, out_ref):
    rank = up_ref.shape[2]
    head = 128
    blocks = up_ref.shape[3] // head
    reduced = (mine_ref[: n * cap, :] + other_ref[: n * cap, :]).astype(BF16)
    terms = []
    for c in range(2):
        kept = reduced[:, c * rank : (c + 1) * rank]
        wide = dot(kept, up_ref[0, c]).astype(BF16)
        terms += [wide[:, g * head : (g + 1) * head] for g in range(blocks)]
    out_ref[...] = dot(table_ref[...], jnp.concatenate(terms, axis=0)).astype(BF16)


def prepare_kernel(n, cap, slot_ref, rank_ref, mine_ref, other_ref, _, base_ref, one_hot_ref):
    pieces = one_hot_ref.shape[0] // slot_ref.shape[1]
    size = one_hot_ref.shape[1]
    rows = mine_ref.shape[0]
    width = other_ref.shape[1]
    for i in range(mine_ref.shape[1] // width):
        lanes, first = slice(i * width, (i + 1) * width), n * cap + i * rows
        base_ref[:, lanes] = mine_ref[:, lanes] + other_ref[first : first + rows, :]
    one_hot = one_hot_of(codes_of(slot_ref[...], rank_ref[...], cap, pieces), 0, size)
    same = (iota((size, size), 0) == iota((size, size), 1)).astype(F32).astype(BF16)
    one_hot_ref[...] = dot_first(one_hot, same).astype(BF16)


def base_kernel(
    core_ref, hidden_ref, weight_hbm, first_ref, second_ref, mine_ref, other_ref, weight_ref, sems
):
    blocks, depth = weight_ref.shape[:2]
    copies = []
    for k in range(blocks):
        part = weight_hbm.at[pl.ds(k * depth, depth), :]
        copies.append(pltpu.make_async_copy(part, weight_ref.at[k], sems.at[k]))
        copies[k].start()
    rows, columns = mine_ref.shape
    total = jnp.zeros((rows, 2 * columns), F32)
    for k in range(blocks):
        copies[k].wait()
        total = total + dot(hidden_ref[:, k * depth : (k + 1) * depth], weight_ref[k])
    first, second = total[:, :columns], total[:, columns:]
    mine_ref[...] = jnp.where(core_ref[0] == 0, first, second)
    other_ref[...] = jnp.where(core_ref[0] == 0, second, first)


def cache_kernel(query_ref, key_ref, value_ref, length_ref, _, acc_ref, max_ref, sum_ref):
    rows, groups, positions, head = key_ref.shape
    per_group = query_ref.shape[1] // (groups * head)
    tile = 16
    wide, deep = tile * positions, tile * per_group
    scale = head ** (-0.5)
    row_of = iota((deep, wide), 0) % tile
    own_row = row_of == iota((deep, wide), 1) // positions
    position = iota((deep, wide), 1) % positions
    lane = iota((tile, head), 1)
    for first in range(0, rows, tile):
        at = slice(first, first + tile)
        length = jnp.concatenate([length_ref[at, :]] * per_group, axis=0)
        valid = own_row & (position < length)
        tops = jnp.zeros((tile, head), F32)
        sums = jnp.zeros((tile, head), F32)
        for g in range(groups):
            query = jnp.concatenate(
                [query_ref[at, h * head : (h + 1) * head] for h in range(g * per_group, (g + 1) * per_group)],
                axis=0,
            )
            key = key_ref[at, g].reshape(wide, head)
            value = value_ref[at, g].reshape(wide, head)
            scores = lax.dot_general(query, key, (((1,), (1,)), ((), ())), preferred_element_type=F32)
            scores = jnp.where(valid, scores * scale, -jnp.inf)
            top = jnp.max(scores, axis=1, keepdims=True)
            weight = jnp.exp(scores - top)
            total = jnp.sum(weight, axis=1, keepdims=True)
            mixed = dot(weight.astype(BF16), value)
            for i in range(per_group):
                h = g * per_group + i
                part = slice(i * tile, (i + 1) * tile)
                acc_ref[at, h * head : (h + 1) * head] = mixed[part]
                tops = jnp.where(lane == h, top[part], tops)
                sums = jnp.where(lane == h, total[part], sums)
        max_ref[at, :] = tops
        sum_ref[at, :] = sums


def combine_kernel(
    delta_ref, one_hot_ref, base_ref, query_ref, max_ref, sum_ref, acc_ref, token_ref, out_ref
):
    rows = base_ref.shape[0]
    head = 128
    groups = base_ref.shape[1] // (2 * head)
    delta = dot(one_hot_ref[...], delta_ref[...])
    heads = query_ref.shape[1] // head
    per_group = heads // groups
    scale = head ** (-0.5)
    lane = iota((rows, head), 1)
    own = jnp.zeros((rows, head), F32)
    values = []
    for g in range(groups):
        made = []
        for c in range(2):
            at = (g * 2 + c) * head
            piece = c * groups + g
            made.append((base_ref[:, at : at + head] + delta[piece * rows : (piece + 1) * rows]).astype(BF16))
            token_ref[:, at : at + head] = made[-1]
        key = made[0].astype(F32)
        values.append(made[1].astype(F32))
        for h in range(g * per_group, (g + 1) * per_group):
            query = query_ref[:, h * head : (h + 1) * head].astype(F32)
            own = jnp.where(lane == h, jnp.sum(query * key, axis=1, keepdims=True), own)
    own = own[:, :heads] * scale
    cache_max = max_ref[:, :heads]
    highest = jnp.maximum(own, cache_max)
    cache_factor = jnp.exp(cache_max - highest)
    own_factor = jnp.exp(own - highest)
    inverse = 1.0 / (sum_ref[:, :heads] * cache_factor + own_factor)
    cache_factor = cache_factor * inverse
    own_factor = own_factor * inverse
    for h in range(heads):
        lanes = slice(h * head, (h + 1) * head)
        out = acc_ref[:, lanes] * cache_factor[:, h : h + 1]
        out = out + values[h // per_group] * own_factor[:, h : h + 1]
        out_ref[:, lanes] = out.astype(BF16)


VMEM = pl.BlockSpec(memory_space=pltpu.VMEM)
SMEM = pl.BlockSpec(memory_space=pltpu.SMEM)
HBM = pl.BlockSpec(memory_space=pltpu.HBM)
ANY = pl.BlockSpec(memory_space=pl.ANY)
NO_COST = pl.CostEstimate(flops=0, bytes_accessed=0, transcendentals=0)


def call(kernel, outs, specs, scratch=(), cost=NO_COST):
    return pl.pallas_call(
        kernel,
        out_shape=outs,
        in_specs=specs,
        out_specs=[VMEM] * len(outs),
        scratch_shapes=scratch,
        compiler_params=pltpu.CompilerParams(vmem_limit_bytes=VMEM_LIMIT),
        cost_estimate=cost,
    )


def shards(
    hidden,
    queries,
    key_value_weight,
    adapter_down_weight,
    adapter_up_weight,
    stored_cache_keys,
    stored_cache_values,
    row_adapter_index,
    stored_cache_lengths,
    adapter_slot_table,
):
    n = lax.axis_size("pool")
    rows, width = hidden.shape
    cap = -(-2 * rows // n)
    pieces = split_count(cap)
    groups = stored_cache_keys.shape[1]
    head = stored_cache_keys.shape[3]
    columns = key_value_weight.shape[1] // 2
    out_pieces = 2 * groups
    rank2 = adapter_down_weight.shape[2]

    swap = functools.partial(lax.ppermute, axis_name="tp", perm=[(0, 1), (1, 0)])

    me = lax.axis_index("pool").reshape(1)
    slot, rank, *packed = call(
        functools.partial(pack_kernel, n, cap, pieces),
        [jax.ShapeDtypeStruct((1, rows), I32)] * 2
        + [jax.ShapeDtypeStruct((pieces * cap, width // pieces), BF16)] * n,
        [SMEM, VMEM, VMEM, VMEM],
    )(me, row_adapter_index.reshape(1, rows), adapter_slot_table.reshape(1, n), hidden)
    half = n // 2
    order = [0, 1, 2, *range(half, n), *range(3, half)]
    arrived = {0: packed[0]}
    for s in order[1:]:
        arrived[s] = lax.ppermute(packed[s], "pool", [(i, i ^ s) for i in range(n)])

    blocks = 4
    base_mine, base_other = call(
        base_kernel,
        [jax.ShapeDtypeStruct((rows, columns), F32)] * 2,
        [SMEM, VMEM, ANY, ANY, ANY],
        [
            pltpu.VMEM((blocks, width // blocks, 2 * columns), BF16),
            pltpu.SemaphoreType.DMA((blocks,)),
        ],
        pl.CostEstimate(
            flops=4 * rows * width * columns, bytes_accessed=16 * width * columns, transcendentals=0
        ),
    )(lax.axis_index("tp").reshape(1), hidden, key_value_weight, arrived[1], arrived[2])

    size = n * out_pieces * cap
    shrink_table, expand_table = call(
        functools.partial(tables_kernel, n, cap, pieces, out_pieces),
        [
            jax.ShapeDtypeStruct((half * cap, half * pieces * cap), BF16),
            jax.ShapeDtypeStruct((size, size), BF16),
        ],
        [SMEM, ANY],
    )(me, base_mine)
    (near_sum,) = call(
        functools.partial(shrink_near_kernel, cap, pieces),
        [jax.ShapeDtypeStruct((half * cap, rank2), F32)],
        [VMEM] * (half + 2),
    )(*[arrived[s] for s in range(half)], adapter_down_weight, shrink_table)
    (sums,) = call(
        functools.partial(shrink_far_kernel, cap, pieces),
        [jax.ShapeDtypeStruct((n * cap + rows * columns // rank2, rank2), F32)],
        [VMEM] * (half + 4),
    )(*[arrived[s] for s in range(half, n)], adapter_down_weight, shrink_table, near_sum, base_other)
    other_sums = swap(sums)
    (terms,) = call(
        functools.partial(expand_kernel, n, cap),
        [jax.ShapeDtypeStruct((size, head), BF16)],
        [VMEM] * 4,
    )(sums, other_sums, adapter_up_weight, expand_table)
    base, one_hot = call(
        functools.partial(prepare_kernel, n, cap),
        [
            jax.ShapeDtypeStruct((rows, columns), F32),
            jax.ShapeDtypeStruct((out_pieces * rows, size), BF16),
        ],
        [VMEM] * 4 + [ANY],
    )(slot, rank, base_mine, other_sums, terms)
    deltas = lax.all_to_all(terms, "pool", split_axis=0, concat_axis=0, tiled=True)
    attended, cache_max, cache_sum = call(
        cache_kernel,
        [jax.ShapeDtypeStruct(queries.shape, F32)] + [jax.ShapeDtypeStruct((rows, head), F32)] * 2,
        [VMEM] * 4 + [ANY],
    )(queries, stored_cache_keys, stored_cache_values, stored_cache_lengths.reshape(rows, 1), terms)
    token, out = call(
        combine_kernel,
        [jax.ShapeDtypeStruct((rows, columns), BF16), jax.ShapeDtypeStruct(queries.shape, BF16)],
        [VMEM] * 7,
    )(deltas, one_hot, base, queries, cache_max, cache_sum, attended)
    return token, out


def solution(mesh):
    in_specs = (
        P(("grp", "pool"), "tp"),
        P(("grp", "pool"), "tp"),
        P("tp", None),
        P("pool", "tp", None),
        P("pool", None, None, "tp"),
        P(("grp", "pool"), "tp", None, None),
        P(("grp", "pool"), "tp", None, None),
        P(("grp", "pool"), None),
        P(("grp", "pool")),
        P(),
    )
    out_specs = (P(("grp", "pool"), "tp"), P(("grp", "pool"), "tp"))
    return jax.shard_map(shards, mesh=mesh, in_specs=in_specs, out_specs=out_specs, check_vma=False)
```

```python
import functools

import jax
import jax.numpy as jnp
from jax import lax
from jax.experimental import pallas as pl
from jax.experimental.pallas import tpu as pltpu
from jax.sharding import PartitionSpec as P

BF16 = jnp.bfloat16
F32 = jnp.float32
I32 = jnp.int32
VMEM_LIMIT = 20 * 1024 * 1024


def iota(shape, dim):
    return lax.broadcasted_iota(I32, shape, dim)


def split_count(cap):
    pieces = 4
    while cap * pieces % 16:
        pieces *= 2
    return pieces


def dot(a, b):
    return jnp.dot(a, b, preferred_element_type=F32)


def dot_first(a, b):
    return lax.dot_general(a, b, (((0,), (0,)), ((), ())), preferred_element_type=F32)


def select_sum(one_hot, x):
    high = x.astype(BF16)
    low = (x - high.astype(F32)).astype(BF16)
    both = dot(one_hot, jnp.concatenate([high, low], axis=1))
    return both[:, : x.shape[1]] + both[:, x.shape[1] :]


def codes_of(place, rank, cap, pieces):
    code = place * (pieces * cap) + rank
    return jnp.concatenate([code + piece * cap for piece in range(pieces)], axis=1)


def one_hot_of(codes, first, count):
    return ((iota((count, codes.shape[1]), 0) + first) == codes).astype(F32).astype(BF16)


def stack_pieces(hidden, pieces):
    width = hidden.shape[1] // pieces
    return jnp.concatenate(
        [hidden[:, piece * width : (piece + 1) * width] for piece in range(pieces)], axis=0
    )


def pack_kernel(n, cap, pieces, me_ref, idx_ref, table_ref, hidden_ref, slot_ref, rank_ref, *out_refs):
    rows = hidden_ref.shape[0]
    named = (iota((n, rows), 0) == idx_ref[...]).astype(F32).astype(BF16)
    table = jnp.broadcast_to(table_ref[...].astype(F32).astype(BF16), (16, n))
    slot = dot(table, named)[0:1, :].astype(I32)
    member = (iota((n, rows), 0) == slot).astype(F32)
    before = (iota((rows, rows), 0) < iota((rows, rows), 1)).astype(F32).astype(BF16)
    count = dot(member.astype(BF16), before)
    rank = jnp.sum(member * count, axis=0, keepdims=True).astype(I32)
    slot_ref[...] = slot
    rank_ref[...] = rank
    per = pieces * cap
    apart = lax.bitwise_xor(slot, me_ref[0])
    one_hot = one_hot_of(codes_of(apart, rank, cap, pieces), 0, n * per)
    packed = dot(one_hot, stack_pieces(hidden_ref[...], pieces)).astype(BF16)
    for s, out_ref in enumerate(out_refs):
        out_ref[...] = packed[s * per : (s + 1) * per]


def tables_kernel(n, cap, pieces, out_pieces, me_ref, _, shrink_ref, expand_ref):
    per = pieces * cap
    out_row, in_row = iota(shrink_ref.shape, 0), iota(shrink_ref.shape, 1)
    same = (out_row // cap == in_row // per) & (out_row % cap == in_row % cap)
    shrink_ref[...] = same.astype(F32).astype(BF16)
    per = out_pieces * cap
    out_row, in_row = iota(expand_ref.shape, 0), iota(expand_ref.shape, 1)
    apart = lax.bitwise_xor(out_row // per, me_ref[0])
    source = (out_row // cap % out_pieces) * (n * cap) + apart * cap + out_row % cap
    expand_ref[...] = (source == in_row).astype(F32).astype(BF16)


def shrink(cap, pieces, received_refs, down_ref, table_ref):
    width = received_refs[0].shape[1]
    rank2 = down_ref.shape[2]
    received = jnp.concatenate([ref[...] for ref in received_refs], axis=0)
    size = received.shape[0]
    total = jnp.zeros((size, rank2), F32)
    piece_of = (iota((size, rank2), 0) // cap) % pieces
    for piece in range(pieces):
        part = dot(received, down_ref[0, piece * width : (piece + 1) * width, :])
        total = total + jnp.where(piece_of == piece, part, 0.0)
    return select_sum(table_ref[...], total)


def shrink_near_kernel(cap, pieces, *refs):
    refs[-1][...] = shrink(cap, pieces, refs[:-3], *refs[-3:-1])


def shrink_far_kernel(cap, pieces, *refs):
    near_ref, base_ref, out_ref = refs[-3:]
    half = near_ref.shape[0]
    out_ref[:half, :] = near_ref[...]
    out_ref[half : 2 * half, :] = shrink(cap, pieces, refs[:-5], *refs[-5:-3])
    rows = base_ref.shape[0]
    lanes = out_ref.shape[1]
    for i in range(base_ref.shape[1] // lanes):
        first = 2 * half + i * rows
        out_ref[first : first + rows, :] = base_ref[:, i * lanes : (i + 1) * lanes]


def expand_kernel(n, cap, mine_ref, other_ref, up_ref, table_ref, out_ref):
    rank = up_ref.shape[2]
    head = 128
    blocks = up_ref.shape[3] // head
    reduced = (mine_ref[: n * cap, :] + other_ref[: n * cap, :]).astype(BF16)
    terms = []
    for c in range(2):
        kept = reduced[:, c * rank : (c + 1) * rank]
        wide = dot(kept, up_ref[0, c]).astype(BF16)
        terms += [wide[:, g * head : (g + 1) * head] for g in range(blocks)]
    out_ref[...] = dot(table_ref[...], jnp.concatenate(terms, axis=0)).astype(BF16)


def prepare_kernel(n, cap, slot_ref, rank_ref, mine_ref, other_ref, _, base_ref, one_hot_ref):
    pieces = one_hot_ref.shape[0] // slot_ref.shape[1]
    size = one_hot_ref.shape[1]
    rows = mine_ref.shape[0]
    width = other_ref.shape[1]
    for i in range(mine_ref.shape[1] // width):
        lanes, first = slice(i * width, (i + 1) * width), n * cap + i * rows
        base_ref[:, lanes] = mine_ref[:, lanes] + other_ref[first : first + rows, :]
    one_hot = one_hot_of(codes_of(slot_ref[...], rank_ref[...], cap, pieces), 0, size)
    same = (iota((size, size), 0) == iota((size, size), 1)).astype(F32).astype(BF16)
    one_hot_ref[...] = dot_first(one_hot, same).astype(BF16)


def base_kernel(
    core_ref, hidden_ref, weight_hbm, first_ref, second_ref, mine_ref, other_ref, weight_ref, sems
):
    slots, depth = weight_ref.shape[:2]
    blocks = hidden_ref.shape[1] // depth

    def copy(k):
        part = weight_hbm.at[pl.ds(k * depth, depth), :]
        return pltpu.make_async_copy(part, weight_ref.at[k % slots], sems.at[k % slots])

    for k in range(slots):
        copy(k).start()
    rows, columns = mine_ref.shape
    total = jnp.zeros((rows, 2 * columns), F32)
    for k in range(blocks):
        copy(k).wait()
        total = total + dot(hidden_ref[:, k * depth : (k + 1) * depth], weight_ref[k % slots])
        if k + slots < blocks:
            copy(k + slots).start()
    first, second = total[:, :columns], total[:, columns:]
    mine_ref[...] = jnp.where(core_ref[0] == 0, first, second)
    other_ref[...] = jnp.where(core_ref[0] == 0, second, first)


def cache_kernel(query_ref, key_ref, value_ref, length_ref, _, acc_ref, max_ref, sum_ref):
    rows, groups, positions, head = key_ref.shape
    per_group = query_ref.shape[1] // (groups * head)
    tile = 16
    wide, deep = tile * positions, tile * per_group
    scale = head ** (-0.5)
    row_of = iota((deep, wide), 0) % tile
    own_row = row_of == iota((deep, wide), 1) // positions
    position = iota((deep, wide), 1) % positions
    lane = iota((tile, head), 1)
    for first in range(0, rows, tile):
        at = slice(first, first + tile)
        length = jnp.concatenate([length_ref[at, :]] * per_group, axis=0)
        valid = own_row & (position < length)
        tops = jnp.zeros((tile, head), F32)
        sums = jnp.zeros((tile, head), F32)
        for g in range(groups):
            query = jnp.concatenate(
                [query_ref[at, h * head : (h + 1) * head] for h in range(g * per_group, (g + 1) * per_group)],
                axis=0,
            )
            key = key_ref[at, g].reshape(wide, head)
            value = value_ref[at, g].reshape(wide, head)
            scores = lax.dot_general(query, key, (((1,), (1,)), ((), ())), preferred_element_type=F32)
            scores = jnp.where(valid, scores * scale, -jnp.inf)
            top = jnp.max(scores, axis=1, keepdims=True)
            weight = jnp.exp(scores - top)
            total = jnp.sum(weight, axis=1, keepdims=True)
            mixed = dot(weight.astype(BF16), value)
            for i in range(per_group):
                h = g * per_group + i
                part = slice(i * tile, (i + 1) * tile)
                acc_ref[at, h * head : (h + 1) * head] = mixed[part]
                tops = jnp.where(lane == h, top[part], tops)
                sums = jnp.where(lane == h, total[part], sums)
        max_ref[at, :] = tops
        sum_ref[at, :] = sums


def combine_kernel(
    delta_ref, one_hot_ref, base_ref, query_ref, max_ref, sum_ref, acc_ref, token_ref, out_ref
):
    rows = base_ref.shape[0]
    head = 128
    groups = base_ref.shape[1] // (2 * head)
    delta = dot(one_hot_ref[...], delta_ref[...])
    heads = query_ref.shape[1] // head
    per_group = heads // groups
    scale = head ** (-0.5)
    lane = iota((rows, head), 1)
    own = jnp.zeros((rows, head), F32)
    values = []
    for g in range(groups):
        made = []
        for c in range(2):
            at = (g * 2 + c) * head
            piece = c * groups + g
            made.append((base_ref[:, at : at + head] + delta[piece * rows : (piece + 1) * rows]).astype(BF16))
            token_ref[:, at : at + head] = made[-1]
        key = made[0].astype(F32)
        values.append(made[1].astype(F32))
        for h in range(g * per_group, (g + 1) * per_group):
            query = query_ref[:, h * head : (h + 1) * head].astype(F32)
            own = jnp.where(lane == h, jnp.sum(query * key, axis=1, keepdims=True), own)
    own = own[:, :heads] * scale
    cache_max = max_ref[:, :heads]
    highest = jnp.maximum(own, cache_max)
    cache_factor = jnp.exp(cache_max - highest)
    own_factor = jnp.exp(own - highest)
    inverse = 1.0 / (sum_ref[:, :heads] * cache_factor + own_factor)
    cache_factor = cache_factor * inverse
    own_factor = own_factor * inverse
    for h in range(heads):
        lanes = slice(h * head, (h + 1) * head)
        out = acc_ref[:, lanes] * cache_factor[:, h : h + 1]
        out = out + values[h // per_group] * own_factor[:, h : h + 1]
        out_ref[:, lanes] = out.astype(BF16)


VMEM = pl.BlockSpec(memory_space=pltpu.VMEM)
SMEM = pl.BlockSpec(memory_space=pltpu.SMEM)
HBM = pl.BlockSpec(memory_space=pltpu.HBM)
ANY = pl.BlockSpec(memory_space=pl.ANY)
NO_COST = pl.CostEstimate(flops=0, bytes_accessed=0, transcendentals=0)


def call(kernel, outs, specs, scratch=(), cost=NO_COST):
    return pl.pallas_call(
        kernel,
        out_shape=outs,
        in_specs=specs,
        out_specs=[VMEM] * len(outs),
        scratch_shapes=scratch,
        compiler_params=pltpu.CompilerParams(vmem_limit_bytes=VMEM_LIMIT),
        cost_estimate=cost,
    )


def shards(
    hidden,
    queries,
    key_value_weight,
    adapter_down_weight,
    adapter_up_weight,
    stored_cache_keys,
    stored_cache_values,
    row_adapter_index,
    stored_cache_lengths,
    adapter_slot_table,
):
    n = lax.axis_size("pool")
    rows, width = hidden.shape
    cap = -(-2 * rows // n)
    pieces = split_count(cap)
    groups = stored_cache_keys.shape[1]
    head = stored_cache_keys.shape[3]
    columns = key_value_weight.shape[1] // 2
    out_pieces = 2 * groups
    rank2 = adapter_down_weight.shape[2]

    swap = functools.partial(lax.ppermute, axis_name="tp", perm=[(0, 1), (1, 0)])

    me = lax.axis_index("pool").reshape(1)
    slot, rank, *packed = call(
        functools.partial(pack_kernel, n, cap, pieces),
        [jax.ShapeDtypeStruct((1, rows), I32)] * 2
        + [jax.ShapeDtypeStruct((pieces * cap, width // pieces), BF16)] * n,
        [SMEM, VMEM, VMEM, VMEM],
    )(me, row_adapter_index.reshape(1, rows), adapter_slot_table.reshape(1, n), hidden)
    half = n // 2
    order = [0, 1, 2, *range(half, n), *range(3, half)]
    arrived = {0: packed[0]}
    for s in order[1:]:
        arrived[s] = lax.ppermute(packed[s], "pool", [(i, i ^ s) for i in range(n)])

    slots, depth = 4, 512
    base_mine, base_other = call(
        base_kernel,
        [jax.ShapeDtypeStruct((rows, columns), F32)] * 2,
        [SMEM, VMEM, ANY, ANY, ANY],
        [
            pltpu.VMEM((slots, depth, 2 * columns), BF16),
            pltpu.SemaphoreType.DMA((slots,)),
        ],
        pl.CostEstimate(
            flops=4 * rows * width * columns, bytes_accessed=16 * width * columns, transcendentals=0
        ),
    )(lax.axis_index("tp").reshape(1), hidden, key_value_weight, arrived[1], arrived[2])

    size = n * out_pieces * cap
    shrink_table, expand_table = call(
        functools.partial(tables_kernel, n, cap, pieces, out_pieces),
        [
            jax.ShapeDtypeStruct((half * cap, half * pieces * cap), BF16),
            jax.ShapeDtypeStruct((size, size), BF16),
        ],
        [SMEM, ANY],
    )(me, base_mine)
    (near_sum,) = call(
        functools.partial(shrink_near_kernel, cap, pieces),
        [jax.ShapeDtypeStruct((half * cap, rank2), F32)],
        [VMEM] * (half + 2),
    )(*[arrived[s] for s in range(half)], adapter_down_weight, shrink_table)
    (sums,) = call(
        functools.partial(shrink_far_kernel, cap, pieces),
        [jax.ShapeDtypeStruct((n * cap + rows * columns // rank2, rank2), F32)],
        [VMEM] * (half + 4),
    )(*[arrived[s] for s in range(half, n)], adapter_down_weight, shrink_table, near_sum, base_other)
    other_sums = swap(sums)
    (terms,) = call(
        functools.partial(expand_kernel, n, cap),
        [jax.ShapeDtypeStruct((size, head), BF16)],
        [VMEM] * 4,
    )(sums, other_sums, adapter_up_weight, expand_table)
    base, one_hot = call(
        functools.partial(prepare_kernel, n, cap),
        [
            jax.ShapeDtypeStruct((rows, columns), F32),
            jax.ShapeDtypeStruct((out_pieces * rows, size), BF16),
        ],
        [VMEM] * 4 + [ANY],
    )(slot, rank, base_mine, other_sums, terms)
    deltas = lax.all_to_all(terms, "pool", split_axis=0, concat_axis=0, tiled=True)
    attended, cache_max, cache_sum = call(
        cache_kernel,
        [jax.ShapeDtypeStruct(queries.shape, F32)] + [jax.ShapeDtypeStruct((rows, head), F32)] * 2,
        [VMEM] * 4 + [ANY],
    )(queries, stored_cache_keys, stored_cache_values, stored_cache_lengths.reshape(rows, 1), terms)
    token, out = call(
        combine_kernel,
        [jax.ShapeDtypeStruct((rows, columns), BF16), jax.ShapeDtypeStruct(queries.shape, BF16)],
        [VMEM] * 7,
    )(deltas, one_hot, base, queries, cache_max, cache_sum, attended)
    return token, out


def solution(mesh):
    in_specs = (
        P(("grp", "pool"), "tp"),
        P(("grp", "pool"), "tp"),
        P("tp", None),
        P("pool", "tp", None),
        P("pool", None, None, "tp"),
        P(("grp", "pool"), "tp", None, None),
        P(("grp", "pool"), "tp", None, None),
        P(("grp", "pool"), None),
        P(("grp", "pool")),
        P(),
    )
    out_specs = (P(("grp", "pool"), "tp"), P(("grp", "pool"), "tp"))
    return jax.shard_map(shards, mesh=mesh, in_specs=in_specs, out_specs=out_specs, check_vma=False)
```

```python
import functools

import jax
import jax.numpy as jnp
from jax import lax
from jax.experimental import pallas as pl
from jax.experimental.pallas import tpu as pltpu
from jax.sharding import PartitionSpec as P

BF16 = jnp.bfloat16
F32 = jnp.float32
I32 = jnp.int32
VMEM_LIMIT = 20 * 1024 * 1024


def iota(shape, dim):
    return lax.broadcasted_iota(I32, shape, dim)


def split_count(cap):
    pieces = 4
    while cap * pieces % 16:
        pieces *= 2
    return pieces


def dot(a, b):
    return jnp.dot(a, b, preferred_element_type=F32)


def dot_first(a, b):
    return lax.dot_general(a, b, (((0,), (0,)), ((), ())), preferred_element_type=F32)


def select_sum(one_hot, x):
    high = x.astype(BF16)
    low = (x - high.astype(F32)).astype(BF16)
    both = dot(one_hot, jnp.concatenate([high, low], axis=1))
    return both[:, : x.shape[1]] + both[:, x.shape[1] :]


def codes_of(place, rank, cap, pieces):
    code = place * (pieces * cap) + rank
    return jnp.concatenate([code + piece * cap for piece in range(pieces)], axis=1)


def one_hot_of(codes, first, count):
    return ((iota((count, codes.shape[1]), 0) + first) == codes).astype(F32).astype(BF16)


def stack_pieces(hidden, pieces):
    width = hidden.shape[1] // pieces
    return jnp.concatenate(
        [hidden[:, piece * width : (piece + 1) * width] for piece in range(pieces)], axis=0
    )


def place_of(slot, me, half):
    apart = lax.bitwise_xor(slot, me)
    return jnp.where(apart < half, lax.bitwise_and(slot, half - 1), apart)


def pack_kernel(n, cap, pieces, me_ref, idx_ref, table_ref, hidden_ref, slot_ref, rank_ref, near_ref, *far_refs):
    rows = hidden_ref.shape[0]
    named = (iota((n, rows), 0) == idx_ref[...]).astype(F32).astype(BF16)
    table = jnp.broadcast_to(table_ref[...].astype(F32).astype(BF16), (16, n))
    slot = dot(table, named)[0:1, :].astype(I32)
    member = (iota((n, rows), 0) == slot).astype(F32)
    before = (iota((rows, rows), 0) < iota((rows, rows), 1)).astype(F32).astype(BF16)
    count = dot(member.astype(BF16), before)
    rank = jnp.sum(member * count, axis=0, keepdims=True).astype(I32)
    slot_ref[...] = slot
    rank_ref[...] = rank
    per = pieces * cap
    half = n // 2
    place = place_of(slot, me_ref[0], half)
    one_hot = one_hot_of(codes_of(place, rank, cap, pieces), 0, n * per)
    packed = dot(one_hot, stack_pieces(hidden_ref[...], pieces)).astype(BF16)
    near_ref[...] = packed[: half * per]
    for s, far_ref in enumerate(far_refs, half):
        far_ref[...] = packed[s * per : (s + 1) * per]


def tables_kernel(n, cap, pieces, out_pieces, me_ref, _, shrink_ref, expand_ref):
    per = pieces * cap
    out_row, in_row = iota(shrink_ref.shape, 0), iota(shrink_ref.shape, 1)
    same = (out_row // cap == in_row // per) & (out_row % cap == in_row % cap)
    shrink_ref[...] = same.astype(F32).astype(BF16)
    per = out_pieces * cap
    out_row, in_row = iota(expand_ref.shape, 0), iota(expand_ref.shape, 1)
    place = place_of(out_row // per, me_ref[0], n // 2)
    source = (out_row // cap % out_pieces) * (n * cap) + place * cap + out_row % cap
    expand_ref[...] = (source == in_row).astype(F32).astype(BF16)


def shrink(cap, pieces, received_refs, down_ref, table_ref):
    width = received_refs[0].shape[1]
    rank2 = down_ref.shape[2]
    received = jnp.concatenate([ref[...] for ref in received_refs], axis=0)
    size = received.shape[0]
    total = jnp.zeros((size, rank2), F32)
    piece_of = (iota((size, rank2), 0) // cap) % pieces
    for piece in range(pieces):
        part = dot(received, down_ref[0, piece * width : (piece + 1) * width, :])
        total = total + jnp.where(piece_of == piece, part, 0.0)
    return select_sum(table_ref[...], total)


def shrink_far_kernel(cap, pieces, *refs):
    refs[-1][...] = shrink(cap, pieces, refs[:-3], *refs[-3:-1])


def shrink_near_kernel(cap, pieces, near_ref, down_ref, table_ref, far_ref, base_ref, out_ref):
    half = far_ref.shape[0]
    out_ref[:half, :] = shrink(cap, pieces, [near_ref], down_ref, table_ref)
    out_ref[half : 2 * half, :] = far_ref[...]
    rows = base_ref.shape[0]
    lanes = out_ref.shape[1]
    for i in range(base_ref.shape[1] // lanes):
        first = 2 * half + i * rows
        out_ref[first : first + rows, :] = base_ref[:, i * lanes : (i + 1) * lanes]


def expand_kernel(n, cap, mine_ref, other_ref, up_ref, table_ref, out_ref):
    rank = up_ref.shape[2]
    head = 128
    blocks = up_ref.shape[3] // head
    reduced = (mine_ref[: n * cap, :] + other_ref[: n * cap, :]).astype(BF16)
    terms = []
    for c in range(2):
        kept = reduced[:, c * rank : (c + 1) * rank]
        wide = dot(kept, up_ref[0, c]).astype(BF16)
        terms += [wide[:, g * head : (g + 1) * head] for g in range(blocks)]
    out_ref[...] = dot(table_ref[...], jnp.concatenate(terms, axis=0)).astype(BF16)


def prepare_kernel(n, cap, slot_ref, rank_ref, mine_ref, other_ref, _, base_ref, one_hot_ref):
    pieces = one_hot_ref.shape[0] // slot_ref.shape[1]
    size = one_hot_ref.shape[1]
    rows = mine_ref.shape[0]
    width = other_ref.shape[1]
    for i in range(mine_ref.shape[1] // width):
        lanes, first = slice(i * width, (i + 1) * width), n * cap + i * rows
        base_ref[:, lanes] = mine_ref[:, lanes] + other_ref[first : first + rows, :]
    one_hot = one_hot_of(codes_of(slot_ref[...], rank_ref[...], cap, pieces), 0, size)
    same = (iota((size, size), 0) == iota((size, size), 1)).astype(F32).astype(BF16)
    one_hot_ref[...] = dot_first(one_hot, same).astype(BF16)


def base_kernel(
    core_ref, hidden_ref, weight_hbm, mine_ref, other_ref, weight_ref, sems
):
    slots, depth = weight_ref.shape[:2]
    blocks = hidden_ref.shape[1] // depth

    def copy(k):
        part = weight_hbm.at[pl.ds(k * depth, depth), :]
        return pltpu.make_async_copy(part, weight_ref.at[k % slots], sems.at[k % slots])

    for k in range(slots):
        copy(k).start()
    rows, columns = mine_ref.shape
    total = jnp.zeros((rows, 2 * columns), F32)
    for k in range(blocks):
        copy(k).wait()
        total = total + dot(hidden_ref[:, k * depth : (k + 1) * depth], weight_ref[k % slots])
        if k + slots < blocks:
            copy(k + slots).start()
    first, second = total[:, :columns], total[:, columns:]
    mine_ref[...] = jnp.where(core_ref[0] == 0, first, second)
    other_ref[...] = jnp.where(core_ref[0] == 0, second, first)


def cache_kernel(query_ref, key_ref, value_ref, length_ref, _, acc_ref, max_ref, sum_ref):
    rows, groups, positions, head = key_ref.shape
    per_group = query_ref.shape[1] // (groups * head)
    tile = 16
    wide, deep = tile * positions, tile * per_group
    scale = head ** (-0.5)
    row_of = iota((deep, wide), 0) % tile
    own_row = row_of == iota((deep, wide), 1) // positions
    position = iota((deep, wide), 1) % positions
    lane = iota((tile, head), 1)
    for first in range(0, rows, tile):
        at = slice(first, first + tile)
        length = jnp.concatenate([length_ref[at, :]] * per_group, axis=0)
        valid = own_row & (position < length)
        tops = jnp.zeros((tile, head), F32)
        sums = jnp.zeros((tile, head), F32)
        for g in range(groups):
            query = jnp.concatenate(
                [query_ref[at, h * head : (h + 1) * head] for h in range(g * per_group, (g + 1) * per_group)],
                axis=0,
            )
            key = key_ref[at, g].reshape(wide, head)
            value = value_ref[at, g].reshape(wide, head)
            scores = lax.dot_general(query, key, (((1,), (1,)), ((), ())), preferred_element_type=F32)
            scores = jnp.where(valid, scores * scale, -jnp.inf)
            top = jnp.max(scores, axis=1, keepdims=True)
            weight = jnp.exp(scores - top)
            total = jnp.sum(weight, axis=1, keepdims=True)
            mixed = dot(weight.astype(BF16), value)
            for i in range(per_group):
                h = g * per_group + i
                part = slice(i * tile, (i + 1) * tile)
                acc_ref[at, h * head : (h + 1) * head] = mixed[part]
                tops = jnp.where(lane == h, top[part], tops)
                sums = jnp.where(lane == h, total[part], sums)
        max_ref[at, :] = tops
        sum_ref[at, :] = sums


def combine_kernel(
    delta_ref, one_hot_ref, base_ref, query_ref, max_ref, sum_ref, acc_ref, token_ref, out_ref
):
    rows = base_ref.shape[0]
    head = 128
    groups = base_ref.shape[1] // (2 * head)
    delta = dot(one_hot_ref[...], delta_ref[...])
    heads = query_ref.shape[1] // head
    per_group = heads // groups
    scale = head ** (-0.5)
    lane = iota((rows, head), 1)
    own = jnp.zeros((rows, head), F32)
    values = []
    for g in range(groups):
        made = []
        for c in range(2):
            at = (g * 2 + c) * head
            piece = c * groups + g
            made.append((base_ref[:, at : at + head] + delta[piece * rows : (piece + 1) * rows]).astype(BF16))
            token_ref[:, at : at + head] = made[-1]
        key = made[0].astype(F32)
        values.append(made[1].astype(F32))
        for h in range(g * per_group, (g + 1) * per_group):
            query = query_ref[:, h * head : (h + 1) * head].astype(F32)
            own = jnp.where(lane == h, jnp.sum(query * key, axis=1, keepdims=True), own)
    own = own[:, :heads] * scale
    cache_max = max_ref[:, :heads]
    highest = jnp.maximum(own, cache_max)
    cache_factor = jnp.exp(cache_max - highest)
    own_factor = jnp.exp(own - highest)
    inverse = 1.0 / (sum_ref[:, :heads] * cache_factor + own_factor)
    cache_factor = cache_factor * inverse
    own_factor = own_factor * inverse
    for h in range(heads):
        lanes = slice(h * head, (h + 1) * head)
        out = acc_ref[:, lanes] * cache_factor[:, h : h + 1]
        out = out + values[h // per_group] * own_factor[:, h : h + 1]
        out_ref[:, lanes] = out.astype(BF16)


VMEM = pl.BlockSpec(memory_space=pltpu.VMEM)
SMEM = pl.BlockSpec(memory_space=pltpu.SMEM)
HBM = pl.BlockSpec(memory_space=pltpu.HBM)
ANY = pl.BlockSpec(memory_space=pl.ANY)
NO_COST = pl.CostEstimate(flops=0, bytes_accessed=0, transcendentals=0)


def call(kernel, outs, specs, scratch=(), cost=NO_COST):
    return pl.pallas_call(
        kernel,
        out_shape=outs,
        in_specs=specs,
        out_specs=[VMEM] * len(outs),
        scratch_shapes=scratch,
        compiler_params=pltpu.CompilerParams(vmem_limit_bytes=VMEM_LIMIT),
        cost_estimate=cost,
    )


def shards(
    hidden,
    queries,
    key_value_weight,
    adapter_down_weight,
    adapter_up_weight,
    stored_cache_keys,
    stored_cache_values,
    row_adapter_index,
    stored_cache_lengths,
    adapter_slot_table,
):
    n = lax.axis_size("pool")
    rows, width = hidden.shape
    cap = -(-2 * rows // n)
    pieces = split_count(cap)
    groups = stored_cache_keys.shape[1]
    head = stored_cache_keys.shape[3]
    columns = key_value_weight.shape[1] // 2
    out_pieces = 2 * groups
    rank2 = adapter_down_weight.shape[2]

    swap = functools.partial(lax.ppermute, axis_name="tp", perm=[(0, 1), (1, 0)])

    me = lax.axis_index("pool").reshape(1)
    half = n // 2
    per = pieces * cap
    slot, rank, near, *far = call(
        functools.partial(pack_kernel, n, cap, pieces),
        [jax.ShapeDtypeStruct((1, rows), I32)] * 2
        + [jax.ShapeDtypeStruct((half * per, width // pieces), BF16)]
        + [jax.ShapeDtypeStruct((per, width // pieces), BF16)] * half,
        [SMEM, VMEM, VMEM, VMEM],
    )(me, row_adapter_index.reshape(1, rows), adapter_slot_table.reshape(1, n), hidden)
    far = [
        lax.ppermute(chunk, "pool", [(i, i ^ s) for i in range(n)]) for s, chunk in enumerate(far, half)
    ]
    near = lax.all_to_all(
        near,
        "pool",
        split_axis=0,
        concat_axis=0,
        tiled=True,
        axis_index_groups=[list(range(half)), list(range(half, n))],
    )

    slots, depth = 4, 512
    base_mine, base_other = call(
        base_kernel,
        [jax.ShapeDtypeStruct((rows, columns), F32)] * 2,
        [SMEM, VMEM, ANY],
        [
            pltpu.VMEM((slots, depth, 2 * columns), BF16),
            pltpu.SemaphoreType.DMA((slots,)),
        ],
        pl.CostEstimate(
            flops=4 * rows * width * columns, bytes_accessed=128 * width * columns, transcendentals=0
        ),
    )(lax.axis_index("tp").reshape(1), hidden, key_value_weight)

    size = n * out_pieces * cap
    shrink_table, expand_table = call(
        functools.partial(tables_kernel, n, cap, pieces, out_pieces),
        [
            jax.ShapeDtypeStruct((half * cap, half * pieces * cap), BF16),
            jax.ShapeDtypeStruct((size, size), BF16),
        ],
        [SMEM, ANY],
    )(me, base_mine)
    (far_sum,) = call(
        functools.partial(shrink_far_kernel, cap, pieces),
        [jax.ShapeDtypeStruct((half * cap, rank2), F32)],
        [VMEM] * (half + 2),
    )(*far, adapter_down_weight, shrink_table)
    (sums,) = call(
        functools.partial(shrink_near_kernel, cap, pieces),
        [jax.ShapeDtypeStruct((n * cap + rows * columns // rank2, rank2), F32)],
        [VMEM] * 5,
    )(near, adapter_down_weight, shrink_table, far_sum, base_other)
    other_sums = swap(sums)
    (terms,) = call(
        functools.partial(expand_kernel, n, cap),
        [jax.ShapeDtypeStruct((size, head), BF16)],
        [VMEM] * 4,
    )(sums, other_sums, adapter_up_weight, expand_table)
    base, one_hot = call(
        functools.partial(prepare_kernel, n, cap),
        [
            jax.ShapeDtypeStruct((rows, columns), F32),
            jax.ShapeDtypeStruct((out_pieces * rows, size), BF16),
        ],
        [VMEM] * 4 + [ANY],
    )(slot, rank, base_mine, other_sums, terms)
    deltas = lax.all_to_all(terms, "pool", split_axis=0, concat_axis=0, tiled=True)
    attended, cache_max, cache_sum = call(
        cache_kernel,
        [jax.ShapeDtypeStruct(queries.shape, F32)] + [jax.ShapeDtypeStruct((rows, head), F32)] * 2,
        [VMEM] * 4 + [ANY],
    )(queries, stored_cache_keys, stored_cache_values, stored_cache_lengths.reshape(rows, 1), terms)
    token, out = call(
        combine_kernel,
        [jax.ShapeDtypeStruct((rows, columns), BF16), jax.ShapeDtypeStruct(queries.shape, BF16)],
        [VMEM] * 7,
    )(deltas, one_hot, base, queries, cache_max, cache_sum, attended)
    return token, out


def solution(mesh):
    in_specs = (
        P(("grp", "pool"), "tp"),
        P(("grp", "pool"), "tp"),
        P("tp", None),
        P("pool", "tp", None),
        P("pool", None, None, "tp"),
        P(("grp", "pool"), "tp", None, None),
        P(("grp", "pool"), "tp", None, None),
        P(("grp", "pool"), None),
        P(("grp", "pool")),
        P(),
    )
    out_specs = (P(("grp", "pool"), "tp"), P(("grp", "pool"), "tp"))
    return jax.shard_map(shards, mesh=mesh, in_specs=in_specs, out_specs=out_specs, check_vma=False)
```

```python
import functools

import jax
import jax.numpy as jnp
from jax import lax
from jax.experimental import pallas as pl
from jax.experimental.pallas import tpu as pltpu
from jax.sharding import PartitionSpec as P

BF16 = jnp.bfloat16
F32 = jnp.float32
I32 = jnp.int32
VMEM_LIMIT = 20 * 1024 * 1024


def iota(shape, dim):
    return lax.broadcasted_iota(I32, shape, dim)


def split_count(cap):
    pieces = 4
    while cap * pieces % 16:
        pieces *= 2
    return pieces


def dot(a, b):
    return jnp.dot(a, b, preferred_element_type=F32)


def dot_first(a, b):
    return lax.dot_general(a, b, (((0,), (0,)), ((), ())), preferred_element_type=F32)


def select_sum(one_hot, x):
    high = x.astype(BF16)
    low = (x - high.astype(F32)).astype(BF16)
    both = dot(one_hot, jnp.concatenate([high, low], axis=1))
    return both[:, : x.shape[1]] + both[:, x.shape[1] :]


def codes_of(place, rank, cap, pieces):
    code = place * (pieces * cap) + rank
    return jnp.concatenate([code + piece * cap for piece in range(pieces)], axis=1)


def one_hot_of(codes, first, count):
    return ((iota((count, codes.shape[1]), 0) + first) == codes).astype(F32).astype(BF16)


def stack_pieces(hidden, pieces):
    width = hidden.shape[1] // pieces
    return jnp.concatenate(
        [hidden[:, piece * width : (piece + 1) * width] for piece in range(pieces)], axis=0
    )


def pack_kernel(n, cap, pieces, me_ref, idx_ref, table_ref, hidden_ref, slot_ref, rank_ref, *out_refs):
    rows = hidden_ref.shape[0]
    named = (iota((n, rows), 0) == idx_ref[...]).astype(F32).astype(BF16)
    table = jnp.broadcast_to(table_ref[...].astype(F32).astype(BF16), (16, n))
    slot = dot(table, named)[0:1, :].astype(I32)
    member = (iota((n, rows), 0) == slot).astype(F32)
    before = (iota((rows, rows), 0) < iota((rows, rows), 1)).astype(F32).astype(BF16)
    count = dot(member.astype(BF16), before)
    rank = jnp.sum(member * count, axis=0, keepdims=True).astype(I32)
    slot_ref[...] = slot
    rank_ref[...] = rank
    per = pieces * cap
    apart = lax.bitwise_xor(slot, me_ref[0])
    one_hot = one_hot_of(codes_of(apart, rank, cap, pieces), 0, n * per)
    packed = dot(one_hot, stack_pieces(hidden_ref[...], pieces)).astype(BF16)
    for s, out_ref in enumerate(out_refs):
        out_ref[...] = packed[s * per : (s + 1) * per]


def tables_kernel(n, cap, pieces, out_pieces, me_ref, _, shrink_ref, expand_ref):
    per = pieces * cap
    out_row, in_row = iota(shrink_ref.shape, 0), iota(shrink_ref.shape, 1)
    same = (out_row // cap == in_row // per) & (out_row % cap == in_row % cap)
    shrink_ref[...] = same.astype(F32).astype(BF16)
    per = out_pieces * cap
    out_row, in_row = iota(expand_ref.shape, 0), iota(expand_ref.shape, 1)
    apart = lax.bitwise_xor(out_row // per, me_ref[0])
    source = (out_row // cap % out_pieces) * (n * cap) + apart * cap + out_row % cap
    expand_ref[...] = (source == in_row).astype(F32).astype(BF16)


def shrink(cap, pieces, received_refs, down_ref, table_ref):
    width = received_refs[0].shape[1]
    rank2 = down_ref.shape[2]
    received = jnp.concatenate([ref[...] for ref in received_refs], axis=0)
    size = received.shape[0]
    total = jnp.zeros((size, rank2), F32)
    piece_of = (iota((size, rank2), 0) // cap) % pieces
    for piece in range(pieces):
        part = dot(received, down_ref[0, piece * width : (piece + 1) * width, :])
        total = total + jnp.where(piece_of == piece, part, 0.0)
    return select_sum(table_ref[...], total)


def shrink_near_kernel(cap, pieces, *refs):
    refs[-1][...] = shrink(cap, pieces, refs[:-3], *refs[-3:-1])


def shrink_far_kernel(cap, pieces, *refs):
    near_ref, out_ref = refs[-2:]
    half = near_ref.shape[0]
    out_ref[:half, :] = near_ref[...]
    out_ref[half:, :] = shrink(cap, pieces, refs[:-4], *refs[-4:-2])


def expand_kernel(mine_ref, other_ref, up_ref, table_ref, out_ref):
    rank = up_ref.shape[2]
    head = 128
    blocks = up_ref.shape[3] // head
    reduced = (mine_ref[...] + other_ref[...]).astype(BF16)
    terms = []
    for c in range(2):
        kept = reduced[:, c * rank : (c + 1) * rank]
        wide = dot(kept, up_ref[0, c]).astype(BF16)
        terms += [wide[:, g * head : (g + 1) * head] for g in range(blocks)]
    out_ref[...] = dot(table_ref[...], jnp.concatenate(terms, axis=0)).astype(BF16)


def prepare_kernel(cap, slot_ref, rank_ref, mine_ref, other_ref, base_ref, one_hot_ref):
    pieces = one_hot_ref.shape[0] // slot_ref.shape[1]
    size = one_hot_ref.shape[1]
    base_ref[...] = mine_ref[...] + other_ref[...]
    one_hot = one_hot_of(codes_of(slot_ref[...], rank_ref[...], cap, pieces), 0, size)
    same = (iota((size, size), 0) == iota((size, size), 1)).astype(F32).astype(BF16)
    one_hot_ref[...] = dot_first(one_hot, same).astype(BF16)


def combine_kernel(
    delta_ref,
    one_hot_ref,
    base_ref,
    query_ref,
    max_ref,
    sum_ref,
    acc_ref,
    token_hbm,
    out_hbm,
    token_ref,
    out_ref,
    sems,
):
    rows = base_ref.shape[0]
    head = 128
    groups = base_ref.shape[1] // (2 * head)
    delta = dot(one_hot_ref[...], delta_ref[...])
    heads = query_ref.shape[1] // head
    per_group = heads // groups
    scale = head ** (-0.5)
    lane = iota((rows, head), 1)
    copies = []
    for g in range(groups):
        made = []
        for c in range(2):
            at = (g * 2 + c) * head
            piece = c * groups + g
            made.append((base_ref[:, at : at + head] + delta[piece * rows : (piece + 1) * rows]).astype(BF16))
            token_ref[:, at : at + head] = made[-1]
        key, value = made[0].astype(F32), made[1].astype(F32)
        own = jnp.zeros((rows, head), F32)
        for h in range(g * per_group, (g + 1) * per_group):
            query = query_ref[:, h * head : (h + 1) * head].astype(F32)
            own = jnp.where(lane == h, jnp.sum(query * key, axis=1, keepdims=True), own)
        own = own * scale
        cache_max = max_ref[...]
        highest = jnp.maximum(own, cache_max)
        cache_factor = jnp.exp(cache_max - highest)
        own_factor = jnp.exp(own - highest)
        inverse = 1.0 / (sum_ref[...] * cache_factor + own_factor)
        cache_factor = cache_factor * inverse
        own_factor = own_factor * inverse
        for h in range(g * per_group, (g + 1) * per_group):
            lanes = slice(h * head, (h + 1) * head)
            out = acc_ref[:, lanes] * cache_factor[:, h : h + 1] + value * own_factor[:, h : h + 1]
            out_ref[:, lanes] = out.astype(BF16)
        for i, (source, target, width) in enumerate(
            [(token_ref, token_hbm, 2 * head), (out_ref, out_hbm, per_group * head)]
        ):
            part = pl.ds(g * width, width)
            copies.append(pltpu.make_async_copy(source.at[:, part], target.at[:, part], sems.at[2 * g + i]))
            copies[-1].start()
    for copy in copies:
        copy.wait()


def base_kernel(
    core_ref, hidden_ref, weight_hbm, first_ref, second_ref, mine_ref, other_ref, weight_ref, sems
):
    slots, depth = weight_ref.shape[:2]
    blocks = hidden_ref.shape[1] // depth

    def copy(k):
        part = weight_hbm.at[pl.ds(k * depth, depth), :]
        return pltpu.make_async_copy(part, weight_ref.at[k % slots], sems.at[k % slots])

    for k in range(slots):
        copy(k).start()
    rows, columns = mine_ref.shape
    total = jnp.zeros((rows, 2 * columns), F32)
    for k in range(blocks):
        copy(k).wait()
        total = total + dot(hidden_ref[:, k * depth : (k + 1) * depth], weight_ref[k % slots])
        if k + slots < blocks:
            copy(k + slots).start()
    first, second = total[:, :columns], total[:, columns:]
    mine_ref[...] = jnp.where(core_ref[0] == 0, first, second)
    other_ref[...] = jnp.where(core_ref[0] == 0, second, first)


def cache_kernel(
    query_ref, key_ref, value_ref, length_ref, base_ref, _, acc_ref, max_ref, sum_ref, handed_ref
):
    handed_ref[...] = base_ref[...]
    rows, groups, positions, head = key_ref.shape
    per_group = query_ref.shape[1] // (groups * head)
    tile = 16
    wide, deep = tile * positions, tile * per_group
    scale = head ** (-0.5)
    row_of = iota((deep, wide), 0) % tile
    own_row = row_of == iota((deep, wide), 1) // positions
    position = iota((deep, wide), 1) % positions
    lane = iota((tile, head), 1)
    for first in range(0, rows, tile):
        at = slice(first, first + tile)
        length = jnp.concatenate([length_ref[at, :]] * per_group, axis=0)
        valid = own_row & (position < length)
        tops = jnp.zeros((tile, head), F32)
        sums = jnp.zeros((tile, head), F32)
        for g in range(groups):
            query = jnp.concatenate(
                [query_ref[at, h * head : (h + 1) * head] for h in range(g * per_group, (g + 1) * per_group)],
                axis=0,
            )
            key = key_ref[at, g].reshape(wide, head)
            value = value_ref[at, g].reshape(wide, head)
            scores = lax.dot_general(query, key, (((1,), (1,)), ((), ())), preferred_element_type=F32)
            scores = jnp.where(valid, scores * scale, -jnp.inf)
            top = jnp.max(scores, axis=1, keepdims=True)
            weight = jnp.exp(scores - top)
            total = jnp.sum(weight, axis=1, keepdims=True)
            mixed = dot(weight.astype(BF16), value)
            for i in range(per_group):
                h = g * per_group + i
                part = slice(i * tile, (i + 1) * tile)
                acc_ref[at, h * head : (h + 1) * head] = mixed[part]
                tops = jnp.where(lane == h, top[part], tops)
                sums = jnp.where(lane == h, total[part], sums)
        max_ref[at, :] = tops
        sum_ref[at, :] = sums


VMEM = pl.BlockSpec(memory_space=pltpu.VMEM)
SMEM = pl.BlockSpec(memory_space=pltpu.SMEM)
HBM = pl.BlockSpec(memory_space=pltpu.HBM)
ANY = pl.BlockSpec(memory_space=pl.ANY)
NO_COST = pl.CostEstimate(flops=0, bytes_accessed=0, transcendentals=0)


def call(kernel, outs, specs, scratch=(), cost=NO_COST):
    return pl.pallas_call(
        kernel,
        out_shape=outs,
        in_specs=specs,
        out_specs=[VMEM] * len(outs),
        scratch_shapes=scratch,
        compiler_params=pltpu.CompilerParams(vmem_limit_bytes=VMEM_LIMIT),
        cost_estimate=cost,
    )


def shards(
    hidden,
    queries,
    key_value_weight,
    adapter_down_weight,
    adapter_up_weight,
    stored_cache_keys,
    stored_cache_values,
    row_adapter_index,
    stored_cache_lengths,
    adapter_slot_table,
):
    n = lax.axis_size("pool")
    rows, width = hidden.shape
    cap = -(-2 * rows // n)
    pieces = split_count(cap)
    groups = stored_cache_keys.shape[1]
    head = stored_cache_keys.shape[3]
    columns = key_value_weight.shape[1] // 2
    out_pieces = 2 * groups
    rank2 = adapter_down_weight.shape[2]

    swap = functools.partial(lax.ppermute, axis_name="tp", perm=[(0, 1), (1, 0)])

    me = lax.axis_index("pool").reshape(1)
    slot, rank, *packed = call(
        functools.partial(pack_kernel, n, cap, pieces),
        [jax.ShapeDtypeStruct((1, rows), I32)] * 2
        + [jax.ShapeDtypeStruct((pieces * cap, width // pieces), BF16)] * n,
        [SMEM, VMEM, VMEM, VMEM],
    )(me, row_adapter_index.reshape(1, rows), adapter_slot_table.reshape(1, n), hidden)
    half = n // 2
    order = [0, 1, 2, *range(half, n), *range(3, half)]
    arrived = {0: packed[0]}
    for s in order[1:]:
        arrived[s] = lax.ppermute(packed[s], "pool", [(i, i ^ s) for i in range(n)])

    slots, depth = 4, 512
    base_mine, base_other = call(
        base_kernel,
        [jax.ShapeDtypeStruct((rows, columns), F32)] * 2,
        [SMEM, VMEM, ANY, ANY, ANY],
        [
            pltpu.VMEM((slots, depth, 2 * columns), BF16),
            pltpu.SemaphoreType.DMA((slots,)),
        ],
        pl.CostEstimate(
            flops=4 * rows * width * columns, bytes_accessed=16 * width * columns, transcendentals=0
        ),
    )(lax.axis_index("tp").reshape(1), hidden, key_value_weight, arrived[1], arrived[2])

    size = n * out_pieces * cap
    shrink_table, expand_table = call(
        functools.partial(tables_kernel, n, cap, pieces, out_pieces),
        [
            jax.ShapeDtypeStruct((half * cap, half * pieces * cap), BF16),
            jax.ShapeDtypeStruct((size, size), BF16),
        ],
        [SMEM, ANY],
    )(me, base_mine)
    (near_sum,) = call(
        functools.partial(shrink_near_kernel, cap, pieces),
        [jax.ShapeDtypeStruct((half * cap, rank2), F32)],
        [VMEM] * (half + 2),
    )(*[arrived[s] for s in range(half)], adapter_down_weight, shrink_table)
    (sums,) = call(
        functools.partial(shrink_far_kernel, cap, pieces),
        [jax.ShapeDtypeStruct((n * cap, rank2), F32)],
        [VMEM] * (half + 3),
    )(*[arrived[s] for s in range(half, n)], adapter_down_weight, shrink_table, near_sum)
    (terms,) = call(
        expand_kernel,
        [jax.ShapeDtypeStruct((size, head), BF16)],
        [VMEM] * 4,
    )(sums, swap(sums), adapter_up_weight, expand_table)
    deltas = lax.all_to_all(terms, "pool", split_axis=0, concat_axis=0, tiled=True)
    attended, cache_max, cache_sum, base_other = call(
        cache_kernel,
        [jax.ShapeDtypeStruct(queries.shape, F32)]
        + [jax.ShapeDtypeStruct((rows, head), F32)] * 2
        + [jax.ShapeDtypeStruct((rows, columns), F32)],
        [VMEM] * 5 + [ANY],
    )(
        queries,
        stored_cache_keys,
        stored_cache_values,
        stored_cache_lengths.reshape(rows, 1),
        base_other,
        terms,
    )
    base, one_hot = call(
        functools.partial(prepare_kernel, cap),
        [
            jax.ShapeDtypeStruct((rows, columns), F32),
            jax.ShapeDtypeStruct((out_pieces * rows, size), BF16),
        ],
        [VMEM] * 4,
    )(slot, rank, base_mine, swap(base_other))
    token, out = pl.pallas_call(
        combine_kernel,
        out_shape=[jax.ShapeDtypeStruct((rows, columns), BF16), jax.ShapeDtypeStruct(queries.shape, BF16)],
        in_specs=[VMEM] * 7,
        out_specs=[ANY] * 2,
        scratch_shapes=[
            pltpu.VMEM((rows, columns), BF16),
            pltpu.VMEM(queries.shape, BF16),
            pltpu.SemaphoreType.DMA((2 * groups,)),
        ],
        compiler_params=pltpu.CompilerParams(vmem_limit_bytes=VMEM_LIMIT),
        cost_estimate=NO_COST,
    )(deltas, one_hot, base, queries, cache_max, cache_sum, attended)
    return token, out


def solution(mesh):
    in_specs = (
        P(("grp", "pool"), "tp"),
        P(("grp", "pool"), "tp"),
        P("tp", None),
        P("pool", "tp", None),
        P("pool", None, None, "tp"),
        P(("grp", "pool"), "tp", None, None),
        P(("grp", "pool"), "tp", None, None),
        P(("grp", "pool"), None),
        P(("grp", "pool")),
        P(),
    )
    out_specs = (P(("grp", "pool"), "tp"), P(("grp", "pool"), "tp"))
    return jax.shard_map(shards, mesh=mesh, in_specs=in_specs, out_specs=out_specs, check_vma=False)
```

```python
import functools

import jax
import jax.numpy as jnp
from jax import lax
from jax.experimental import pallas as pl
from jax.experimental.pallas import tpu as pltpu
from jax.sharding import PartitionSpec as P

BF16 = jnp.bfloat16
F32 = jnp.float32
I32 = jnp.int32
VMEM_LIMIT = 20 * 1024 * 1024


def iota(shape, dim):
    return lax.broadcasted_iota(I32, shape, dim)


def split_count(cap):
    pieces = 4
    while cap * pieces % 16:
        pieces *= 2
    return pieces


def dot(a, b):
    return jnp.dot(a, b, preferred_element_type=F32)


def dot_first(a, b):
    return lax.dot_general(a, b, (((0,), (0,)), ((), ())), preferred_element_type=F32)


def select_sum(one_hot, x):
    high = x.astype(BF16)
    low = (x - high.astype(F32)).astype(BF16)
    both = dot(one_hot, jnp.concatenate([high, low], axis=1))
    return both[:, : x.shape[1]] + both[:, x.shape[1] :]


def codes_of(place, rank, cap, pieces):
    code = place * (pieces * cap) + rank
    return jnp.concatenate([code + piece * cap for piece in range(pieces)], axis=1)


def one_hot_of(codes, first, count):
    return ((iota((count, codes.shape[1]), 0) + first) == codes).astype(F32).astype(BF16)


def stack_pieces(hidden, pieces):
    width = hidden.shape[1] // pieces
    return jnp.concatenate(
        [hidden[:, piece * width : (piece + 1) * width] for piece in range(pieces)], axis=0
    )


def pack_kernel(n, cap, pieces, me_ref, small_ref, hidden_ref, slot_ref, rank_ref, *out_refs):
    rows = hidden_ref.shape[0]
    named = (iota((n, rows), 0) == small_ref[:, :rows]).astype(F32).astype(BF16)
    table = jnp.broadcast_to(small_ref[:, rows:].astype(F32).astype(BF16), (16, n))
    slot = dot(table, named)[0:1, :].astype(I32)
    member = (iota((n, rows), 0) == slot).astype(F32)
    before = (iota((rows, rows), 0) < iota((rows, rows), 1)).astype(F32).astype(BF16)
    count = dot(member.astype(BF16), before)
    rank = jnp.sum(member * count, axis=0, keepdims=True).astype(I32)
    slot_ref[...] = slot
    rank_ref[...] = rank
    per = pieces * cap
    apart = lax.bitwise_xor(slot, me_ref[0])
    one_hot = one_hot_of(codes_of(apart, rank, cap, pieces), 0, n * per)
    packed = dot(one_hot, stack_pieces(hidden_ref[...], pieces)).astype(BF16)
    for s, out_ref in enumerate(out_refs):
        out_ref[...] = packed[s * per : (s + 1) * per]


def tables_kernel(n, cap, pieces, out_pieces, me_ref, _, shrink_ref, expand_ref):
    per = pieces * cap
    out_row, in_row = iota(shrink_ref.shape, 0), iota(shrink_ref.shape, 1)
    same = (out_row // cap == in_row // per) & (out_row % cap == in_row % cap)
    shrink_ref[...] = same.astype(F32).astype(BF16)
    per = out_pieces * cap
    out_row, in_row = iota(expand_ref.shape, 0), iota(expand_ref.shape, 1)
    apart = lax.bitwise_xor(out_row // per, me_ref[0])
    source = (out_row // cap % out_pieces) * (n * cap) + apart * cap + out_row % cap
    expand_ref[...] = (source == in_row).astype(F32).astype(BF16)


def shrink(cap, pieces, received_refs, down_ref, table_ref):
    width = received_refs[0].shape[1]
    rank2 = down_ref.shape[2]
    received = jnp.concatenate([ref[...] for ref in received_refs], axis=0)
    size = received.shape[0]
    total = jnp.zeros((size, rank2), F32)
    piece_of = (iota((size, rank2), 0) // cap) % pieces
    for piece in range(pieces):
        part = dot(received, down_ref[0, piece * width : (piece + 1) * width, :])
        total = total + jnp.where(piece_of == piece, part, 0.0)
    return select_sum(table_ref[...], total)


def shrink_near_kernel(cap, pieces, *refs):
    refs[-1][...] = shrink(cap, pieces, refs[:-3], *refs[-3:-1])


def shrink_far_kernel(cap, pieces, *refs):
    near_ref, base_ref, out_ref = refs[-3:]
    half = near_ref.shape[0]
    out_ref[:half, :] = near_ref[...]
    out_ref[half : 2 * half, :] = shrink(cap, pieces, refs[:-5], *refs[-5:-3])
    rows = base_ref.shape[0]
    lanes = out_ref.shape[1]
    for i in range(base_ref.shape[1] // lanes):
        first = 2 * half + i * rows
        out_ref[first : first + rows, :] = base_ref[:, i * lanes : (i + 1) * lanes]


def expand_kernel(n, cap, mine_ref, other_ref, up_ref, table_ref, out_ref):
    rank = up_ref.shape[2]
    head = 128
    blocks = up_ref.shape[3] // head
    reduced = (mine_ref[: n * cap, :] + other_ref[: n * cap, :]).astype(BF16)
    terms = []
    for c in range(2):
        kept = reduced[:, c * rank : (c + 1) * rank]
        wide = dot(kept, up_ref[0, c]).astype(BF16)
        terms += [wide[:, g * head : (g + 1) * head] for g in range(blocks)]
    out_ref[...] = dot(table_ref[...], jnp.concatenate(terms, axis=0)).astype(BF16)


def prepare_kernel(n, cap, slot_ref, rank_ref, mine_ref, other_ref, _, base_ref, one_hot_ref):
    pieces = one_hot_ref.shape[0] // slot_ref.shape[1]
    size = one_hot_ref.shape[1]
    rows = mine_ref.shape[0]
    width = other_ref.shape[1]
    for i in range(mine_ref.shape[1] // width):
        lanes, first = slice(i * width, (i + 1) * width), n * cap + i * rows
        base_ref[:, lanes] = mine_ref[:, lanes] + other_ref[first : first + rows, :]
    one_hot = one_hot_of(codes_of(slot_ref[...], rank_ref[...], cap, pieces), 0, size)
    same = (iota((size, size), 0) == iota((size, size), 1)).astype(F32).astype(BF16)
    one_hot_ref[...] = dot_first(one_hot, same).astype(BF16)


def base_kernel(
    core_ref, hidden_ref, weight_hbm, first_ref, second_ref, mine_ref, other_ref, weight_ref, sems
):
    slots, depth = weight_ref.shape[:2]
    blocks = hidden_ref.shape[1] // depth

    def copy(k):
        part = weight_hbm.at[pl.ds(k * depth, depth), :]
        return pltpu.make_async_copy(part, weight_ref.at[k % slots], sems.at[k % slots])

    for k in range(slots):
        copy(k).start()
    rows, columns = mine_ref.shape
    total = jnp.zeros((rows, 2 * columns), F32)
    for k in range(blocks):
        copy(k).wait()
        total = total + dot(hidden_ref[:, k * depth : (k + 1) * depth], weight_ref[k % slots])
        if k + slots < blocks:
            copy(k + slots).start()
    first, second = total[:, :columns], total[:, columns:]
    mine_ref[...] = jnp.where(core_ref[0] == 0, first, second)
    other_ref[...] = jnp.where(core_ref[0] == 0, second, first)


def cache_kernel(query_ref, key_ref, value_ref, length_ref, _, acc_ref, max_ref, sum_ref):
    rows, groups, positions, head = key_ref.shape
    per_group = query_ref.shape[1] // (groups * head)
    tile = 16
    wide, deep = tile * positions, tile * per_group
    scale = head ** (-0.5)
    row_of = iota((deep, wide), 0) % tile
    own_row = row_of == iota((deep, wide), 1) // positions
    position = iota((deep, wide), 1) % positions
    lane = iota((tile, head), 1)
    for first in range(0, rows, tile):
        at = slice(first, first + tile)
        length = jnp.concatenate([length_ref[at, :]] * per_group, axis=0)
        valid = own_row & (position < length)
        tops = jnp.zeros((tile, head), F32)
        sums = jnp.zeros((tile, head), F32)
        for g in range(groups):
            query = jnp.concatenate(
                [query_ref[at, h * head : (h + 1) * head] for h in range(g * per_group, (g + 1) * per_group)],
                axis=0,
            )
            key = key_ref[at, g].reshape(wide, head)
            value = value_ref[at, g].reshape(wide, head)
            scores = lax.dot_general(query, key, (((1,), (1,)), ((), ())), preferred_element_type=F32)
            scores = jnp.where(valid, scores * scale, -jnp.inf)
            top = jnp.max(scores, axis=1, keepdims=True)
            weight = jnp.exp(scores - top)
            total = jnp.sum(weight, axis=1, keepdims=True)
            mixed = dot(weight.astype(BF16), value)
            for i in range(per_group):
                h = g * per_group + i
                part = slice(i * tile, (i + 1) * tile)
                acc_ref[at, h * head : (h + 1) * head] = mixed[part]
                tops = jnp.where(lane == h, top[part], tops)
                sums = jnp.where(lane == h, total[part], sums)
        max_ref[at, :] = tops
        sum_ref[at, :] = sums


def combine_kernel(
    delta_ref, one_hot_ref, base_ref, query_ref, max_ref, sum_ref, acc_ref, token_ref, out_ref
):
    rows = base_ref.shape[0]
    head = 128
    groups = base_ref.shape[1] // (2 * head)
    delta = dot(one_hot_ref[...], delta_ref[...])
    heads = query_ref.shape[1] // head
    per_group = heads // groups
    scale = head ** (-0.5)
    lane = iota((rows, head), 1)
    own = jnp.zeros((rows, head), F32)
    values = []
    for g in range(groups):
        made = []
        for c in range(2):
            at = (g * 2 + c) * head
            piece = c * groups + g
            made.append((base_ref[:, at : at + head] + delta[piece * rows : (piece + 1) * rows]).astype(BF16))
            token_ref[:, at : at + head] = made[-1]
        key = made[0].astype(F32)
        values.append(made[1].astype(F32))
        for h in range(g * per_group, (g + 1) * per_group):
            query = query_ref[:, h * head : (h + 1) * head].astype(F32)
            own = jnp.where(lane == h, jnp.sum(query * key, axis=1, keepdims=True), own)
    own = own[:, :heads] * scale
    cache_max = max_ref[:, :heads]
    highest = jnp.maximum(own, cache_max)
    cache_factor = jnp.exp(cache_max - highest)
    own_factor = jnp.exp(own - highest)
    inverse = 1.0 / (sum_ref[:, :heads] * cache_factor + own_factor)
    cache_factor = cache_factor * inverse
    own_factor = own_factor * inverse
    for h in range(heads):
        lanes = slice(h * head, (h + 1) * head)
        out = acc_ref[:, lanes] * cache_factor[:, h : h + 1]
        out = out + values[h // per_group] * own_factor[:, h : h + 1]
        out_ref[:, lanes] = out.astype(BF16)


VMEM = pl.BlockSpec(memory_space=pltpu.VMEM)
SMEM = pl.BlockSpec(memory_space=pltpu.SMEM)
HBM = pl.BlockSpec(memory_space=pltpu.HBM)
ANY = pl.BlockSpec(memory_space=pl.ANY)
NO_COST = pl.CostEstimate(flops=0, bytes_accessed=0, transcendentals=0)


def call(kernel, outs, specs, scratch=(), cost=NO_COST):
    return pl.pallas_call(
        kernel,
        out_shape=outs,
        in_specs=specs,
        out_specs=[VMEM] * len(outs),
        scratch_shapes=scratch,
        compiler_params=pltpu.CompilerParams(vmem_limit_bytes=VMEM_LIMIT),
        cost_estimate=cost,
    )


def shards(
    hidden,
    queries,
    key_value_weight,
    adapter_down_weight,
    adapter_up_weight,
    stored_cache_keys,
    stored_cache_values,
    row_adapter_index,
    stored_cache_lengths,
    adapter_slot_table,
):
    n = lax.axis_size("pool")
    rows, width = hidden.shape
    cap = -(-2 * rows // n)
    pieces = split_count(cap)
    groups = stored_cache_keys.shape[1]
    head = stored_cache_keys.shape[3]
    columns = key_value_weight.shape[1] // 2
    out_pieces = 2 * groups
    rank2 = adapter_down_weight.shape[2]

    swap = functools.partial(lax.ppermute, axis_name="tp", perm=[(0, 1), (1, 0)])

    me = lax.axis_index("pool").reshape(1)
    small = jnp.concatenate([row_adapter_index.reshape(1, rows), adapter_slot_table.reshape(1, n)], axis=1)
    slot, rank, *packed = call(
        functools.partial(pack_kernel, n, cap, pieces),
        [jax.ShapeDtypeStruct((1, rows), I32)] * 2
        + [jax.ShapeDtypeStruct((pieces * cap, width // pieces), BF16)] * n,
        [SMEM, VMEM, VMEM],
    )(me, small, hidden)
    half = n // 2
    order = [0, 1, 2, *range(half, n), *range(3, half)]
    arrived = {0: packed[0]}
    for s in order[1:]:
        arrived[s] = lax.ppermute(packed[s], "pool", [(i, i ^ s) for i in range(n)])

    slots, depth = 4, 512
    base_mine, base_other = call(
        base_kernel,
        [jax.ShapeDtypeStruct((rows, columns), F32)] * 2,
        [SMEM, VMEM, ANY, ANY, ANY],
        [
            pltpu.VMEM((slots, depth, 2 * columns), BF16),
            pltpu.SemaphoreType.DMA((slots,)),
        ],
        pl.CostEstimate(
            flops=4 * rows * width * columns, bytes_accessed=16 * width * columns, transcendentals=0
        ),
    )(lax.axis_index("tp").reshape(1), hidden, key_value_weight, arrived[1], arrived[2])

    size = n * out_pieces * cap
    shrink_table, expand_table = call(
        functools.partial(tables_kernel, n, cap, pieces, out_pieces),
        [
            jax.ShapeDtypeStruct((half * cap, half * pieces * cap), BF16),
            jax.ShapeDtypeStruct((size, size), BF16),
        ],
        [SMEM, ANY],
    )(me, base_mine)
    (near_sum,) = call(
        functools.partial(shrink_near_kernel, cap, pieces),
        [jax.ShapeDtypeStruct((half * cap, rank2), F32)],
        [VMEM] * (half + 2),
    )(*[arrived[s] for s in range(half)], adapter_down_weight, shrink_table)
    (sums,) = call(
        functools.partial(shrink_far_kernel, cap, pieces),
        [jax.ShapeDtypeStruct((n * cap + rows * columns // rank2, rank2), F32)],
        [VMEM] * (half + 4),
    )(*[arrived[s] for s in range(half, n)], adapter_down_weight, shrink_table, near_sum, base_other)
    other_sums = swap(sums)
    (terms,) = call(
        functools.partial(expand_kernel, n, cap),
        [jax.ShapeDtypeStruct((size, head), BF16)],
        [VMEM] * 4,
    )(sums, other_sums, adapter_up_weight, expand_table)
    base, one_hot = call(
        functools.partial(prepare_kernel, n, cap),
        [
            jax.ShapeDtypeStruct((rows, columns), F32),
            jax.ShapeDtypeStruct((out_pieces * rows, size), BF16),
        ],
        [VMEM] * 4 + [ANY],
    )(slot, rank, base_mine, other_sums, terms)
    deltas = lax.all_to_all(terms, "pool", split_axis=0, concat_axis=0, tiled=True)
    attended, cache_max, cache_sum = call(
        cache_kernel,
        [jax.ShapeDtypeStruct(queries.shape, F32)] + [jax.ShapeDtypeStruct((rows, head), F32)] * 2,
        [VMEM] * 4 + [ANY],
    )(queries, stored_cache_keys, stored_cache_values, stored_cache_lengths.reshape(rows, 1), terms)
    token, out = call(
        combine_kernel,
        [jax.ShapeDtypeStruct((rows, columns), BF16), jax.ShapeDtypeStruct(queries.shape, BF16)],
        [VMEM] * 7,
    )(deltas, one_hot, base, queries, cache_max, cache_sum, attended)
    return token, out


def solution(mesh):
    in_specs = (
        P(("grp", "pool"), "tp"),
        P(("grp", "pool"), "tp"),
        P("tp", None),
        P("pool", "tp", None),
        P("pool", None, None, "tp"),
        P(("grp", "pool"), "tp", None, None),
        P(("grp", "pool"), "tp", None, None),
        P(("grp", "pool"), None),
        P(("grp", "pool")),
        P(),
    )
    out_specs = (P(("grp", "pool"), "tp"), P(("grp", "pool"), "tp"))
    return jax.shard_map(shards, mesh=mesh, in_specs=in_specs, out_specs=out_specs, check_vma=False)
```

```python
import functools

import jax
import jax.numpy as jnp
from jax import lax
from jax.experimental import pallas as pl
from jax.experimental.pallas import tpu as pltpu
from jax.sharding import PartitionSpec as P

BF16 = jnp.bfloat16
F32 = jnp.float32
I32 = jnp.int32
VMEM_LIMIT = 20 * 1024 * 1024


def iota(shape, dim):
    return lax.broadcasted_iota(I32, shape, dim)


def split_count(cap):
    pieces = 4
    while cap * pieces % 16:
        pieces *= 2
    return pieces


def dot(a, b):
    return jnp.dot(a, b, preferred_element_type=F32)


def dot_first(a, b):
    return lax.dot_general(a, b, (((0,), (0,)), ((), ())), preferred_element_type=F32)


def select_sum(one_hot, x):
    high = x.astype(BF16)
    low = (x - high.astype(F32)).astype(BF16)
    both = dot(one_hot, jnp.concatenate([high, low], axis=1))
    return both[:, : x.shape[1]] + both[:, x.shape[1] :]


def codes_of(place, rank, cap, pieces):
    code = place * (pieces * cap) + rank
    return jnp.concatenate([code + piece * cap for piece in range(pieces)], axis=1)


def one_hot_of(codes, first, count):
    return ((iota((count, codes.shape[1]), 0) + first) == codes).astype(F32).astype(BF16)


def stack_pieces(hidden, pieces):
    width = hidden.shape[1] // pieces
    return jnp.concatenate(
        [hidden[:, piece * width : (piece + 1) * width] for piece in range(pieces)], axis=0
    )


def pack_kernel(n, cap, pieces, me_ref, small_ref, hidden_ref, slot_ref, rank_ref, *out_refs):
    rows = hidden_ref.shape[0]
    named = (iota((n, rows), 0) == small_ref[:, :rows]).astype(F32).astype(BF16)
    table = jnp.broadcast_to(small_ref[:, rows:].astype(F32).astype(BF16), (16, n))
    slot = dot(table, named)[0:1, :].astype(I32)
    member = (iota((n, rows), 0) == slot).astype(F32)
    before = (iota((rows, rows), 0) < iota((rows, rows), 1)).astype(F32).astype(BF16)
    count = dot(member.astype(BF16), before)
    rank = jnp.sum(member * count, axis=0, keepdims=True).astype(I32)
    slot_ref[...] = slot
    rank_ref[...] = rank
    per = pieces * cap
    apart = lax.bitwise_xor(slot, me_ref[0])
    one_hot = one_hot_of(codes_of(apart, rank, cap, pieces), 0, n * per)
    packed = dot(one_hot, stack_pieces(hidden_ref[...], pieces)).astype(BF16)
    for s, out_ref in enumerate(out_refs):
        out_ref[...] = packed[s * per : (s + 1) * per]


def tables_kernel(n, cap, pieces, out_pieces, me_ref, _, shrink_ref, expand_ref):
    per = pieces * cap
    out_row, in_row = iota(shrink_ref.shape, 0), iota(shrink_ref.shape, 1)
    same = (out_row // cap == in_row // per) & (out_row % cap == in_row % cap)
    shrink_ref[...] = same.astype(F32).astype(BF16)
    per = out_pieces * cap
    out_row, in_row = iota(expand_ref.shape, 0), iota(expand_ref.shape, 1)
    apart = lax.bitwise_xor(out_row // per, me_ref[0])
    source = (out_row // cap % out_pieces) * (n * cap) + apart * cap + out_row % cap
    expand_ref[...] = (source == in_row).astype(F32).astype(BF16)


def shrink(cap, pieces, received_refs, down_ref, table_ref):
    width = received_refs[0].shape[1]
    rank2 = down_ref.shape[2]
    received = jnp.concatenate([ref[...] for ref in received_refs], axis=0)
    size = received.shape[0]
    total = jnp.zeros((size, rank2), F32)
    piece_of = (iota((size, rank2), 0) // cap) % pieces
    for piece in range(pieces):
        part = dot(received, down_ref[0, piece * width : (piece + 1) * width, :])
        total = total + jnp.where(piece_of == piece, part, 0.0)
    return select_sum(table_ref[...], total)


def shrink_near_kernel(cap, pieces, *refs):
    refs[-1][...] = shrink(cap, pieces, refs[:-3], *refs[-3:-1])


def shrink_far_kernel(cap, pieces, *refs):
    near_ref, out_ref = refs[-2:]
    half = near_ref.shape[0]
    out_ref[:half, :] = near_ref[...]
    out_ref[half:, :] = shrink(cap, pieces, refs[:-4], *refs[-4:-2])


def expand_kernel(mine_ref, other_ref, up_ref, table_ref, out_ref):
    rank = up_ref.shape[2]
    head = 128
    blocks = up_ref.shape[3] // head
    reduced = (mine_ref[...] + other_ref[...]).astype(BF16)
    terms = []
    for c in range(2):
        kept = reduced[:, c * rank : (c + 1) * rank]
        wide = dot(kept, up_ref[0, c]).astype(BF16)
        terms += [wide[:, g * head : (g + 1) * head] for g in range(blocks)]
    out_ref[...] = dot(table_ref[...], jnp.concatenate(terms, axis=0)).astype(BF16)


def prepare_kernel(cap, slot_ref, rank_ref, mine_ref, other_ref, base_ref, one_hot_ref):
    pieces = one_hot_ref.shape[0] // slot_ref.shape[1]
    size = one_hot_ref.shape[1]
    base_ref[...] = mine_ref[...] + other_ref[...]
    one_hot = one_hot_of(codes_of(slot_ref[...], rank_ref[...], cap, pieces), 0, size)
    same = (iota((size, size), 0) == iota((size, size), 1)).astype(F32).astype(BF16)
    one_hot_ref[...] = dot_first(one_hot, same).astype(BF16)


def combine_kernel(
    delta_ref,
    one_hot_ref,
    base_ref,
    query_ref,
    max_ref,
    sum_ref,
    acc_ref,
    token_hbm,
    out_hbm,
    token_ref,
    out_ref,
    sems,
):
    rows = base_ref.shape[0]
    head = 128
    groups = base_ref.shape[1] // (2 * head)
    delta = dot(one_hot_ref[...], delta_ref[...])
    heads = query_ref.shape[1] // head
    per_group = heads // groups
    scale = head ** (-0.5)
    lane = iota((rows, head), 1)
    copies = []
    for g in range(groups):
        made = []
        for c in range(2):
            at = (g * 2 + c) * head
            piece = c * groups + g
            made.append((base_ref[:, at : at + head] + delta[piece * rows : (piece + 1) * rows]).astype(BF16))
            token_ref[:, at : at + head] = made[-1]
        key, value = made[0].astype(F32), made[1].astype(F32)
        own = jnp.zeros((rows, head), F32)
        for h in range(g * per_group, (g + 1) * per_group):
            query = query_ref[:, h * head : (h + 1) * head].astype(F32)
            own = jnp.where(lane == h, jnp.sum(query * key, axis=1, keepdims=True), own)
        own = own * scale
        cache_max = max_ref[...]
        highest = jnp.maximum(own, cache_max)
        cache_factor = jnp.exp(cache_max - highest)
        own_factor = jnp.exp(own - highest)
        inverse = 1.0 / (sum_ref[...] * cache_factor + own_factor)
        cache_factor = cache_factor * inverse
        own_factor = own_factor * inverse
        for h in range(g * per_group, (g + 1) * per_group):
            lanes = slice(h * head, (h + 1) * head)
            out = acc_ref[:, lanes] * cache_factor[:, h : h + 1] + value * own_factor[:, h : h + 1]
            out_ref[:, lanes] = out.astype(BF16)
        for i, (source, target, width) in enumerate(
            [(token_ref, token_hbm, 2 * head), (out_ref, out_hbm, per_group * head)]
        ):
            part = pl.ds(g * width, width)
            copies.append(pltpu.make_async_copy(source.at[:, part], target.at[:, part], sems.at[2 * g + i]))
            copies[-1].start()
    for copy in copies:
        copy.wait()


def base_kernel(
    core_ref, hidden_ref, weight_hbm, first_ref, second_ref, mine_ref, other_ref, weight_ref, sems
):
    slots, depth = weight_ref.shape[:2]
    blocks = hidden_ref.shape[1] // depth

    def copy(k):
        part = weight_hbm.at[pl.ds(k * depth, depth), :]
        return pltpu.make_async_copy(part, weight_ref.at[k % slots], sems.at[k % slots])

    for k in range(slots):
        copy(k).start()
    rows, columns = mine_ref.shape
    total = jnp.zeros((rows, 2 * columns), F32)
    for k in range(blocks):
        copy(k).wait()
        total = total + dot(hidden_ref[:, k * depth : (k + 1) * depth], weight_ref[k % slots])
        if k + slots < blocks:
            copy(k + slots).start()
    first, second = total[:, :columns], total[:, columns:]
    mine_ref[...] = jnp.where(core_ref[0] == 0, first, second)
    other_ref[...] = jnp.where(core_ref[0] == 0, second, first)


def cache_kernel(
    query_ref, key_ref, value_ref, length_ref, base_ref, _, acc_ref, max_ref, sum_ref, handed_ref
):
    handed_ref[...] = base_ref[...]
    rows, groups, positions, head = key_ref.shape
    per_group = query_ref.shape[1] // (groups * head)
    tile = 16
    wide, deep = tile * positions, tile * per_group
    scale = head ** (-0.5)
    row_of = iota((deep, wide), 0) % tile
    own_row = row_of == iota((deep, wide), 1) // positions
    position = iota((deep, wide), 1) % positions
    lane = iota((tile, head), 1)
    for first in range(0, rows, tile):
        at = slice(first, first + tile)
        length = jnp.concatenate([length_ref[at, :]] * per_group, axis=0)
        valid = own_row & (position < length)
        tops = jnp.zeros((tile, head), F32)
        sums = jnp.zeros((tile, head), F32)
        for g in range(groups):
            query = jnp.concatenate(
                [query_ref[at, h * head : (h + 1) * head] for h in range(g * per_group, (g + 1) * per_group)],
                axis=0,
            )
            key = key_ref[at, g].reshape(wide, head)
            value = value_ref[at, g].reshape(wide, head)
            scores = lax.dot_general(query, key, (((1,), (1,)), ((), ())), preferred_element_type=F32)
            scores = jnp.where(valid, scores * scale, -jnp.inf)
            top = jnp.max(scores, axis=1, keepdims=True)
            weight = jnp.exp(scores - top)
            total = jnp.sum(weight, axis=1, keepdims=True)
            mixed = dot(weight.astype(BF16), value)
            for i in range(per_group):
                h = g * per_group + i
                part = slice(i * tile, (i + 1) * tile)
                acc_ref[at, h * head : (h + 1) * head] = mixed[part]
                tops = jnp.where(lane == h, top[part], tops)
                sums = jnp.where(lane == h, total[part], sums)
        max_ref[at, :] = tops
        sum_ref[at, :] = sums


VMEM = pl.BlockSpec(memory_space=pltpu.VMEM)
SMEM = pl.BlockSpec(memory_space=pltpu.SMEM)
HBM = pl.BlockSpec(memory_space=pltpu.HBM)
ANY = pl.BlockSpec(memory_space=pl.ANY)
NO_COST = pl.CostEstimate(flops=0, bytes_accessed=0, transcendentals=0)


def call(kernel, outs, specs, scratch=(), cost=NO_COST):
    return pl.pallas_call(
        kernel,
        out_shape=outs,
        in_specs=specs,
        out_specs=[VMEM] * len(outs),
        scratch_shapes=scratch,
        compiler_params=pltpu.CompilerParams(vmem_limit_bytes=VMEM_LIMIT),
        cost_estimate=cost,
    )


def shards(
    hidden,
    queries,
    key_value_weight,
    adapter_down_weight,
    adapter_up_weight,
    stored_cache_keys,
    stored_cache_values,
    row_adapter_index,
    stored_cache_lengths,
    adapter_slot_table,
):
    n = lax.axis_size("pool")
    rows, width = hidden.shape
    cap = -(-2 * rows // n)
    pieces = split_count(cap)
    groups = stored_cache_keys.shape[1]
    head = stored_cache_keys.shape[3]
    columns = key_value_weight.shape[1] // 2
    out_pieces = 2 * groups
    rank2 = adapter_down_weight.shape[2]

    swap = functools.partial(lax.ppermute, axis_name="tp", perm=[(0, 1), (1, 0)])

    me = lax.axis_index("pool").reshape(1)
    small = jnp.concatenate([row_adapter_index.reshape(1, rows), adapter_slot_table.reshape(1, n)], axis=1)
    slot, rank, *packed = call(
        functools.partial(pack_kernel, n, cap, pieces),
        [jax.ShapeDtypeStruct((1, rows), I32)] * 2
        + [jax.ShapeDtypeStruct((pieces * cap, width // pieces), BF16)] * n,
        [SMEM, VMEM, VMEM],
    )(me, small, hidden)
    half = n // 2
    order = [0, 1, 2, *range(half, n), *range(3, half)]
    arrived = {0: packed[0]}
    for s in order[1:]:
        arrived[s] = lax.ppermute(packed[s], "pool", [(i, i ^ s) for i in range(n)])

    slots, depth = 4, 512
    base_mine, base_other = call(
        base_kernel,
        [jax.ShapeDtypeStruct((rows, columns), F32)] * 2,
        [SMEM, VMEM, ANY, ANY, ANY],
        [
            pltpu.VMEM((slots, depth, 2 * columns), BF16),
            pltpu.SemaphoreType.DMA((slots,)),
        ],
        pl.CostEstimate(
            flops=4 * rows * width * columns, bytes_accessed=16 * width * columns, transcendentals=0
        ),
    )(lax.axis_index("tp").reshape(1), hidden, key_value_weight, arrived[1], arrived[2])

    size = n * out_pieces * cap
    shrink_table, expand_table = call(
        functools.partial(tables_kernel, n, cap, pieces, out_pieces),
        [
            jax.ShapeDtypeStruct((half * cap, half * pieces * cap), BF16),
            jax.ShapeDtypeStruct((size, size), BF16),
        ],
        [SMEM, ANY],
    )(me, base_mine)
    (near_sum,) = call(
        functools.partial(shrink_near_kernel, cap, pieces),
        [jax.ShapeDtypeStruct((half * cap, rank2), F32)],
        [VMEM] * (half + 2),
    )(*[arrived[s] for s in range(half)], adapter_down_weight, shrink_table)
    (sums,) = call(
        functools.partial(shrink_far_kernel, cap, pieces),
        [jax.ShapeDtypeStruct((n * cap, rank2), F32)],
        [VMEM] * (half + 3),
    )(*[arrived[s] for s in range(half, n)], adapter_down_weight, shrink_table, near_sum)
    (terms,) = call(
        expand_kernel,
        [jax.ShapeDtypeStruct((size, head), BF16)],
        [VMEM] * 4,
    )(sums, swap(sums), adapter_up_weight, expand_table)
    deltas = lax.all_to_all(terms, "pool", split_axis=0, concat_axis=0, tiled=True)
    attended, cache_max, cache_sum, base_other = call(
        cache_kernel,
        [jax.ShapeDtypeStruct(queries.shape, F32)]
        + [jax.ShapeDtypeStruct((rows, head), F32)] * 2
        + [jax.ShapeDtypeStruct((rows, columns), F32)],
        [VMEM] * 5 + [ANY],
    )(
        queries,
        stored_cache_keys,
        stored_cache_values,
        stored_cache_lengths.reshape(rows, 1),
        base_other,
        terms,
    )
    base, one_hot = call(
        functools.partial(prepare_kernel, cap),
        [
            jax.ShapeDtypeStruct((rows, columns), F32),
            jax.ShapeDtypeStruct((out_pieces * rows, size), BF16),
        ],
        [VMEM] * 4,
    )(slot, rank, base_mine, swap(base_other))
    token, out = pl.pallas_call(
        combine_kernel,
        out_shape=[jax.ShapeDtypeStruct((rows, columns), BF16), jax.ShapeDtypeStruct(queries.shape, BF16)],
        in_specs=[VMEM] * 7,
        out_specs=[ANY] * 2,
        scratch_shapes=[
            pltpu.VMEM((rows, columns), BF16),
            pltpu.VMEM(queries.shape, BF16),
            pltpu.SemaphoreType.DMA((2 * groups,)),
        ],
        compiler_params=pltpu.CompilerParams(vmem_limit_bytes=VMEM_LIMIT),
        cost_estimate=NO_COST,
    )(deltas, one_hot, base, queries, cache_max, cache_sum, attended)
    return token, out


def solution(mesh):
    in_specs = (
        P(("grp", "pool"), "tp"),
        P(("grp", "pool"), "tp"),
        P("tp", None),
        P("pool", "tp", None),
        P("pool", None, None, "tp"),
        P(("grp", "pool"), "tp", None, None),
        P(("grp", "pool"), "tp", None, None),
        P(("grp", "pool"), None),
        P(("grp", "pool")),
        P(),
    )
    out_specs = (P(("grp", "pool"), "tp"), P(("grp", "pool"), "tp"))
    return jax.shard_map(shards, mesh=mesh, in_specs=in_specs, out_specs=out_specs, check_vma=False)
```

```python
import functools

import jax
import jax.numpy as jnp
from jax import lax
from jax.experimental import pallas as pl
from jax.experimental.pallas import tpu as pltpu
from jax.sharding import PartitionSpec as P

BF16 = jnp.bfloat16
F32 = jnp.float32
I32 = jnp.int32
VMEM_LIMIT = 20 * 1024 * 1024


def iota(shape, dim):
    return lax.broadcasted_iota(I32, shape, dim)


def split_count(cap):
    pieces = 4
    while cap * pieces % 16:
        pieces *= 2
    return pieces


def dot(a, b):
    return jnp.dot(a, b, preferred_element_type=F32)


def dot_first(a, b):
    return lax.dot_general(a, b, (((0,), (0,)), ((), ())), preferred_element_type=F32)


def select_sum(one_hot, x):
    high = x.astype(BF16)
    low = (x - high.astype(F32)).astype(BF16)
    both = dot(one_hot, jnp.concatenate([high, low], axis=1))
    return both[:, : x.shape[1]] + both[:, x.shape[1] :]


def codes_of(place, rank, cap, pieces):
    code = place * (pieces * cap) + rank
    return jnp.concatenate([code + piece * cap for piece in range(pieces)], axis=1)


def one_hot_of(codes, first, count):
    return ((iota((count, codes.shape[1]), 0) + first) == codes).astype(F32).astype(BF16)


def stack_pieces(hidden, pieces):
    width = hidden.shape[1] // pieces
    return jnp.concatenate(
        [hidden[:, piece * width : (piece + 1) * width] for piece in range(pieces)], axis=0
    )


def pack_kernel(n, cap, pieces, me_ref, small_ref, hidden_ref, slot_ref, rank_ref, *out_refs):
    rows = hidden_ref.shape[0]
    named = (iota((n, rows), 0) == small_ref[:, :rows]).astype(F32).astype(BF16)
    table = jnp.broadcast_to(small_ref[:, rows:].astype(F32).astype(BF16), (16, n))
    slot = dot(table, named)[0:1, :].astype(I32)
    member = (iota((n, rows), 0) == slot).astype(F32)
    before = (iota((rows, rows), 0) < iota((rows, rows), 1)).astype(F32).astype(BF16)
    count = dot(member.astype(BF16), before)
    rank = jnp.sum(member * count, axis=0, keepdims=True).astype(I32)
    slot_ref[...] = slot
    rank_ref[...] = rank
    per = pieces * cap
    apart = lax.bitwise_xor(slot, me_ref[0])
    one_hot = one_hot_of(codes_of(apart, rank, cap, pieces), 0, n * per)
    packed = dot(one_hot, stack_pieces(hidden_ref[...], pieces)).astype(BF16)
    for s, out_ref in enumerate(out_refs):
        out_ref[...] = packed[s * per : (s + 1) * per]


def tables_kernel(n, cap, pieces, out_pieces, me_ref, _, shrink_ref, part_ref, expand_ref):
    per = pieces * cap
    for ref in (shrink_ref, part_ref):
        out_row, in_row = iota(ref.shape, 0), iota(ref.shape, 1)
        same = (out_row // cap == in_row // per) & (out_row % cap == in_row % cap)
        ref[...] = same.astype(F32).astype(BF16)
    per = out_pieces * cap
    out_row, in_row = iota(expand_ref.shape, 0), iota(expand_ref.shape, 1)
    apart = lax.bitwise_xor(out_row // per, me_ref[0])
    source = (out_row // cap % out_pieces) * (n * cap) + apart * cap + out_row % cap
    expand_ref[...] = (source == in_row).astype(F32).astype(BF16)


def shrink(cap, pieces, received_refs, down_ref, table_ref):
    width = received_refs[0].shape[1]
    rank2 = down_ref.shape[2]
    received = jnp.concatenate([ref[...] for ref in received_refs], axis=0)
    size = received.shape[0]
    total = jnp.zeros((size, rank2), F32)
    piece_of = (iota((size, rank2), 0) // cap) % pieces
    for piece in range(pieces):
        part = dot(received, down_ref[0, piece * width : (piece + 1) * width, :])
        total = total + jnp.where(piece_of == piece, part, 0.0)
    return select_sum(table_ref[...], total)


def shrink_near_kernel(cap, pieces, count, *refs):
    refs[-1][...] = shrink(cap, pieces, refs[:count], *refs[count : count + 2])


def shrink_far_kernel(cap, pieces, *refs):
    near_ref, part_ref, out_ref = refs[-3:]
    half = near_ref.shape[0]
    done = half + part_ref.shape[0]
    out_ref[:half, :] = near_ref[...]
    out_ref[half:done, :] = part_ref[...]
    out_ref[done:, :] = shrink(cap, pieces, refs[:-5], *refs[-5:-3])


def expand_kernel(mine_ref, other_ref, up_ref, table_ref, out_ref):
    rank = up_ref.shape[2]
    head = 128
    blocks = up_ref.shape[3] // head
    reduced = (mine_ref[...] + other_ref[...]).astype(BF16)
    terms = []
    for c in range(2):
        kept = reduced[:, c * rank : (c + 1) * rank]
        wide = dot(kept, up_ref[0, c]).astype(BF16)
        terms += [wide[:, g * head : (g + 1) * head] for g in range(blocks)]
    out_ref[...] = dot(table_ref[...], jnp.concatenate(terms, axis=0)).astype(BF16)


def prepare_kernel(cap, slot_ref, rank_ref, mine_ref, other_ref, base_ref, one_hot_ref):
    pieces = one_hot_ref.shape[0] // slot_ref.shape[1]
    size = one_hot_ref.shape[1]
    base_ref[...] = mine_ref[...] + other_ref[...]
    one_hot = one_hot_of(codes_of(slot_ref[...], rank_ref[...], cap, pieces), 0, size)
    same = (iota((size, size), 0) == iota((size, size), 1)).astype(F32).astype(BF16)
    one_hot_ref[...] = dot_first(one_hot, same).astype(BF16)


def combine_kernel(
    delta_ref,
    one_hot_ref,
    base_ref,
    query_ref,
    max_ref,
    sum_ref,
    acc_ref,
    token_hbm,
    out_hbm,
    token_ref,
    out_ref,
    sems,
):
    rows = base_ref.shape[0]
    head = 128
    groups = base_ref.shape[1] // (2 * head)
    delta = dot(one_hot_ref[...], delta_ref[...])
    heads = query_ref.shape[1] // head
    per_group = heads // groups
    scale = head ** (-0.5)
    lane = iota((rows, head), 1)
    copies = []
    for g in range(groups):
        made = []
        for c in range(2):
            at = (g * 2 + c) * head
            piece = c * groups + g
            made.append((base_ref[:, at : at + head] + delta[piece * rows : (piece + 1) * rows]).astype(BF16))
            token_ref[:, at : at + head] = made[-1]
        key, value = made[0].astype(F32), made[1].astype(F32)
        own = jnp.zeros((rows, head), F32)
        for h in range(g * per_group, (g + 1) * per_group):
            query = query_ref[:, h * head : (h + 1) * head].astype(F32)
            own = jnp.where(lane == h, jnp.sum(query * key, axis=1, keepdims=True), own)
        own = own * scale
        cache_max = max_ref[...]
        highest = jnp.maximum(own, cache_max)
        cache_factor = jnp.exp(cache_max - highest)
        own_factor = jnp.exp(own - highest)
        inverse = 1.0 / (sum_ref[...] * cache_factor + own_factor)
        cache_factor = cache_factor * inverse
        own_factor = own_factor * inverse
        for h in range(g * per_group, (g + 1) * per_group):
            lanes = slice(h * head, (h + 1) * head)
            out = acc_ref[:, lanes] * cache_factor[:, h : h + 1] + value * own_factor[:, h : h + 1]
            out_ref[:, lanes] = out.astype(BF16)
        for i, (source, target, width) in enumerate(
            [(token_ref, token_hbm, 2 * head), (out_ref, out_hbm, per_group * head)]
        ):
            part = pl.ds(g * width, width)
            copies.append(pltpu.make_async_copy(source.at[:, part], target.at[:, part], sems.at[2 * g + i]))
            copies[-1].start()
    for copy in copies:
        copy.wait()


def base_kernel(
    core_ref, hidden_ref, weight_hbm, first_ref, second_ref, mine_ref, other_ref, weight_ref, sems
):
    slots, depth = weight_ref.shape[:2]
    blocks = hidden_ref.shape[1] // depth

    def copy(k):
        part = weight_hbm.at[pl.ds(k * depth, depth), :]
        return pltpu.make_async_copy(part, weight_ref.at[k % slots], sems.at[k % slots])

    for k in range(slots):
        copy(k).start()
    rows, columns = mine_ref.shape
    total = jnp.zeros((rows, 2 * columns), F32)
    for k in range(blocks):
        copy(k).wait()
        total = total + dot(hidden_ref[:, k * depth : (k + 1) * depth], weight_ref[k % slots])
        if k + slots < blocks:
            copy(k + slots).start()
    first, second = total[:, :columns], total[:, columns:]
    mine_ref[...] = jnp.where(core_ref[0] == 0, first, second)
    other_ref[...] = jnp.where(core_ref[0] == 0, second, first)


def cache_kernel(
    query_ref, key_ref, value_ref, length_ref, base_ref, _, acc_ref, max_ref, sum_ref, handed_ref
):
    handed_ref[...] = base_ref[...]
    rows, groups, positions, head = key_ref.shape
    per_group = query_ref.shape[1] // (groups * head)
    tile = 16
    wide, deep = tile * positions, tile * per_group
    scale = head ** (-0.5)
    row_of = iota((deep, wide), 0) % tile
    own_row = row_of == iota((deep, wide), 1) // positions
    position = iota((deep, wide), 1) % positions
    lane = iota((tile, head), 1)
    for first in range(0, rows, tile):
        at = slice(first, first + tile)
        length = jnp.concatenate([length_ref[at, :]] * per_group, axis=0)
        valid = own_row & (position < length)
        tops = jnp.zeros((tile, head), F32)
        sums = jnp.zeros((tile, head), F32)
        for g in range(groups):
            query = jnp.concatenate(
                [query_ref[at, h * head : (h + 1) * head] for h in range(g * per_group, (g + 1) * per_group)],
                axis=0,
            )
            key = key_ref[at, g].reshape(wide, head)
            value = value_ref[at, g].reshape(wide, head)
            scores = lax.dot_general(query, key, (((1,), (1,)), ((), ())), preferred_element_type=F32)
            scores = jnp.where(valid, scores * scale, -jnp.inf)
            top = jnp.max(scores, axis=1, keepdims=True)
            weight = jnp.exp(scores - top)
            total = jnp.sum(weight, axis=1, keepdims=True)
            mixed = dot(weight.astype(BF16), value)
            for i in range(per_group):
                h = g * per_group + i
                part = slice(i * tile, (i + 1) * tile)
                acc_ref[at, h * head : (h + 1) * head] = mixed[part]
                tops = jnp.where(lane == h, top[part], tops)
                sums = jnp.where(lane == h, total[part], sums)
        max_ref[at, :] = tops
        sum_ref[at, :] = sums


VMEM = pl.BlockSpec(memory_space=pltpu.VMEM)
SMEM = pl.BlockSpec(memory_space=pltpu.SMEM)
HBM = pl.BlockSpec(memory_space=pltpu.HBM)
ANY = pl.BlockSpec(memory_space=pl.ANY)
NO_COST = pl.CostEstimate(flops=0, bytes_accessed=0, transcendentals=0)


def call(kernel, outs, specs, scratch=(), cost=NO_COST):
    return pl.pallas_call(
        kernel,
        out_shape=outs,
        in_specs=specs,
        out_specs=[VMEM] * len(outs),
        scratch_shapes=scratch,
        compiler_params=pltpu.CompilerParams(vmem_limit_bytes=VMEM_LIMIT),
        cost_estimate=cost,
    )


def shards(
    hidden,
    queries,
    key_value_weight,
    adapter_down_weight,
    adapter_up_weight,
    stored_cache_keys,
    stored_cache_values,
    row_adapter_index,
    stored_cache_lengths,
    adapter_slot_table,
):
    n = lax.axis_size("pool")
    rows, width = hidden.shape
    cap = -(-2 * rows // n)
    pieces = split_count(cap)
    groups = stored_cache_keys.shape[1]
    head = stored_cache_keys.shape[3]
    columns = key_value_weight.shape[1] // 2
    out_pieces = 2 * groups
    rank2 = adapter_down_weight.shape[2]

    swap = functools.partial(lax.ppermute, axis_name="tp", perm=[(0, 1), (1, 0)])

    me = lax.axis_index("pool").reshape(1)
    small = jnp.concatenate([row_adapter_index.reshape(1, rows), adapter_slot_table.reshape(1, n)], axis=1)
    slot, rank, *packed = call(
        functools.partial(pack_kernel, n, cap, pieces),
        [jax.ShapeDtypeStruct((1, rows), I32)] * 2
        + [jax.ShapeDtypeStruct((pieces * cap, width // pieces), BF16)] * n,
        [SMEM, VMEM, VMEM],
    )(me, small, hidden)
    half = n // 2
    order = [0, 1, 2, *range(half, n), *range(3, half)]
    arrived = {0: packed[0]}
    for s in order[1:]:
        arrived[s] = lax.ppermute(packed[s], "pool", [(i, i ^ s) for i in range(n)])

    slots, depth = 4, 512
    base_mine, base_other = call(
        base_kernel,
        [jax.ShapeDtypeStruct((rows, columns), F32)] * 2,
        [SMEM, VMEM, ANY, ANY, ANY],
        [
            pltpu.VMEM((slots, depth, 2 * columns), BF16),
            pltpu.SemaphoreType.DMA((slots,)),
        ],
        pl.CostEstimate(
            flops=4 * rows * width * columns, bytes_accessed=16 * width * columns, transcendentals=0
        ),
    )(lax.axis_index("tp").reshape(1), hidden, key_value_weight, arrived[1], arrived[2])

    size = n * out_pieces * cap
    shrink_table, part_table, expand_table = call(
        functools.partial(tables_kernel, n, cap, pieces, out_pieces),
        [
            jax.ShapeDtypeStruct((half * cap, half * pieces * cap), BF16),
            jax.ShapeDtypeStruct((half // 2 * cap, half // 2 * pieces * cap), BF16),
            jax.ShapeDtypeStruct((size, size), BF16),
        ],
        [SMEM, ANY],
    )(me, base_mine)
    (near_sum,) = call(
        functools.partial(shrink_near_kernel, cap, pieces, half),
        [jax.ShapeDtypeStruct((half * cap, rank2), F32)],
        [VMEM] * (half + 2),
    )(*[arrived[s] for s in range(half)], adapter_down_weight, shrink_table)
    middle = half + half // 2
    (part_sum,) = call(
        functools.partial(shrink_near_kernel, cap, pieces, half // 2),
        [jax.ShapeDtypeStruct((half // 2 * cap, rank2), F32)],
        [VMEM] * (half // 2 + 2) + [ANY],
    )(*[arrived[s] for s in range(half, middle)], adapter_down_weight, part_table, near_sum)
    (sums,) = call(
        functools.partial(shrink_far_kernel, cap, pieces),
        [jax.ShapeDtypeStruct((n * cap, rank2), F32)],
        [VMEM] * (half // 2 + 4),
    )(*[arrived[s] for s in range(middle, n)], adapter_down_weight, part_table, near_sum, part_sum)
    (terms,) = call(
        expand_kernel,
        [jax.ShapeDtypeStruct((size, head), BF16)],
        [VMEM] * 4,
    )(sums, swap(sums), adapter_up_weight, expand_table)
    deltas = lax.all_to_all(terms, "pool", split_axis=0, concat_axis=0, tiled=True)
    attended, cache_max, cache_sum, base_other = call(
        cache_kernel,
        [jax.ShapeDtypeStruct(queries.shape, F32)]
        + [jax.ShapeDtypeStruct((rows, head), F32)] * 2
        + [jax.ShapeDtypeStruct((rows, columns), F32)],
        [VMEM] * 5 + [ANY],
    )(
        queries,
        stored_cache_keys,
        stored_cache_values,
        stored_cache_lengths.reshape(rows, 1),
        base_other,
        terms,
    )
    base, one_hot = call(
        functools.partial(prepare_kernel, cap),
        [
            jax.ShapeDtypeStruct((rows, columns), F32),
            jax.ShapeDtypeStruct((out_pieces * rows, size), BF16),
        ],
        [VMEM] * 4,
    )(slot, rank, base_mine, swap(base_other))
    token, out = pl.pallas_call(
        combine_kernel,
        out_shape=[jax.ShapeDtypeStruct((rows, columns), BF16), jax.ShapeDtypeStruct(queries.shape, BF16)],
        in_specs=[VMEM] * 7,
        out_specs=[ANY] * 2,
        scratch_shapes=[
            pltpu.VMEM((rows, columns), BF16),
            pltpu.VMEM(queries.shape, BF16),
            pltpu.SemaphoreType.DMA((2 * groups,)),
        ],
        compiler_params=pltpu.CompilerParams(vmem_limit_bytes=VMEM_LIMIT),
        cost_estimate=NO_COST,
    )(deltas, one_hot, base, queries, cache_max, cache_sum, attended)
    return token, out


def solution(mesh):
    in_specs = (
        P(("grp", "pool"), "tp"),
        P(("grp", "pool"), "tp"),
        P("tp", None),
        P("pool", "tp", None),
        P("pool", None, None, "tp"),
        P(("grp", "pool"), "tp", None, None),
        P(("grp", "pool"), "tp", None, None),
        P(("grp", "pool"), None),
        P(("grp", "pool")),
        P(),
    )
    out_specs = (P(("grp", "pool"), "tp"), P(("grp", "pool"), "tp"))
    return jax.shard_map(shards, mesh=mesh, in_specs=in_specs, out_specs=out_specs, check_vma=False)
```

```python
import functools

import jax
import jax.numpy as jnp
from jax import lax
from jax.experimental import pallas as pl
from jax.experimental.pallas import tpu as pltpu
from jax.sharding import PartitionSpec as P

BF16 = jnp.bfloat16
F32 = jnp.float32
I32 = jnp.int32
VMEM_LIMIT = 20 * 1024 * 1024


def iota(shape, dim):
    return lax.broadcasted_iota(I32, shape, dim)


def split_count(cap):
    pieces = 4
    while cap * pieces % 16:
        pieces *= 2
    return pieces


def dot(a, b):
    return jnp.dot(a, b, preferred_element_type=F32)


def dot_first(a, b):
    return lax.dot_general(a, b, (((0,), (0,)), ((), ())), preferred_element_type=F32)


def select_sum(one_hot, x):
    high = x.astype(BF16)
    low = (x - high.astype(F32)).astype(BF16)
    both = dot(one_hot, jnp.concatenate([high, low], axis=1))
    return both[:, : x.shape[1]] + both[:, x.shape[1] :]


def codes_of(place, rank, cap, pieces):
    code = place * (pieces * cap) + rank
    return jnp.concatenate([code + piece * cap for piece in range(pieces)], axis=1)


def one_hot_of(codes, first, count):
    return ((iota((count, codes.shape[1]), 0) + first) == codes).astype(F32).astype(BF16)


def stack_pieces(hidden, pieces):
    width = hidden.shape[1] // pieces
    return jnp.concatenate(
        [hidden[:, piece * width : (piece + 1) * width] for piece in range(pieces)], axis=0
    )


def pack_kernel(n, cap, pieces, me_ref, small_ref, hidden_ref, slot_ref, rank_ref, *out_refs):
    rows = hidden_ref.shape[0]
    named = (iota((n, rows), 0) == small_ref[:, :rows]).astype(F32).astype(BF16)
    table = jnp.broadcast_to(small_ref[:, rows:].astype(F32).astype(BF16), (16, n))
    slot = dot(table, named)[0:1, :].astype(I32)
    member = (iota((n, rows), 0) == slot).astype(F32)
    before = (iota((rows, rows), 0) < iota((rows, rows), 1)).astype(F32).astype(BF16)
    count = dot(member.astype(BF16), before)
    rank = jnp.sum(member * count, axis=0, keepdims=True).astype(I32)
    slot_ref[...] = slot
    rank_ref[...] = rank
    per = pieces * cap
    apart = lax.bitwise_xor(slot, me_ref[0])
    one_hot = one_hot_of(codes_of(apart, rank, cap, pieces), 0, n * per)
    packed = dot(one_hot, stack_pieces(hidden_ref[...], pieces)).astype(BF16)
    for s, out_ref in enumerate(out_refs):
        out_ref[...] = packed[s * per : (s + 1) * per]


def tables_kernel(n, cap, pieces, out_pieces, me_ref, _, shrink_ref, expand_ref):
    per = pieces * cap
    out_row, in_row = iota(shrink_ref.shape, 0), iota(shrink_ref.shape, 1)
    same = (out_row // cap == in_row // per) & (out_row % cap == in_row % cap)
    shrink_ref[...] = same.astype(F32).astype(BF16)
    per = out_pieces * cap
    out_row, in_row = iota(expand_ref.shape, 0), iota(expand_ref.shape, 1)
    apart = lax.bitwise_xor(out_row // per, me_ref[0])
    source = (out_row // cap % out_pieces) * (n * cap) + apart * cap + out_row % cap
    expand_ref[...] = (source == in_row).astype(F32).astype(BF16)


def shrink(cap, pieces, received_refs, down_ref, table_ref):
    width = received_refs[0].shape[1]
    rank2 = down_ref.shape[2]
    received = jnp.concatenate([ref[...] for ref in received_refs], axis=0)
    size = received.shape[0]
    total = jnp.zeros((size, rank2), F32)
    piece_of = (iota((size, rank2), 0) // cap) % pieces
    for piece in range(pieces):
        part = dot(received, down_ref[0, piece * width : (piece + 1) * width, :])
        total = total + jnp.where(piece_of == piece, part, 0.0)
    return select_sum(table_ref[...], total)


def shrink_near_kernel(cap, pieces, *refs):
    refs[-1][...] = shrink(cap, pieces, refs[:-3], *refs[-3:-1])


def shrink_far_kernel(cap, pieces, *refs):
    near_ref, out_ref = refs[-2:]
    half = near_ref.shape[0]
    out_ref[:half, :] = near_ref[...]
    count = len(refs) - 4
    received_refs = refs[count // 2 : count] + refs[: count // 2]
    out_ref[half:, :] = shrink(cap, pieces, received_refs, *refs[-4:-2])


def expand_kernel(mine_ref, other_ref, up_ref, table_ref, out_ref):
    rank = up_ref.shape[2]
    head = 128
    blocks = up_ref.shape[3] // head
    reduced = (mine_ref[...] + other_ref[...]).astype(BF16)
    terms = []
    for c in range(2):
        kept = reduced[:, c * rank : (c + 1) * rank]
        wide = dot(kept, up_ref[0, c]).astype(BF16)
        terms += [wide[:, g * head : (g + 1) * head] for g in range(blocks)]
    out_ref[...] = dot(table_ref[...], jnp.concatenate(terms, axis=0)).astype(BF16)


def prepare_kernel(cap, slot_ref, rank_ref, mine_ref, other_ref, base_ref, one_hot_ref):
    pieces = one_hot_ref.shape[0] // slot_ref.shape[1]
    size = one_hot_ref.shape[1]
    base_ref[...] = mine_ref[...] + other_ref[...]
    one_hot = one_hot_of(codes_of(slot_ref[...], rank_ref[...], cap, pieces), 0, size)
    same = (iota((size, size), 0) == iota((size, size), 1)).astype(F32).astype(BF16)
    one_hot_ref[...] = dot_first(one_hot, same).astype(BF16)


def combine_kernel(
    delta_ref,
    one_hot_ref,
    base_ref,
    query_ref,
    max_ref,
    sum_ref,
    acc_ref,
    token_hbm,
    out_hbm,
    token_ref,
    out_ref,
    sems,
):
    rows = base_ref.shape[0]
    head = 128
    groups = base_ref.shape[1] // (2 * head)
    delta = dot(one_hot_ref[...], delta_ref[...])
    heads = query_ref.shape[1] // head
    per_group = heads // groups
    scale = head ** (-0.5)
    lane = iota((rows, head), 1)
    copies = []
    for g in range(groups):
        made = []
        for c in range(2):
            at = (g * 2 + c) * head
            piece = c * groups + g
            made.append((base_ref[:, at : at + head] + delta[piece * rows : (piece + 1) * rows]).astype(BF16))
            token_ref[:, at : at + head] = made[-1]
        key, value = made[0].astype(F32), made[1].astype(F32)
        own = jnp.zeros((rows, head), F32)
        for h in range(g * per_group, (g + 1) * per_group):
            query = query_ref[:, h * head : (h + 1) * head].astype(F32)
            own = jnp.where(lane == h, jnp.sum(query * key, axis=1, keepdims=True), own)
        own = own * scale
        cache_max = max_ref[...]
        highest = jnp.maximum(own, cache_max)
        cache_factor = jnp.exp(cache_max - highest)
        own_factor = jnp.exp(own - highest)
        inverse = 1.0 / (sum_ref[...] * cache_factor + own_factor)
        cache_factor = cache_factor * inverse
        own_factor = own_factor * inverse
        for h in range(g * per_group, (g + 1) * per_group):
            lanes = slice(h * head, (h + 1) * head)
            out = acc_ref[:, lanes] * cache_factor[:, h : h + 1] + value * own_factor[:, h : h + 1]
            out_ref[:, lanes] = out.astype(BF16)
        for i, (source, target, width) in enumerate(
            [(token_ref, token_hbm, 2 * head), (out_ref, out_hbm, per_group * head)]
        ):
            part = pl.ds(g * width, width)
            copies.append(pltpu.make_async_copy(source.at[:, part], target.at[:, part], sems.at[2 * g + i]))
            copies[-1].start()
    for copy in copies:
        copy.wait()


def base_kernel(
    core_ref, hidden_ref, weight_hbm, first_ref, second_ref, mine_ref, other_ref, weight_ref, sems
):
    slots, depth = weight_ref.shape[:2]
    blocks = hidden_ref.shape[1] // depth

    def copy(k):
        part = weight_hbm.at[pl.ds(k * depth, depth), :]
        return pltpu.make_async_copy(part, weight_ref.at[k % slots], sems.at[k % slots])

    for k in range(slots):
        copy(k).start()
    rows, columns = mine_ref.shape
    total = jnp.zeros((rows, 2 * columns), F32)
    for k in range(blocks):
        copy(k).wait()
        total = total + dot(hidden_ref[:, k * depth : (k + 1) * depth], weight_ref[k % slots])
        if k + slots < blocks:
            copy(k + slots).start()
    first, second = total[:, :columns], total[:, columns:]
    mine_ref[...] = jnp.where(core_ref[0] == 0, first, second)
    other_ref[...] = jnp.where(core_ref[0] == 0, second, first)


def cache_kernel(
    query_ref, key_ref, value_ref, length_ref, base_ref, _, acc_ref, max_ref, sum_ref, handed_ref
):
    handed_ref[...] = base_ref[...]
    rows, groups, positions, head = key_ref.shape
    per_group = query_ref.shape[1] // (groups * head)
    tile = 16
    wide, deep = tile * positions, tile * per_group
    scale = head ** (-0.5)
    row_of = iota((deep, wide), 0) % tile
    own_row = row_of == iota((deep, wide), 1) // positions
    position = iota((deep, wide), 1) % positions
    lane = iota((tile, head), 1)
    for first in range(0, rows, tile):
        at = slice(first, first + tile)
        length = jnp.concatenate([length_ref[at, :]] * per_group, axis=0)
        valid = own_row & (position < length)
        tops = jnp.zeros((tile, head), F32)
        sums = jnp.zeros((tile, head), F32)
        for g in range(groups):
            query = jnp.concatenate(
                [query_ref[at, h * head : (h + 1) * head] for h in range(g * per_group, (g + 1) * per_group)],
                axis=0,
            )
            key = key_ref[at, g].reshape(wide, head)
            value = value_ref[at, g].reshape(wide, head)
            scores = lax.dot_general(query, key, (((1,), (1,)), ((), ())), preferred_element_type=F32)
            scores = jnp.where(valid, scores * scale, -jnp.inf)
            top = jnp.max(scores, axis=1, keepdims=True)
            weight = jnp.exp(scores - top)
            total = jnp.sum(weight, axis=1, keepdims=True)
            mixed = dot(weight.astype(BF16), value)
            for i in range(per_group):
                h = g * per_group + i
                part = slice(i * tile, (i + 1) * tile)
                acc_ref[at, h * head : (h + 1) * head] = mixed[part]
                tops = jnp.where(lane == h, top[part], tops)
                sums = jnp.where(lane == h, total[part], sums)
        max_ref[at, :] = tops
        sum_ref[at, :] = sums


VMEM = pl.BlockSpec(memory_space=pltpu.VMEM)
SMEM = pl.BlockSpec(memory_space=pltpu.SMEM)
HBM = pl.BlockSpec(memory_space=pltpu.HBM)
ANY = pl.BlockSpec(memory_space=pl.ANY)
NO_COST = pl.CostEstimate(flops=0, bytes_accessed=0, transcendentals=0)


def call(kernel, outs, specs, scratch=(), cost=NO_COST):
    return pl.pallas_call(
        kernel,
        out_shape=outs,
        in_specs=specs,
        out_specs=[VMEM] * len(outs),
        scratch_shapes=scratch,
        compiler_params=pltpu.CompilerParams(vmem_limit_bytes=VMEM_LIMIT),
        cost_estimate=cost,
    )


def shards(
    hidden,
    queries,
    key_value_weight,
    adapter_down_weight,
    adapter_up_weight,
    stored_cache_keys,
    stored_cache_values,
    row_adapter_index,
    stored_cache_lengths,
    adapter_slot_table,
):
    n = lax.axis_size("pool")
    rows, width = hidden.shape
    cap = -(-2 * rows // n)
    pieces = split_count(cap)
    groups = stored_cache_keys.shape[1]
    head = stored_cache_keys.shape[3]
    columns = key_value_weight.shape[1] // 2
    out_pieces = 2 * groups
    rank2 = adapter_down_weight.shape[2]

    swap = functools.partial(lax.ppermute, axis_name="tp", perm=[(0, 1), (1, 0)])

    me = lax.axis_index("pool").reshape(1)
    small = jnp.concatenate([row_adapter_index.reshape(1, rows), adapter_slot_table.reshape(1, n)], axis=1)
    slot, rank, *packed = call(
        functools.partial(pack_kernel, n, cap, pieces),
        [jax.ShapeDtypeStruct((1, rows), I32)] * 2
        + [jax.ShapeDtypeStruct((pieces * cap, width // pieces), BF16)] * n,
        [SMEM, VMEM, VMEM],
    )(me, small, hidden)
    half = n // 2
    far = [*range(half + half // 2, n), *range(half, half + half // 2)]
    order = [0, 1, 2, *far, *range(3, half)]
    arrived = {0: packed[0]}
    for s in order[1:]:
        arrived[s] = lax.ppermute(packed[s], "pool", [(i, i ^ s) for i in range(n)])

    slots, depth = 4, 512
    base_mine, base_other = call(
        base_kernel,
        [jax.ShapeDtypeStruct((rows, columns), F32)] * 2,
        [SMEM, VMEM, ANY, ANY, ANY],
        [
            pltpu.VMEM((slots, depth, 2 * columns), BF16),
            pltpu.SemaphoreType.DMA((slots,)),
        ],
        pl.CostEstimate(
            flops=4 * rows * width * columns, bytes_accessed=16 * width * columns, transcendentals=0
        ),
    )(lax.axis_index("tp").reshape(1), hidden, key_value_weight, arrived[1], arrived[2])

    size = n * out_pieces * cap
    shrink_table, expand_table = call(
        functools.partial(tables_kernel, n, cap, pieces, out_pieces),
        [
            jax.ShapeDtypeStruct((half * cap, half * pieces * cap), BF16),
            jax.ShapeDtypeStruct((size, size), BF16),
        ],
        [SMEM, ANY],
    )(me, base_mine)
    (near_sum,) = call(
        functools.partial(shrink_near_kernel, cap, pieces),
        [jax.ShapeDtypeStruct((half * cap, rank2), F32)],
        [VMEM] * (half + 2),
    )(*[arrived[s] for s in range(half)], adapter_down_weight, shrink_table)
    (sums,) = call(
        functools.partial(shrink_far_kernel, cap, pieces),
        [jax.ShapeDtypeStruct((n * cap, rank2), F32)],
        [VMEM] * (half + 3),
    )(*[arrived[s] for s in far], adapter_down_weight, shrink_table, near_sum)
    (terms,) = call(
        expand_kernel,
        [jax.ShapeDtypeStruct((size, head), BF16)],
        [VMEM] * 4,
    )(sums, swap(sums), adapter_up_weight, expand_table)
    deltas = lax.all_to_all(terms, "pool", split_axis=0, concat_axis=0, tiled=True)
    attended, cache_max, cache_sum, base_other = call(
        cache_kernel,
        [jax.ShapeDtypeStruct(queries.shape, F32)]
        + [jax.ShapeDtypeStruct((rows, head), F32)] * 2
        + [jax.ShapeDtypeStruct((rows, columns), F32)],
        [VMEM] * 5 + [ANY],
    )(
        queries,
        stored_cache_keys,
        stored_cache_values,
        stored_cache_lengths.reshape(rows, 1),
        base_other,
        terms,
    )
    base, one_hot = call(
        functools.partial(prepare_kernel, cap),
        [
            jax.ShapeDtypeStruct((rows, columns), F32),
            jax.ShapeDtypeStruct((out_pieces * rows, size), BF16),
        ],
        [VMEM] * 4,
    )(slot, rank, base_mine, swap(base_other))
    token, out = pl.pallas_call(
        combine_kernel,
        out_shape=[jax.ShapeDtypeStruct((rows, columns), BF16), jax.ShapeDtypeStruct(queries.shape, BF16)],
        in_specs=[VMEM] * 7,
        out_specs=[ANY] * 2,
        scratch_shapes=[
            pltpu.VMEM((rows, columns), BF16),
            pltpu.VMEM(queries.shape, BF16),
            pltpu.SemaphoreType.DMA((2 * groups,)),
        ],
        compiler_params=pltpu.CompilerParams(vmem_limit_bytes=VMEM_LIMIT),
        cost_estimate=NO_COST,
    )(deltas, one_hot, base, queries, cache_max, cache_sum, attended)
    return token, out


def solution(mesh):
    in_specs = (
        P(("grp", "pool"), "tp"),
        P(("grp", "pool"), "tp"),
        P("tp", None),
        P("pool", "tp", None),
        P("pool", None, None, "tp"),
        P(("grp", "pool"), "tp", None, None),
        P(("grp", "pool"), "tp", None, None),
        P(("grp", "pool"), None),
        P(("grp", "pool")),
        P(),
    )
    out_specs = (P(("grp", "pool"), "tp"), P(("grp", "pool"), "tp"))
    return jax.shard_map(shards, mesh=mesh, in_specs=in_specs, out_specs=out_specs, check_vma=False)
```

```python
import functools

import jax
import jax.numpy as jnp
from jax import lax
from jax.experimental import pallas as pl
from jax.experimental.pallas import tpu as pltpu
from jax.sharding import PartitionSpec as P

BF16 = jnp.bfloat16
F32 = jnp.float32
I32 = jnp.int32
VMEM_LIMIT = 20 * 1024 * 1024


def iota(shape, dim):
    return lax.broadcasted_iota(I32, shape, dim)


def split_count(cap):
    pieces = 4
    while cap * pieces % 16:
        pieces *= 2
    return pieces


def dot(a, b):
    return jnp.dot(a, b, preferred_element_type=F32)


def dot_first(a, b):
    return lax.dot_general(a, b, (((0,), (0,)), ((), ())), preferred_element_type=F32)


def select_sum(one_hot, x):
    high = x.astype(BF16)
    low = (x - high.astype(F32)).astype(BF16)
    both = dot(one_hot, jnp.concatenate([high, low], axis=1))
    return both[:, : x.shape[1]] + both[:, x.shape[1] :]


def codes_of(place, rank, cap, pieces):
    code = place * (pieces * cap) + rank
    return jnp.concatenate([code + piece * cap for piece in range(pieces)], axis=1)


def one_hot_of(codes, first, count):
    return ((iota((count, codes.shape[1]), 0) + first) == codes).astype(F32).astype(BF16)


def stack_pieces(hidden, pieces):
    width = hidden.shape[1] // pieces
    return jnp.concatenate(
        [hidden[:, piece * width : (piece + 1) * width] for piece in range(pieces)], axis=0
    )


def pack_kernel(n, cap, pieces, me_ref, small_ref, hidden_ref, slot_ref, rank_ref, *out_refs):
    rows = hidden_ref.shape[0]
    named = (iota((n, rows), 0) == small_ref[:, :rows]).astype(F32).astype(BF16)
    table = jnp.broadcast_to(small_ref[:, rows:].astype(F32).astype(BF16), (16, n))
    slot = dot(table, named)[0:1, :].astype(I32)
    member = (iota((n, rows), 0) == slot).astype(F32)
    before = (iota((rows, rows), 0) < iota((rows, rows), 1)).astype(F32).astype(BF16)
    count = dot(member.astype(BF16), before)
    rank = jnp.sum(member * count, axis=0, keepdims=True).astype(I32)
    slot_ref[...] = slot
    rank_ref[...] = rank
    per = pieces * cap
    apart = lax.bitwise_xor(slot, me_ref[0])
    one_hot = one_hot_of(codes_of(apart, rank, cap, pieces), 0, n * per)
    packed = dot(one_hot, stack_pieces(hidden_ref[...], pieces)).astype(BF16)
    for s, out_ref in enumerate(out_refs):
        out_ref[...] = packed[s * per : (s + 1) * per]


def tables_kernel(n, cap, pieces, out_pieces, me_ref, _, shrink_ref, expand_ref):
    per = pieces * cap
    out_row, in_row = iota(shrink_ref.shape, 0), iota(shrink_ref.shape, 1)
    same = (out_row // cap == in_row // per) & (out_row % cap == in_row % cap)
    shrink_ref[...] = same.astype(F32).astype(BF16)
    per = out_pieces * cap
    out_row, in_row = iota(expand_ref.shape, 0), iota(expand_ref.shape, 1)
    apart = lax.bitwise_xor(out_row // per, me_ref[0])
    source = (out_row // cap % out_pieces) * (n * cap) + apart * cap + out_row % cap
    expand_ref[...] = (source == in_row).astype(F32).astype(BF16)


def shrink(cap, pieces, received_refs, down_ref, table_ref):
    width = received_refs[0].shape[1]
    rank2 = down_ref.shape[2]
    received = jnp.concatenate([ref[...] for ref in received_refs], axis=0)
    size = received.shape[0]
    total = jnp.zeros((size, rank2), F32)
    piece_of = (iota((size, rank2), 0) // cap) % pieces
    for piece in range(pieces):
        part = dot(received, down_ref[0, piece * width : (piece + 1) * width, :])
        total = total + jnp.where(piece_of == piece, part, 0.0)
    return select_sum(table_ref[...], total)


def shrink_near_kernel(cap, pieces, *refs):
    refs[-1][...] = shrink(cap, pieces, refs[:-3], *refs[-3:-1])


def shrink_far_kernel(cap, pieces, *refs):
    near_ref, out_ref = refs[-2:]
    half = near_ref.shape[0]
    out_ref[:half, :] = near_ref[...]
    count = len(refs) - 4
    received_refs = refs[0:count:2] + refs[1:count:2]
    out_ref[half:, :] = shrink(cap, pieces, received_refs, *refs[-4:-2])


def expand_kernel(mine_ref, other_ref, up_ref, table_ref, out_ref):
    rank = up_ref.shape[2]
    head = 128
    blocks = up_ref.shape[3] // head
    reduced = (mine_ref[...] + other_ref[...]).astype(BF16)
    terms = []
    for c in range(2):
        kept = reduced[:, c * rank : (c + 1) * rank]
        wide = dot(kept, up_ref[0, c]).astype(BF16)
        terms += [wide[:, g * head : (g + 1) * head] for g in range(blocks)]
    out_ref[...] = dot(table_ref[...], jnp.concatenate(terms, axis=0)).astype(BF16)


def prepare_kernel(cap, slot_ref, rank_ref, mine_ref, other_ref, base_ref, one_hot_ref):
    pieces = one_hot_ref.shape[0] // slot_ref.shape[1]
    size = one_hot_ref.shape[1]
    base_ref[...] = mine_ref[...] + other_ref[...]
    one_hot = one_hot_of(codes_of(slot_ref[...], rank_ref[...], cap, pieces), 0, size)
    same = (iota((size, size), 0) == iota((size, size), 1)).astype(F32).astype(BF16)
    one_hot_ref[...] = dot_first(one_hot, same).astype(BF16)


def combine_kernel(
    delta_ref,
    one_hot_ref,
    base_ref,
    query_ref,
    max_ref,
    sum_ref,
    acc_ref,
    token_hbm,
    out_hbm,
    token_ref,
    out_ref,
    sems,
):
    rows = base_ref.shape[0]
    head = 128
    groups = base_ref.shape[1] // (2 * head)
    delta = dot(one_hot_ref[...], delta_ref[...])
    heads = query_ref.shape[1] // head
    per_group = heads // groups
    scale = head ** (-0.5)
    lane = iota((rows, head), 1)
    copies = []
    for g in range(groups):
        made = []
        for c in range(2):
            at = (g * 2 + c) * head
            piece = c * groups + g
            made.append((base_ref[:, at : at + head] + delta[piece * rows : (piece + 1) * rows]).astype(BF16))
            token_ref[:, at : at + head] = made[-1]
        key, value = made[0].astype(F32), made[1].astype(F32)
        own = jnp.zeros((rows, head), F32)
        for h in range(g * per_group, (g + 1) * per_group):
            query = query_ref[:, h * head : (h + 1) * head].astype(F32)
            own = jnp.where(lane == h, jnp.sum(query * key, axis=1, keepdims=True), own)
        own = own * scale
        cache_max = max_ref[...]
        highest = jnp.maximum(own, cache_max)
        cache_factor = jnp.exp(cache_max - highest)
        own_factor = jnp.exp(own - highest)
        inverse = 1.0 / (sum_ref[...] * cache_factor + own_factor)
        cache_factor = cache_factor * inverse
        own_factor = own_factor * inverse
        for h in range(g * per_group, (g + 1) * per_group):
            lanes = slice(h * head, (h + 1) * head)
            out = acc_ref[:, lanes] * cache_factor[:, h : h + 1] + value * own_factor[:, h : h + 1]
            out_ref[:, lanes] = out.astype(BF16)
        for i, (source, target, width) in enumerate(
            [(token_ref, token_hbm, 2 * head), (out_ref, out_hbm, per_group * head)]
        ):
            part = pl.ds(g * width, width)
            copies.append(pltpu.make_async_copy(source.at[:, part], target.at[:, part], sems.at[2 * g + i]))
            copies[-1].start()
    for copy in copies:
        copy.wait()


def base_kernel(
    core_ref, hidden_ref, weight_hbm, first_ref, second_ref, mine_ref, other_ref, weight_ref, sems
):
    slots, depth = weight_ref.shape[:2]
    blocks = hidden_ref.shape[1] // depth

    def copy(k):
        part = weight_hbm.at[pl.ds(k * depth, depth), :]
        return pltpu.make_async_copy(part, weight_ref.at[k % slots], sems.at[k % slots])

    for k in range(slots):
        copy(k).start()
    rows, columns = mine_ref.shape
    total = jnp.zeros((rows, 2 * columns), F32)
    for k in range(blocks):
        copy(k).wait()
        total = total + dot(hidden_ref[:, k * depth : (k + 1) * depth], weight_ref[k % slots])
        if k + slots < blocks:
            copy(k + slots).start()
    first, second = total[:, :columns], total[:, columns:]
    mine_ref[...] = jnp.where(core_ref[0] == 0, first, second)
    other_ref[...] = jnp.where(core_ref[0] == 0, second, first)


def cache_kernel(
    query_ref, key_ref, value_ref, length_ref, base_ref, _, acc_ref, max_ref, sum_ref, handed_ref
):
    handed_ref[...] = base_ref[...]
    rows, groups, positions, head = key_ref.shape
    per_group = query_ref.shape[1] // (groups * head)
    tile = 16
    wide, deep = tile * positions, tile * per_group
    scale = head ** (-0.5)
    row_of = iota((deep, wide), 0) % tile
    own_row = row_of == iota((deep, wide), 1) // positions
    position = iota((deep, wide), 1) % positions
    lane = iota((tile, head), 1)
    for first in range(0, rows, tile):
        at = slice(first, first + tile)
        length = jnp.concatenate([length_ref[at, :]] * per_group, axis=0)
        valid = own_row & (position < length)
        tops = jnp.zeros((tile, head), F32)
        sums = jnp.zeros((tile, head), F32)
        for g in range(groups):
            query = jnp.concatenate(
                [query_ref[at, h * head : (h + 1) * head] for h in range(g * per_group, (g + 1) * per_group)],
                axis=0,
            )
            key = key_ref[at, g].reshape(wide, head)
            value = value_ref[at, g].reshape(wide, head)
            scores = lax.dot_general(query, key, (((1,), (1,)), ((), ())), preferred_element_type=F32)
            scores = jnp.where(valid, scores * scale, -jnp.inf)
            top = jnp.max(scores, axis=1, keepdims=True)
            weight = jnp.exp(scores - top)
            total = jnp.sum(weight, axis=1, keepdims=True)
            mixed = dot(weight.astype(BF16), value)
            for i in range(per_group):
                h = g * per_group + i
                part = slice(i * tile, (i + 1) * tile)
                acc_ref[at, h * head : (h + 1) * head] = mixed[part]
                tops = jnp.where(lane == h, top[part], tops)
                sums = jnp.where(lane == h, total[part], sums)
        max_ref[at, :] = tops
        sum_ref[at, :] = sums


VMEM = pl.BlockSpec(memory_space=pltpu.VMEM)
SMEM = pl.BlockSpec(memory_space=pltpu.SMEM)
HBM = pl.BlockSpec(memory_space=pltpu.HBM)
ANY = pl.BlockSpec(memory_space=pl.ANY)
NO_COST = pl.CostEstimate(flops=0, bytes_accessed=0, transcendentals=0)


def call(kernel, outs, specs, scratch=(), cost=NO_COST):
    return pl.pallas_call(
        kernel,
        out_shape=outs,
        in_specs=specs,
        out_specs=[VMEM] * len(outs),
        scratch_shapes=scratch,
        compiler_params=pltpu.CompilerParams(vmem_limit_bytes=VMEM_LIMIT),
        cost_estimate=cost,
    )


def shards(
    hidden,
    queries,
    key_value_weight,
    adapter_down_weight,
    adapter_up_weight,
    stored_cache_keys,
    stored_cache_values,
    row_adapter_index,
    stored_cache_lengths,
    adapter_slot_table,
):
    n = lax.axis_size("pool")
    rows, width = hidden.shape
    cap = -(-2 * rows // n)
    pieces = split_count(cap)
    groups = stored_cache_keys.shape[1]
    head = stored_cache_keys.shape[3]
    columns = key_value_weight.shape[1] // 2
    out_pieces = 2 * groups
    rank2 = adapter_down_weight.shape[2]

    swap = functools.partial(lax.ppermute, axis_name="tp", perm=[(0, 1), (1, 0)])

    me = lax.axis_index("pool").reshape(1)
    small = jnp.concatenate([row_adapter_index.reshape(1, rows), adapter_slot_table.reshape(1, n)], axis=1)
    slot, rank, *packed = call(
        functools.partial(pack_kernel, n, cap, pieces),
        [jax.ShapeDtypeStruct((1, rows), I32)] * 2
        + [jax.ShapeDtypeStruct((pieces * cap, width // pieces), BF16)] * n,
        [SMEM, VMEM, VMEM],
    )(me, small, hidden)
    half = n // 2
    far = [s for i in range(half // 2) for s in (half + i, half + half // 2 + i)]
    order = [0, 1, 2, *far, *range(3, half)]
    arrived = {0: packed[0]}
    for s in order[1:]:
        arrived[s] = lax.ppermute(packed[s], "pool", [(i, i ^ s) for i in range(n)])

    slots, depth = 4, 512
    base_mine, base_other = call(
        base_kernel,
        [jax.ShapeDtypeStruct((rows, columns), F32)] * 2,
        [SMEM, VMEM, ANY, ANY, ANY],
        [
            pltpu.VMEM((slots, depth, 2 * columns), BF16),
            pltpu.SemaphoreType.DMA((slots,)),
        ],
        pl.CostEstimate(
            flops=4 * rows * width * columns, bytes_accessed=16 * width * columns, transcendentals=0
        ),
    )(lax.axis_index("tp").reshape(1), hidden, key_value_weight, arrived[1], arrived[2])

    size = n * out_pieces * cap
    shrink_table, expand_table = call(
        functools.partial(tables_kernel, n, cap, pieces, out_pieces),
        [
            jax.ShapeDtypeStruct((half * cap, half * pieces * cap), BF16),
            jax.ShapeDtypeStruct((size, size), BF16),
        ],
        [SMEM, ANY],
    )(me, base_mine)
    (near_sum,) = call(
        functools.partial(shrink_near_kernel, cap, pieces),
        [jax.ShapeDtypeStruct((half * cap, rank2), F32)],
        [VMEM] * (half + 2),
    )(*[arrived[s] for s in range(half)], adapter_down_weight, shrink_table)
    (sums,) = call(
        functools.partial(shrink_far_kernel, cap, pieces),
        [jax.ShapeDtypeStruct((n * cap, rank2), F32)],
        [VMEM] * (half + 3),
    )(*[arrived[s] for s in far], adapter_down_weight, shrink_table, near_sum)
    (terms,) = call(
        expand_kernel,
        [jax.ShapeDtypeStruct((size, head), BF16)],
        [VMEM] * 4,
    )(sums, swap(sums), adapter_up_weight, expand_table)
    deltas = lax.all_to_all(terms, "pool", split_axis=0, concat_axis=0, tiled=True)
    attended, cache_max, cache_sum, base_other = call(
        cache_kernel,
        [jax.ShapeDtypeStruct(queries.shape, F32)]
        + [jax.ShapeDtypeStruct((rows, head), F32)] * 2
        + [jax.ShapeDtypeStruct((rows, columns), F32)],
        [VMEM] * 5 + [ANY],
    )(
        queries,
        stored_cache_keys,
        stored_cache_values,
        stored_cache_lengths.reshape(rows, 1),
        base_other,
        terms,
    )
    base, one_hot = call(
        functools.partial(prepare_kernel, cap),
        [
            jax.ShapeDtypeStruct((rows, columns), F32),
            jax.ShapeDtypeStruct((out_pieces * rows, size), BF16),
        ],
        [VMEM] * 4,
    )(slot, rank, base_mine, swap(base_other))
    token, out = pl.pallas_call(
        combine_kernel,
        out_shape=[jax.ShapeDtypeStruct((rows, columns), BF16), jax.ShapeDtypeStruct(queries.shape, BF16)],
        in_specs=[VMEM] * 7,
        out_specs=[ANY] * 2,
        scratch_shapes=[
            pltpu.VMEM((rows, columns), BF16),
            pltpu.VMEM(queries.shape, BF16),
            pltpu.SemaphoreType.DMA((2 * groups,)),
        ],
        compiler_params=pltpu.CompilerParams(vmem_limit_bytes=VMEM_LIMIT),
        cost_estimate=NO_COST,
    )(deltas, one_hot, base, queries, cache_max, cache_sum, attended)
    return token, out


def solution(mesh):
    in_specs = (
        P(("grp", "pool"), "tp"),
        P(("grp", "pool"), "tp"),
        P("tp", None),
        P("pool", "tp", None),
        P("pool", None, None, "tp"),
        P(("grp", "pool"), "tp", None, None),
        P(("grp", "pool"), "tp", None, None),
        P(("grp", "pool"), None),
        P(("grp", "pool")),
        P(),
    )
    out_specs = (P(("grp", "pool"), "tp"), P(("grp", "pool"), "tp"))
    return jax.shard_map(shards, mesh=mesh, in_specs=in_specs, out_specs=out_specs, check_vma=False)
```
